32 devices in a mesh: row: 16 (over z, y, core), col: 2 (over x).
Axes of the slice: x: 2, y: 2, z: 4, core: 2. Of those that a mesh axis runs over, the one named last changes fastest.
Arguments:
- frames: bfloat16 [64, 3, 12288], P('col', None, 'row'), may hold values from -6 to 6
- rotations: float32 [3, 3, 64], replicated, may hold values from -1 to 1, as said below
- inverse_cov: float32 [12288, 12288], P('row', 'col'), may hold values from -1 to 11, as said below
Outputs:
- covariance: float32 [12288, 12288], P('row', 'col')
- fitted_rotations: float32 [3, 3, 64], P(None, None, 'col')
The draws below stay inside these ranges and needn't reach their ends.
Inputs may be any that keep to these rules, and one draw needn't show every extreme that they name: `rotations`: each frame's 3 x 3 matrix is a rotation. `inverse_cov`: symmetric.
All inputs are finite; a program needn't handle non-finite values.
Results may differ from the reference program's by a relative error of at most 0.00031.
Values may be sent and summed in bfloat16 or wider, within the bound.
No kernel may reach another device: no remote copies, remote signals or barrier semaphores. Data moves between devices by JAX's collectives and lax.ppermute only.
A program may use at most 128 MiB of HBM per device.

```python
import math
import jax
import jax.numpy as jnp
from jax import lax

ATOMS = 12288
POLAR = 12
FRAMES = 64


def euler_matrix(angles):
    cos_a, cos_b, cos_c = (jnp.cos(angles[0]), jnp.cos(angles[1]), jnp.cos(angles[2]))
    sin_a, sin_b, sin_c = (jnp.sin(angles[0]), jnp.sin(angles[1]), jnp.sin(angles[2]))
    first = jnp.stack([cos_a * cos_b, cos_a * sin_b * sin_c - sin_a * cos_c, cos_a * sin_b * cos_c + sin_a * sin_c])
    second = jnp.stack([sin_a * cos_b, sin_a * sin_b * sin_c + cos_a * cos_c, sin_a * sin_b * cos_c - cos_a * sin_c])
    third = jnp.stack([-sin_b, cos_b * sin_c, cos_b * cos_c])
    return jnp.stack([first, second, third])


def start_angles(key):
    return jax.random.uniform(jax.random.fold_in(key, 5), (3, FRAMES), jnp.float32, -math.pi, math.pi)


def unit_layout(key):
    return jax.random.uniform(jax.random.fold_in(key, 13), (3, ATOMS), jnp.float32, -1.0, 1.0)


def draw_rotations(key, part):
    truth = euler_matrix(start_angles(key))
    angle = jax.random.uniform(jax.random.fold_in(key, 7), (FRAMES,), jnp.float32, 0.2, 3.2)
    cosine = jnp.cos(angle)
    sine = jnp.sin(angle)
    third = 1.0 / 3.0
    root = 1.0 / math.sqrt(3.0)
    identity = jnp.eye(3, dtype=jnp.float32)
    cross_form = root * jnp.array([[0.0, -1.0, 1.0], [1.0, 0.0, -1.0], [-1.0, 1.0, 0.0]], jnp.float32)
    outer_form = third * jnp.ones((3, 3), jnp.float32)
    turned = identity[:, :, None] * cosine - cross_form[:, :, None] * sine + outer_form[:, :, None] * (1.0 - cosine)
    result = turned[:, 0, None, :] * truth[0][None] + turned[:, 1, None, :] * truth[1][None] + turned[:, 2, None, :] * truth[2][None]
    return result.astype(jnp.float32)


def draw_frames(key, part):
    truth = euler_matrix(start_angles(key))
    noise_key = jax.random.fold_in(key, 17)
    size_key = jax.random.fold_in(key, 19)
    unit = unit_layout(key)
    scales = jnp.array([3.5, 2.5, 1.8], jnp.float32)
    structure = scales[:, None] * unit
    spreads = jnp.exp(jax.random.uniform(size_key, (ATOMS,), jnp.float32, math.log(0.1), math.log(0.5)))
    noise = jnp.clip(jax.random.normal(noise_key, (FRAMES, 3, ATOMS), jnp.float32), -2.5, 2.5)
    turned = jnp.transpose(truth, (2, 1, 0))
    placed = turned[:, :, 0, None] * structure[0] + turned[:, :, 1, None] * structure[1] + turned[:, :, 2, None] * structure[2]
    return (placed + spreads[None, None, :] * noise).astype(jnp.bfloat16)


def draw_inverse_cov(key, part):
    noise_key = jax.random.fold_in(key, 11)
    diag_key = jax.random.fold_in(key, 23)
    unit = unit_layout(key)
    scales = jnp.array([3.5, 2.5, 1.8], jnp.float32)
    diagonal = jnp.exp(jax.random.uniform(diag_key, (ATOMS,), jnp.float32, 0.0, math.log(10.0)))
    positions = scales[:, None] * unit
    kernel_width = 0.25
    distance = (positions[0][:, None] - positions[0][None, :]) ** 2
    distance = distance + (positions[1][:, None] - positions[1][None, :]) ** 2
    distance = distance + (positions[2][:, None] - positions[2][None, :]) ** 2
    amplitude = jnp.exp(unit[0] * unit[1])
    coupling = 0.15 * amplitude[:, None] * amplitude[None, :] * jnp.exp(distance * (-0.5 / (kernel_width * kernel_width)))
    noise = jax.random.normal(noise_key, (ATOMS, ATOMS), jnp.float32)
    symmetric = (noise + noise.T) * (0.5 * ATOMS ** (-0.5))
    rows_idx = lax.broadcasted_iota(jnp.int32, (ATOMS, ATOMS), 0)
    cols_idx = lax.broadcasted_iota(jnp.int32, (ATOMS, ATOMS), 1)
    same = rows_idx == cols_idx
    return symmetric + jnp.where(same, diagonal[:, None], coupling)


def setup_inputs(seed: int = 0) -> dict:
    arg_keys = jax.random.split(jax.random.key(seed), 4)
    return {
        "frames": draw_frames(jax.random.fold_in(arg_keys[3], 71), 0),
        "rotations": draw_rotations(jax.random.fold_in(arg_keys[3], 71), 0),
        "inverse_cov": draw_inverse_cov(jax.random.fold_in(arg_keys[3], 71), 0),
    }


def orthogonalize(fitted):
    scaling = jnp.sqrt(1.0 + lax.optimization_barrier(jnp.sum(fitted * fitted, axis=(0, 1))))
    current = jnp.transpose(fitted, (1, 0, 2)) / scaling
    for sweep in range(POLAR):
        square = jnp.einsum('ijf,kjf->ikf', current, current, precision=lax.Precision.HIGHEST)
        cubed_term = jnp.einsum('ikf,klf->ilf', square, current, precision=lax.Precision.HIGHEST)
        current = 1.5 * current - 0.5 * cubed_term
    return current

def reference(frames, rotations, inverse_cov):
    coords = frames.astype(jnp.float32)
    centre = jnp.einsum('klf,fla->ka', rotations, coords, precision=lax.Precision.HIGHEST) / FRAMES
    weighted = jnp.dot(centre, inverse_cov.T, precision=lax.Precision.HIGHEST)
    fitted = jnp.einsum('fka,la->klf', coords, weighted, precision=lax.Precision.HIGHEST)
    fitted_rotations = orthogonalize(fitted)
    moved = jnp.einsum('klf,fla->fka', fitted_rotations, coords, precision=lax.Precision.HIGHEST)
    deviation = (moved - centre[None]).astype(jnp.bfloat16)
    flat_dev = deviation.reshape(3 * FRAMES, ATOMS).astype(jnp.float32)
    covariance = jnp.dot(flat_dev.T, flat_dev, precision=lax.Precision.HIGHEST) / (3 * FRAMES)
    return (covariance, fitted_rotations)
```

```python
import functools

import jax
import jax.numpy as jnp
from jax import lax
from jax.experimental import pallas as pl
from jax.experimental.pallas import tpu as pltpu
from jax.sharding import PartitionSpec as P

POLAR = 12
F32 = jnp.float32
BF16 = jnp.bfloat16
VMEM = pltpu.VMEM
MIB = 1 << 20


def whole_vmem():
    return pl.BlockSpec(memory_space=VMEM)


def smem():
    return pl.BlockSpec(memory_space=pltpu.SMEM)


def three_pieces(value):
    high = value.astype(BF16)
    rest = value - high.astype(F32)
    mid = rest.astype(BF16)
    low = (rest - mid.astype(F32)).astype(BF16)
    return high, mid, low


def rotated_sum(rot, coords):
    depth = coords.shape[0] * coords.shape[1]
    flat = jnp.concatenate([rot[:, part, :] for part in range(3)], axis=1)
    padded = jnp.concatenate([flat, jnp.zeros((5, depth), F32)], axis=0)
    stacked = jnp.concatenate(three_pieces(padded), axis=0)
    product = jnp.dot(stacked, coords.reshape(depth, coords.shape[2]), preferred_element_type=F32)
    return (product[16:19] + product[8:11]) + product[0:3]


def partial_centre_kernel(frame_total, where, rot_ref, coords_ref, out_ref):
    local = coords_ref.shape[1]
    col_count = frame_total // local
    block = lax.broadcasted_iota(jnp.int32, rot_ref.shape, 2) // local
    rot = jnp.where(block == where[1], rot_ref[...], 0.0)
    coords = coords_ref[...]
    out_ref[...] = rotated_sum(rot, jnp.concatenate([coords] * col_count, axis=1)) * (1.0 / frame_total)


def assemble_kernel(col_count, group_size, where, *refs):
    out_ref = refs[-1]
    local = refs[0].shape[1]
    group = where[0] // group_size
    for step in range(col_count):
        block = lax.rem(group + step, col_count)
        out_ref[:, pl.ds(pl.multiple_of(block * local, local), local), :] = refs[step][...]


def product_kernel(col_count, where, rot_ref, *refs):
    coords_refs = refs[:col_count]
    inv_ref, product_ref, rows_ref, centre_ref = refs[col_count:]
    local = coords_refs[0].shape[1]

    @pl.when(pl.program_id(0) == 0)
    def _():
        for step in range(col_count):
            block = lax.rem(where[1] + step, col_count)
            rows_ref[:, pl.ds(pl.multiple_of(block * local, local), local), :] = coords_refs[step][...]
        centre_ref[...] = rotated_sum(rot_ref[...], rows_ref[...]) * (1.0 / (local * col_count))

    value = inv_ref[...]
    high = value.astype(BF16)
    low = (value - high.astype(F32)).astype(BF16)
    rows = rows_ref[...].reshape(3 * local * col_count, rows_ref.shape[2])
    product_ref[...] = jnp.dot(rows, low, preferred_element_type=F32) + jnp.dot(rows, high, preferred_element_type=F32)


def fit_kernel(members, where, product_ref, *refs):
    centre_refs, out_ref = refs[:members], refs[members]
    member = lax.rem(where[0], members)
    frame_total = product_ref.shape[0] // 3
    width = centre_refs[0].shape[1]
    lanes = 128
    entries = []
    for part in range(3):
        sums = [jnp.zeros((frame_total, lanes), F32)] * 3
        for mask in range(members):
            block = member ^ mask
            for chunk in range(width // lanes):
                start = pl.multiple_of(block * width + chunk * lanes, lanes)
                value = product_ref[pl.ds(part * frame_total, frame_total), pl.ds(start, lanes)]
                for comp in range(3):
                    factor = centre_refs[mask][comp : comp + 1, chunk * lanes : (chunk + 1) * lanes]
                    sums[comp] = sums[comp] + value * factor
        entries += [jnp.sum(total.T, axis=0, keepdims=True) for total in sums]
    first = jnp.concatenate(entries[:8], axis=0)
    last = jnp.concatenate([entries[8], jnp.zeros((7, frame_total), F32)], axis=0)
    message = jnp.concatenate([first, last], axis=1)
    out_ref[...] = jnp.broadcast_to(message[None], out_ref.shape)


def orthogonalized(message, frame_total):
    fitted = [message[entry : entry + 1, :frame_total] for entry in range(8)]
    fitted.append(message[0:1, frame_total:])
    norm = functools.reduce(lambda a, b: a + b, [value * value for value in fitted])
    scaling = jnp.sqrt(1.0 + norm)
    current = [[fitted[3 * col + row] / scaling for col in range(3)] for row in range(3)]
    for _ in range(POLAR):
        square = [[None] * 3 for _ in range(3)]
        for a in range(3):
            for b in range(a, 3):
                x, y = current[a], current[b]
                square[a][b] = square[b][a] = x[0] * y[0] + x[1] * y[1] + x[2] * y[2]
        cubed = [
            [sum(square[a][k] * current[k][b] for k in range(1, 3)) + square[a][0] * current[0][b] for b in range(3)]
            for a in range(3)
        ]
        current = [[1.5 * current[a][b] - 0.5 * cubed[a][b] for b in range(3)] for a in range(3)]
    return current


def covariance_kernel(members, where, fits_ref, rows_ref, rows_centre_ref, *refs):
    panel_refs, centre_refs = refs[:members], refs[members : 2 * members]
    out_ref, rot_out_ref, wide_ref, rows_dev_ref, dev_ref = refs[2 * members :]
    frame_total = rows_ref.shape[1]
    local = rot_out_ref.shape[2]
    lanes = 128

    def deviations(coords_ref, centre_ref):
        for chunk in range(coords_ref.shape[2] // lanes):
            span = slice(chunk * lanes, (chunk + 1) * lanes)
            coords = [coords_ref[part, :, span].astype(F32) for part in range(3)]
            for comp in range(3):
                moved = wide_ref[3 * comp] * coords[0]
                moved = moved + wide_ref[3 * comp + 1] * coords[1]
                moved = moved + wide_ref[3 * comp + 2] * coords[2]
                value = moved - centre_ref[comp : comp + 1, span]
                dev_ref[comp * frame_total : (comp + 1) * frame_total, span] = value.astype(BF16)

    @pl.when(pl.program_id(0) == 0)
    def _():
        message = jnp.sum(fits_ref[...], axis=0)
        current = orthogonalized(message, frame_total)
        for a in range(3):
            flat = jnp.concatenate(current[a], axis=0)
            kept = flat[:, :local]
            for block in range(1, frame_total // local):
                kept = jnp.where(where[1] == block, flat[:, block * local : (block + 1) * local], kept)
            rot_out_ref[a] = kept
        for a in range(3):
            for b in range(3):
                column = jnp.broadcast_to(current[a][b], (lanes, frame_total)).T
                wide_ref[3 * a + b] = column
        deviations(rows_ref, rows_centre_ref)
        rows_dev_ref[...] = dev_ref[...].T

    for mask in range(members):

        @pl.when(pl.program_id(0) == mask)
        def _(mask=mask):
            deviations(panel_refs[mask], centre_refs[mask])

    product = jnp.dot(rows_dev_ref[...], dev_ref[...], preferred_element_type=F32)
    out_ref[...] = product * (1.0 / (3 * frame_total))


def per_device(frames, rotations, inverse_cov):
    row_count, col_count = lax.axis_size("row"), lax.axis_size("col")
    members = row_count // col_count
    row, col = lax.axis_index("row"), lax.axis_index("col")
    where = jnp.stack([row, col]).astype(jnp.int32)
    local, _, width = frames.shape
    frame_total = local * col_count
    device_total = row_count * col_count
    coords = jnp.transpose(frames, (1, 0, 2))
    axes = ("row", "col")

    def move(value, source_of):
        pairs = []
        for group in range(col_count):
            for member in range(members):
                for place in range(col_count):
                    from_group, from_member, from_col = source_of(group, member, place)
                    source = (from_group * members + from_member) * col_count + from_col
                    pairs.append((source, (group * members + member) * col_count + place))
        return lax.ppermute(value, axes, pairs)

    def from_panel_row(value, step):
        return move(value, lambda g, m, c: (c, m, (g + step) % col_count))

    def from_member(value, mask):
        return move(value, lambda g, m, c: (g, m ^ mask, c))

    partial = pl.pallas_call(
        functools.partial(partial_centre_kernel, frame_total),
        out_shape=jax.ShapeDtypeStruct((3, width), F32),
        in_specs=[smem(), whole_vmem(), whole_vmem()],
        out_specs=whole_vmem(),
        name="partial_centre",
    )(where, rotations, coords)
    parts = [from_panel_row(partial, step) for step in range(col_count)]
    panel_parts = [from_panel_row(coords, step) for step in range(col_count)]
    others = [move(coords, lambda g, m, c, s=step: (g, m, (c + s) % col_count)) for step in range(1, col_count)]

    own_centre = functools.reduce(lambda a, b: a + b, parts)
    centres = [own_centre] + [from_member(own_centre, mask) for mask in range(1, members)]

    own_block = pl.pallas_call(
        functools.partial(assemble_kernel, col_count, members),
        out_shape=jax.ShapeDtypeStruct((3, frame_total, width), BF16),
        in_specs=[smem()] + [whole_vmem()] * col_count,
        out_specs=whole_vmem(),
        name="assemble",
    )(where, *panel_parts)
    panel = [own_block] + [None] * (members - 1)
    for mask in range(2, members, 2):
        panel[mask] = from_member(own_block, mask)
    for mask in range(1, members, 2):
        panel[mask] = from_member(panel[mask - 1], 1)

    col_width = inverse_cov.shape[1]
    step_width = 512 if col_width % 512 == 0 else 128
    const2 = lambda i: (0, 0)
    const3 = lambda i: (0, 0, 0)
    product, rows_all, rows_centre = pl.pallas_call(
        functools.partial(product_kernel, col_count),
        grid=(col_width // step_width,),
        out_shape=(
            jax.ShapeDtypeStruct((3 * frame_total, col_width), F32),
            jax.ShapeDtypeStruct((3, frame_total, width), BF16),
            jax.ShapeDtypeStruct((3, width), F32),
        ),
        in_specs=[smem(), whole_vmem()]
        + [whole_vmem()] * col_count
        + [pl.BlockSpec((width, step_width), lambda i: (0, i))],
        out_specs=(
            pl.BlockSpec((3 * frame_total, step_width), lambda i: (0, i)),
            pl.BlockSpec((3, frame_total, width), const3),
            pl.BlockSpec((3, width), const2),
        ),
        compiler_params=pltpu.CompilerParams(vmem_limit_bytes=32 * MIB),
        cost_estimate=pl.CostEstimate(
            flops=12 * frame_total * width * col_width, bytes_accessed=4 * width * col_width, transcendentals=0
        ),
        name="frames_times_inverse",
    )(where, rotations, coords, *others, inverse_cov)

    message = pl.pallas_call(
        functools.partial(fit_kernel, members),
        out_shape=jax.ShapeDtypeStruct((device_total, 8, 2 * frame_total), F32),
        in_specs=[smem(), whole_vmem()] + [whole_vmem()] * members,
        out_specs=whole_vmem(),
        compiler_params=pltpu.CompilerParams(vmem_limit_bytes=32 * MIB),
        name="fit_part",
    )(where, product, *centres)
    fits = lax.all_to_all(message, axes, split_axis=0, concat_axis=0, tiled=True)

    covariance, transforms = pl.pallas_call(
        functools.partial(covariance_kernel, members),
        grid_spec=pltpu.PrefetchScalarGridSpec(
            num_scalar_prefetch=1,
            grid=(members,),
            in_specs=[whole_vmem()] * (3 + 2 * members),
            out_specs=(
                pl.BlockSpec((width, width), lambda i, where: (0, lax.rem(where[0], members) ^ i)),
                pl.BlockSpec((3, 3, local), lambda i, where: (0, 0, 0)),
            ),
            scratch_shapes=[
                pltpu.VMEM((9, frame_total, 128), F32),
                pltpu.VMEM((width, 3 * frame_total), BF16),
                pltpu.VMEM((3 * frame_total, width), BF16),
            ],
        ),
        out_shape=(
            jax.ShapeDtypeStruct((width, col_width), F32),
            jax.ShapeDtypeStruct((3, 3, local), F32),
        ),
        compiler_params=pltpu.CompilerParams(vmem_limit_bytes=40 * MIB),
        cost_estimate=pl.CostEstimate(
            flops=6 * frame_total * width * col_width, bytes_accessed=4 * width * col_width, transcendentals=0
        ),
        name="covariance",
    )(where, fits, rows_all, rows_centre, *panel, *centres)
    return (covariance, transforms)


def solution(mesh):
    placed = (P("col", None, "row"), P(), P("row", "col"))
    return jax.shard_map(
        per_device,
        mesh=mesh,
        in_specs=placed,
        out_specs=(P("row", "col"), P(None, None, "col")),
        check_vma=False,
    )
```

```python
import functools

import jax
import jax.numpy as jnp
from jax import lax
from jax.experimental import pallas as pl
from jax.experimental.pallas import tpu as pltpu
from jax.sharding import PartitionSpec as P

POLAR = 12
LANES = 128
F32 = jnp.float32
BF16 = jnp.bfloat16
MIB = 1 << 20


def vmem():
    return pl.BlockSpec(memory_space=pltpu.VMEM)


def smem():
    return pl.BlockSpec(memory_space=pltpu.SMEM)


def three_pieces(value):
    high = value.astype(BF16)
    rest = value - high.astype(F32)
    mid = rest.astype(BF16)
    low = (rest - mid.astype(F32)).astype(BF16)
    return high, mid, low


def rotated_sum(rot, coords):
    depth = coords.shape[0] * coords.shape[1]
    flat = jnp.concatenate([rot[:, part, :] for part in range(3)], axis=1)
    padded = jnp.concatenate([flat, jnp.zeros((5, depth), F32)], axis=0)
    stacked = jnp.concatenate(three_pieces(padded), axis=0)
    product = jnp.dot(stacked, coords.reshape(depth, coords.shape[2]), preferred_element_type=F32)
    return (product[16:19] + product[8:11]) + product[0:3]


def partial_centre_kernel(frame_total, col, rot_ref, coords_ref, out_ref):
    local = coords_ref.shape[1]
    block = lax.broadcasted_iota(jnp.int32, rot_ref.shape, 2) // local
    rot = jnp.where(block == col[0], rot_ref[...], 0.0)
    coords = jnp.concatenate([coords_ref[...]] * (frame_total // local), axis=1)
    out_ref[...] = rotated_sum(rot, coords) * (1.0 / frame_total)


def put_block(out_ref, block, value):
    local = value.shape[1]
    out_ref[:, pl.ds(pl.multiple_of(block * local, local), local), :] = value


def assemble_kernel(members, row, *refs):
    blocks, out_ref = refs[:-1], refs[-1]
    for step, ref in enumerate(blocks):
        put_block(out_ref, lax.rem(row[0] // members + step, len(blocks)), ref[...])


def rows_kernel(members, row, col, rot_ref, own_ref, panel_ref, *refs):
    others, (rows_ref, centre_ref) = refs[:-2], refs[-2:]
    at_home = row[0] // members == col[0]

    @pl.when(at_home)
    def _():
        rows_ref[...] = panel_ref[...]

    @pl.when(jnp.logical_not(at_home))
    def _():
        for step, ref in enumerate((own_ref, *others)):
            put_block(rows_ref, lax.rem(col[0] + step, len(others) + 1), ref[...])

    centre_ref[...] = rotated_sum(rot_ref[...], rows_ref[...]) * (1.0 / rows_ref.shape[1])


def add_weighted(inv_ref, centre, sums_ref):
    height, width = inv_ref.shape
    group = 64 if height % 64 == 0 else 8

    def body(step, carry):
        rows = pl.ds(pl.multiple_of(step * group, group), group)
        sums = [sums_ref[comp, rows, :] for comp in range(3)]
        for chunk in range(width // LANES):
            span = slice(chunk * LANES, (chunk + 1) * LANES)
            value = inv_ref[rows, span]
            for comp in range(3):
                sums[comp] = sums[comp] + value * centre[comp : comp + 1, span]
        for comp in range(3):
            sums_ref[comp, rows, :] = sums[comp]
        return carry

    lax.fori_loop(0, height // group, body, 0)


def weighted_kernel(halves, row, inv_ref, centre_ref, *refs):
    sums_ref = refs[-1]
    step = pl.program_id(0)

    @pl.when(step == 0)
    def _():
        sums_ref[...] = jnp.zeros_like(sums_ref)

    width = inv_ref.shape[1]
    for half in range(halves):

        @pl.when(lax.rem(step, halves) == half)
        def _(half=half):
            add_weighted(inv_ref, centre_ref[step // halves, :, half * width : (half + 1) * width], sums_ref)


def weighted_fit_kernel(halves, row, inv_ref, centre_ref, before_ref, rows_ref, out_ref, sums_ref):
    step = pl.program_id(0)

    @pl.when(step == 0)
    def _():
        sums_ref[...] = before_ref[...]

    width = inv_ref.shape[1]
    for half in range(halves):

        @pl.when(lax.rem(step, halves) == half)
        def _(half=half):
            add_weighted(inv_ref, centre_ref[step // halves, :, half * width : (half + 1) * width], sums_ref)

    @pl.when(step == pl.num_programs(0) - 1)
    def _():
        frame_total = rows_ref.shape[1]
        rows = rows_ref[...].reshape(3 * frame_total, rows_ref.shape[2])
        sums = jnp.concatenate([sums_ref[comp] for comp in range(3)], axis=1)
        high, mid, low = (jnp.dot(rows, piece, preferred_element_type=F32) for piece in three_pieces(sums))
        spread = (low + mid) + high
        entries = []
        for part in range(3):
            for comp in range(3):
                tile = spread[part * frame_total : (part + 1) * frame_total, comp * LANES : (comp + 1) * LANES]
                entries.append(jnp.sum(tile.T, axis=0, keepdims=True))
        first = jnp.concatenate(entries[:8], axis=0)
        last = jnp.concatenate([entries[8], jnp.zeros((7, frame_total), F32)], axis=0)
        message = jnp.concatenate([first, last], axis=1)
        out_ref[...] = jnp.broadcast_to(message[None], out_ref.shape)


def orthogonalized(message, frame_total):
    fitted = [message[entry : entry + 1, :frame_total] for entry in range(8)]
    fitted.append(message[0:1, frame_total:])
    norm = functools.reduce(lambda a, b: a + b, [value * value for value in fitted])
    scaling = jnp.sqrt(1.0 + norm)
    current = [[fitted[3 * col + row] / scaling for col in range(3)] for row in range(3)]
    for _ in range(POLAR):
        square = [[None] * 3 for _ in range(3)]
        for a in range(3):
            for b in range(a, 3):
                x, y = current[a], current[b]
                square[a][b] = square[b][a] = x[0] * y[0] + x[1] * y[1] + x[2] * y[2]
        cubed = [
            [square[a][0] * current[0][b] + square[a][1] * current[1][b] + square[a][2] * current[2][b] for b in range(3)]
            for a in range(3)
        ]
        current = [[1.5 * current[a][b] - 0.5 * cubed[a][b] for b in range(3)] for a in range(3)]
    return current


def put_deviations(wide_ref, coords_ref, centre, chunk, dev_ref):
    frame_total = coords_ref.shape[1]
    span = slice(chunk * LANES, (chunk + 1) * LANES)
    coords = [coords_ref[part, :, span].astype(F32) for part in range(3)]
    for comp in range(3):
        moved = wide_ref[3 * comp] * coords[0]
        moved = moved + wide_ref[3 * comp + 1] * coords[1]
        moved = moved + wide_ref[3 * comp + 2] * coords[2]
        value = moved - centre[comp : comp + 1, span]
        dev_ref[comp * frame_total : (comp + 1) * frame_total, span] = value.astype(BF16)


def put_tile(wide_ref, coords_ref, centre, rows_dev_ref, dev_ref, out_ref):
    width = coords_ref.shape[2]
    scale = 1.0 / (3 * coords_ref.shape[1])
    stride = 2 * LANES if width % (2 * LANES) == 0 else LANES
    for start in range(0, width, stride):
        for chunk in range(start // LANES, (start + stride) // LANES):
            put_deviations(wide_ref, coords_ref, centre, chunk, dev_ref)
        product = jnp.dot(rows_dev_ref[...], dev_ref[:, start : start + stride], preferred_element_type=F32)
        out_ref[:, start : start + stride] = product * scale


def first_tiles_kernel(count, row, col, fits_ref, rows_ref, rows_centre_ref, centre_ref, *refs):
    panel_refs = refs[:count]
    out_ref, rot_out_ref, wide_ref, rows_dev_ref, dev_ref = refs[count:]
    frame_total = rows_ref.shape[1]
    local = rot_out_ref.shape[2]

    @pl.when(pl.program_id(0) == 0)
    def _():
        current = orthogonalized(jnp.sum(fits_ref[...], axis=0), frame_total)
        for a in range(3):
            flat = jnp.concatenate(current[a], axis=0)
            kept = flat[:, :local]
            for block in range(1, frame_total // local):
                kept = jnp.where(col[0] == block, flat[:, block * local : (block + 1) * local], kept)
            rot_out_ref[a] = kept
            for b in range(3):
                wide_ref[3 * a + b] = jnp.broadcast_to(current[a][b], (LANES, frame_total)).T
        centre = rows_centre_ref[...]
        for chunk in range(rows_ref.shape[2] // LANES):
            put_deviations(wide_ref, rows_ref, centre, chunk, dev_ref)
        rows_dev_ref[...] = dev_ref[...].T

    for step in range(count):

        @pl.when(pl.program_id(0) == step)
        def _(step=step):
            put_tile(wide_ref, panel_refs[step], centre_ref[step], rows_dev_ref, dev_ref, out_ref)


def last_tiles_kernel(count, row, before_ref, wide_ref, rows_dev_ref, centre_ref, *refs):
    panel_refs = refs[:count]
    out_ref, dev_ref = refs[count:]
    for step in range(count):

        @pl.when(pl.program_id(0) == step)
        def _(step=step):
            put_tile(wide_ref, panel_refs[step], centre_ref[step], rows_dev_ref, dev_ref, out_ref)


def per_device(frames, rotations, inverse_cov):
    row_count, col_count = lax.axis_size("row"), lax.axis_size("col")
    members = row_count // col_count
    row = lax.axis_index("row").astype(jnp.int32).reshape(1)
    col = lax.axis_index("col").astype(jnp.int32).reshape(1)
    local, _, width = frames.shape
    frame_total = local * col_count
    device_total = row_count * col_count
    col_width = inverse_cov.shape[1]
    pairs_of_members = members // 2
    coords = jnp.transpose(frames, (1, 0, 2))

    def move(value, source_of, receives=lambda group, col: True):
        pairs = []
        for group in range(col_count):
            for member in range(members):
                for place in range(col_count):
                    if receives(group, place):
                        from_group, from_member, from_col = source_of(group, member, place)
                        source = (from_group * members + from_member) * col_count + from_col
                        pairs.append((source, (group * members + member) * col_count + place))
        return lax.ppermute(value, ("row", "col"), pairs)

    def from_panel_row(value, step):
        return move(value, lambda g, m, c: (c, m, (g + step) % col_count))

    def from_member(value, mask):
        return move(value, lambda g, m, c: (g, m ^ mask, c))

    panel_parts = [from_panel_row(coords, step) for step in range(col_count)]
    partial = pl.pallas_call(
        functools.partial(partial_centre_kernel, frame_total),
        out_shape=jax.ShapeDtypeStruct((3, width), F32),
        in_specs=[smem(), vmem(), vmem()],
        out_specs=vmem(),
        name="partial_centre",
    )(col, rotations, coords)
    parts = [from_panel_row(partial, step) for step in range(col_count)]
    own_centre = functools.reduce(lambda a, b: a + b, parts)
    centres = [own_centre] + [from_member(own_centre, 2 * step) for step in range(1, pairs_of_members)]
    centres, panel_parts, late_coords = lax.optimization_barrier((centres, panel_parts, coords))
    even_centres = jnp.stack(centres)
    odd_centres = from_member(even_centres, 1)

    others = [
        move(late_coords, lambda g, m, c, s=step: (g, m, (c + s) % col_count), lambda g, c: g != c)
        for step in range(1, col_count)
    ]
    own_block = pl.pallas_call(
        functools.partial(assemble_kernel, members),
        out_shape=jax.ShapeDtypeStruct((3, frame_total, width), BF16),
        in_specs=[smem()] + [vmem()] * col_count,
        out_specs=vmem(),
        name="assemble",
    )(row, *panel_parts)
    even_panel = [own_block] + [from_member(own_block, 2 * step) for step in range(1, pairs_of_members)]

    rows_all, rows_centre = pl.pallas_call(
        functools.partial(rows_kernel, members),
        out_shape=(
            jax.ShapeDtypeStruct((3, frame_total, width), BF16),
            jax.ShapeDtypeStruct((3, width), F32),
        ),
        in_specs=[smem(), smem()] + [vmem()] * (2 + col_count),
        out_specs=(vmem(), vmem()),
        name="rows",
    )(row, col, rotations, coords, own_block, *others)

    halves = 2 if width % (2 * LANES) == 0 else 1
    piece = width // halves
    steps = pairs_of_members * halves

    def inv_spec(odd):
        def index(i, row):
            return (0, (lax.rem(row[0], members) ^ (2 * (i // halves) + odd)) * halves + lax.rem(i, halves))

        return pl.BlockSpec((width, piece), index)

    weighted_cost = pl.CostEstimate(
        flops=3 * width * col_width, bytes_accessed=2 * width * col_width, transcendentals=0
    )
    even_sums = pl.pallas_call(
        functools.partial(weighted_kernel, halves),
        grid_spec=pltpu.PrefetchScalarGridSpec(
            num_scalar_prefetch=1, grid=(steps,), in_specs=[inv_spec(0), vmem()], out_specs=vmem()
        ),
        out_shape=jax.ShapeDtypeStruct((3, width, LANES), F32),
        compiler_params=pltpu.CompilerParams(vmem_limit_bytes=24 * MIB),
        cost_estimate=weighted_cost,
        name="weighted_even",
    )(row, inverse_cov, even_centres)
    message = pl.pallas_call(
        functools.partial(weighted_fit_kernel, halves),
        grid_spec=pltpu.PrefetchScalarGridSpec(
            num_scalar_prefetch=1,
            grid=(steps,),
            in_specs=[inv_spec(1)] + [vmem()] * 3,
            out_specs=vmem(),
            scratch_shapes=[pltpu.VMEM((3, width, LANES), F32)],
        ),
        out_shape=jax.ShapeDtypeStruct((device_total, 8, 2 * frame_total), F32),
        compiler_params=pltpu.CompilerParams(vmem_limit_bytes=24 * MIB),
        cost_estimate=weighted_cost,
        name="weighted_odd_and_fit",
    )(row, inverse_cov, odd_centres, even_sums, rows_all)
    fits = lax.all_to_all(message, ("row", "col"), split_axis=0, concat_axis=0, tiled=True)
    fits, even_panel = lax.optimization_barrier((fits, even_panel))
    odd_panel = [from_member(block, 1) for block in even_panel]

    def tile_spec(odd):
        return pl.BlockSpec((width, width), lambda i, row, *_: (0, lax.rem(row[0], members) ^ (2 * i + odd)))

    tiles_cost = pl.CostEstimate(
        flops=3 * frame_total * width * col_width, bytes_accessed=2 * width * col_width, transcendentals=0
    )
    dev_scratch = pltpu.VMEM((3 * frame_total, width), BF16)
    half_done, transforms, wide, rows_dev = pl.pallas_call(
        functools.partial(first_tiles_kernel, pairs_of_members),
        grid_spec=pltpu.PrefetchScalarGridSpec(
            num_scalar_prefetch=2,
            grid=(pairs_of_members,),
            in_specs=[vmem()] * (4 + pairs_of_members),
            out_specs=(tile_spec(0), vmem(), vmem(), vmem()),
            scratch_shapes=[dev_scratch],
        ),
        out_shape=(
            jax.ShapeDtypeStruct((width, col_width), F32),
            jax.ShapeDtypeStruct((3, 3, local), F32),
            jax.ShapeDtypeStruct((9, frame_total, LANES), F32),
            jax.ShapeDtypeStruct((width, 3 * frame_total), BF16),
        ),
        compiler_params=pltpu.CompilerParams(vmem_limit_bytes=32 * MIB),
        cost_estimate=tiles_cost,
        name="steps_and_even_tiles",
    )(row, col, fits, rows_all, rows_centre, even_centres, *even_panel)
    covariance = pl.pallas_call(
        functools.partial(last_tiles_kernel, pairs_of_members),
        grid_spec=pltpu.PrefetchScalarGridSpec(
            num_scalar_prefetch=1,
            grid=(pairs_of_members,),
            in_specs=[pl.BlockSpec(memory_space=pl.ANY)] + [vmem()] * (3 + pairs_of_members),
            out_specs=tile_spec(1),
            scratch_shapes=[dev_scratch],
        ),
        out_shape=jax.ShapeDtypeStruct((width, col_width), F32),
        input_output_aliases={1: 0},
        compiler_params=pltpu.CompilerParams(vmem_limit_bytes=32 * MIB),
        cost_estimate=tiles_cost,
        name="odd_tiles",
    )(row, half_done, wide, rows_dev, odd_centres, *odd_panel)
    return (covariance, transforms)


def solution(mesh):
    placed = (P("col", None, "row"), P(), P("row", "col"))
    return jax.shard_map(
        per_device,
        mesh=mesh,
        in_specs=placed,
        out_specs=(P("row", "col"), P(None, None, "col")),
        check_vma=False,
    )
```

```python
import functools

import jax
import jax.numpy as jnp
from jax import lax
from jax.experimental import pallas as pl
from jax.experimental.pallas import tpu as pltpu
from jax.sharding import PartitionSpec as P

POLAR = 12
LANES = 128
F32 = jnp.float32
BF16 = jnp.bfloat16
MIB = 1 << 20


def vmem():
    return pl.BlockSpec(memory_space=pltpu.VMEM)


def smem():
    return pl.BlockSpec(memory_space=pltpu.SMEM)


def three_pieces(value):
    high = value.astype(BF16)
    rest = value - high.astype(F32)
    mid = rest.astype(BF16)
    low = (rest - mid.astype(F32)).astype(BF16)
    return high, mid, low


def rotated_sum(rot, coords):
    depth = coords.shape[0] * coords.shape[1]
    flat = jnp.concatenate([rot[:, part, :] for part in range(3)], axis=1)
    padded = jnp.concatenate([flat, jnp.zeros((5, depth), F32)], axis=0)
    stacked = jnp.concatenate(three_pieces(padded), axis=0)
    product = jnp.dot(stacked, coords.reshape(depth, coords.shape[2]), preferred_element_type=F32)
    return (product[16:19] + product[8:11]) + product[0:3]


def partial_centre_kernel(frame_total, col, rot_ref, coords_ref, out_ref):
    local = coords_ref.shape[1]
    block = lax.broadcasted_iota(jnp.int32, rot_ref.shape, 2) // local
    rot = jnp.where(block == col[0], rot_ref[...], 0.0)
    coords = jnp.concatenate([coords_ref[...]] * (frame_total // local), axis=1)
    out_ref[...] = rotated_sum(rot, coords) * (1.0 / frame_total)


def put_block(out_ref, block, value):
    local = value.shape[1]
    out_ref[:, pl.ds(pl.multiple_of(block * local, local), local), :] = value


def assemble_kernel(members, row, *refs):
    blocks, out_ref = refs[:-1], refs[-1]
    for step, ref in enumerate(blocks):
        put_block(out_ref, lax.rem(row[0] // members + step, len(blocks)), ref[...])


def add_weighted(inv_ref, centre, sums_ref):
    height, width = inv_ref.shape
    group = 64 if height % 64 == 0 else 8

    def body(step, carry):
        rows = pl.ds(pl.multiple_of(step * group, group), group)
        sums = [sums_ref[comp, rows, :] for comp in range(3)]
        for chunk in range(width // LANES):
            span = slice(chunk * LANES, (chunk + 1) * LANES)
            value = inv_ref[rows, span]
            for comp in range(3):
                sums[comp] = sums[comp] + value * centre[comp : comp + 1, span]
        for comp in range(3):
            sums_ref[comp, rows, :] = sums[comp]
        return carry

    lax.fori_loop(0, height // group, body, 0)


def weighted_fit_kernel(members, halves, row, col, inv_ref, centre_ref, rot_ref, own_ref, panel_ref, *refs):
    others, (out_ref, rows_ref, rows_centre_ref, sums_ref) = refs[:-4], refs[-4:]
    step = pl.program_id(0)
    at_home = row[0] // members == col[0]

    @pl.when(step == 0)
    def _():
        sums_ref[...] = jnp.zeros_like(sums_ref)

        @pl.when(at_home)
        def _():
            rows_ref[...] = panel_ref[...]

        @pl.when(jnp.logical_not(at_home))
        def _():
            for shift, ref in enumerate((own_ref, *others)):
                put_block(rows_ref, lax.rem(col[0] + shift, len(others) + 1), ref[...])

        rows_centre_ref[...] = rotated_sum(rot_ref[...], rows_ref[...]) * (1.0 / rows_ref.shape[1])

    width = inv_ref.shape[1]
    for half in range(halves):

        @pl.when(lax.rem(step, halves) == half)
        def _(half=half):
            add_weighted(inv_ref, centre_ref[step // halves, :, half * width : (half + 1) * width], sums_ref)

    @pl.when(step == pl.num_programs(0) - 1)
    def _():
        frame_total = rows_ref.shape[1]
        rows = rows_ref[...].reshape(3 * frame_total, rows_ref.shape[2])
        sums = jnp.concatenate([sums_ref[comp] for comp in range(3)], axis=1)
        high, mid, low = (jnp.dot(rows, piece, preferred_element_type=F32) for piece in three_pieces(sums))
        spread = (low + mid) + high
        entries = []
        for part in range(3):
            for comp in range(3):
                tile = spread[part * frame_total : (part + 1) * frame_total, comp * LANES : (comp + 1) * LANES]
                entries.append(jnp.sum(tile.T, axis=0, keepdims=True))
        first = jnp.concatenate(entries[:8], axis=0)
        last = jnp.concatenate([entries[8], jnp.zeros((7, frame_total), F32)], axis=0)
        message = jnp.concatenate([first, last], axis=1)
        out_ref[...] = jnp.broadcast_to(message[None], out_ref.shape)


def orthogonalized(message, frame_total):
    fitted = [message[entry : entry + 1, :frame_total] for entry in range(8)]
    fitted.append(message[0:1, frame_total:])
    norm = functools.reduce(lambda a, b: a + b, [value * value for value in fitted])
    scaling = jnp.sqrt(1.0 + norm)
    current = [[fitted[3 * col + row] / scaling for col in range(3)] for row in range(3)]
    for _ in range(POLAR):
        square = [[None] * 3 for _ in range(3)]
        for a in range(3):
            for b in range(a, 3):
                x, y = current[a], current[b]
                square[a][b] = square[b][a] = x[0] * y[0] + x[1] * y[1] + x[2] * y[2]
        cubed = [
            [square[a][0] * current[0][b] + square[a][1] * current[1][b] + square[a][2] * current[2][b] for b in range(3)]
            for a in range(3)
        ]
        current = [[1.5 * current[a][b] - 0.5 * cubed[a][b] for b in range(3)] for a in range(3)]
    return current


def put_deviations(wide_ref, coords_ref, centre, chunk, dev_ref):
    frame_total = coords_ref.shape[1]
    span = slice(chunk * LANES, (chunk + 1) * LANES)
    coords = [coords_ref[part, :, span].astype(F32) for part in range(3)]
    for comp in range(3):
        moved = wide_ref[3 * comp] * coords[0]
        moved = moved + wide_ref[3 * comp + 1] * coords[1]
        moved = moved + wide_ref[3 * comp + 2] * coords[2]
        value = moved - centre[comp : comp + 1, span]
        dev_ref[comp * frame_total : (comp + 1) * frame_total, span] = value.astype(BF16)


def put_tile(wide_ref, coords_ref, centre, rows_dev_ref, dev_ref, out_ref):
    width = coords_ref.shape[2]
    scale = 1.0 / (3 * coords_ref.shape[1])
    stride = 2 * LANES if width % (2 * LANES) == 0 else LANES
    for start in range(0, width, stride):
        for chunk in range(start // LANES, (start + stride) // LANES):
            put_deviations(wide_ref, coords_ref, centre, chunk, dev_ref)
        product = jnp.dot(rows_dev_ref[...], dev_ref[:, start : start + stride], preferred_element_type=F32)
        out_ref[:, start : start + stride] = product * scale


def covariance_kernel(members, row, col, fits_ref, rows_ref, rows_centre_ref, centre_ref, *refs):
    panel_refs = refs[:members]
    out_ref, rot_out_ref, wide_ref, rows_dev_ref, dev_ref = refs[members:]
    frame_total = rows_ref.shape[1]
    local = rot_out_ref.shape[2]

    @pl.when(pl.program_id(0) == 0)
    def _():
        current = orthogonalized(jnp.sum(fits_ref[...], axis=0), frame_total)
        for a in range(3):
            flat = jnp.concatenate(current[a], axis=0)
            kept = flat[:, :local]
            for block in range(1, frame_total // local):
                kept = jnp.where(col[0] == block, flat[:, block * local : (block + 1) * local], kept)
            rot_out_ref[a] = kept
        entries = [current[a][b] for a in range(3) for b in range(3)]
        columns = jnp.concatenate(entries + [jnp.zeros((7, frame_total), F32)], axis=0).T
        for entry in range(9):
            wide_ref[entry] = jnp.broadcast_to(columns[:, entry : entry + 1], (frame_total, LANES))
        centre = rows_centre_ref[...]
        for chunk in range(rows_ref.shape[2] // LANES):
            put_deviations(wide_ref, rows_ref, centre, chunk, dev_ref)
        rows_dev_ref[...] = dev_ref[...].T

    member = lax.rem(row[0], members)
    for step in range(members):

        @pl.when(pl.program_id(0) == step)
        def _(step=step):
            put_tile(wide_ref, panel_refs[step], centre_ref[member ^ step], rows_dev_ref, dev_ref, out_ref)


def per_device(frames, rotations, inverse_cov):
    row_count, col_count = lax.axis_size("row"), lax.axis_size("col")
    members = row_count // col_count
    row = lax.axis_index("row").astype(jnp.int32).reshape(1)
    col = lax.axis_index("col").astype(jnp.int32).reshape(1)
    local, _, width = frames.shape
    frame_total = local * col_count
    device_total = row_count * col_count
    col_width = inverse_cov.shape[1]
    coords = jnp.transpose(frames, (1, 0, 2))

    def move(value, source_of, receives=lambda group, col: True):
        pairs = []
        for group in range(col_count):
            for member in range(members):
                for place in range(col_count):
                    if receives(group, place):
                        from_group, from_member, from_col = source_of(group, member, place)
                        source = (from_group * members + from_member) * col_count + from_col
                        pairs.append((source, (group * members + member) * col_count + place))
        return lax.ppermute(value, ("row", "col"), pairs)

    def from_panel_row(value, step):
        return move(value, lambda g, m, c: (c, m, (g + step) % col_count))

    def from_member(value, mask):
        return move(value, lambda g, m, c: (g, m ^ mask, c))

    partial = pl.pallas_call(
        functools.partial(partial_centre_kernel, frame_total),
        out_shape=jax.ShapeDtypeStruct((3, width), F32),
        in_specs=[smem(), vmem(), vmem()],
        out_specs=vmem(),
        name="partial_centre",
    )(col, rotations, coords)
    parts = [from_panel_row(partial, step) for step in range(col_count)]
    _, late_coords = lax.optimization_barrier((partial, coords))
    panel_parts = [from_panel_row(late_coords, step) for step in range(col_count)]
    others = [
        move(late_coords, lambda g, m, c, s=step: (g, m, (c + s) % col_count), lambda g, c: g != c)
        for step in range(1, col_count)
    ]

    own_centre = functools.reduce(lambda a, b: a + b, parts)
    repeated = jnp.broadcast_to(own_centre[None], (members, 3, width))
    _, panel_parts = lax.optimization_barrier((repeated, panel_parts))
    groups = [[group * members + member for member in range(members)] for group in range(col_count)]
    centres = lax.all_to_all(repeated, "row", split_axis=0, concat_axis=0, axis_index_groups=groups, tiled=True)

    own_block = pl.pallas_call(
        functools.partial(assemble_kernel, members),
        out_shape=jax.ShapeDtypeStruct((3, frame_total, width), BF16),
        in_specs=[smem()] + [vmem()] * col_count,
        out_specs=vmem(),
        name="assemble",
    )(row, *panel_parts)
    even_panel = [own_block] + [from_member(own_block, 2 * step) for step in range(1, members // 2)]

    halves = 2 if width % (2 * LANES) == 0 else 1
    piece = width // halves
    message, rows_all, rows_centre = pl.pallas_call(
        functools.partial(weighted_fit_kernel, members, halves),
        grid_spec=pltpu.PrefetchScalarGridSpec(
            num_scalar_prefetch=2,
            grid=(members * halves,),
            in_specs=[pl.BlockSpec((width, piece), lambda i, *_: (0, i))] + [vmem()] * (3 + col_count),
            out_specs=(vmem(), vmem(), vmem()),
            scratch_shapes=[pltpu.VMEM((3, width, LANES), F32)],
        ),
        out_shape=(
            jax.ShapeDtypeStruct((device_total, 8, 2 * frame_total), F32),
            jax.ShapeDtypeStruct((3, frame_total, width), BF16),
            jax.ShapeDtypeStruct((3, width), F32),
        ),
        compiler_params=pltpu.CompilerParams(vmem_limit_bytes=40 * MIB),
        cost_estimate=pl.CostEstimate(
            flops=6 * width * col_width, bytes_accessed=4 * width * col_width, transcendentals=0
        ),
        name="weighted_fit",
    )(
        row,
        col,
        pltpu.with_memory_space_constraint(inverse_cov, pltpu.HBM),
        centres,
        rotations,
        coords,
        own_block,
        *others,
    )
    _, even_panel = lax.optimization_barrier((message, even_panel))
    fits = lax.all_to_all(message, ("row", "col"), split_axis=0, concat_axis=0, tiled=True)
    panel = [None] * members
    panel[0::2] = even_panel
    panel[1::2] = [from_member(block, 1) for block in even_panel]

    covariance, transforms = pl.pallas_call(
        functools.partial(covariance_kernel, members),
        grid_spec=pltpu.PrefetchScalarGridSpec(
            num_scalar_prefetch=2,
            grid=(members,),
            in_specs=[vmem()] * (4 + members),
            out_specs=(
                pl.BlockSpec((width, width), lambda i, row, col: (0, lax.rem(row[0], members) ^ i)),
                vmem(),
            ),
            scratch_shapes=[
                pltpu.VMEM((9, frame_total, LANES), F32),
                pltpu.VMEM((width, 3 * frame_total), BF16),
                pltpu.VMEM((3 * frame_total, width), BF16),
            ],
        ),
        out_shape=(
            jax.ShapeDtypeStruct((width, col_width), F32),
            jax.ShapeDtypeStruct((3, 3, local), F32),
        ),
        compiler_params=pltpu.CompilerParams(vmem_limit_bytes=32 * MIB),
        cost_estimate=pl.CostEstimate(
            flops=6 * frame_total * width * col_width, bytes_accessed=4 * width * col_width, transcendentals=0
        ),
        name="covariance",
    )(row, col, fits, rows_all, rows_centre, centres, *panel)
    return (covariance, transforms)


def solution(mesh):
    placed = (P("col", None, "row"), P(), P("row", "col"))
    return jax.shard_map(
        per_device,
        mesh=mesh,
        in_specs=placed,
        out_specs=(P("row", "col"), P(None, None, "col")),
        check_vma=False,
    )
```

```python
import functools

import jax
import jax.numpy as jnp
from jax import lax
from jax.experimental import pallas as pl
from jax.experimental.pallas import tpu as pltpu
from jax.sharding import PartitionSpec as P

POLAR = 12
LANES = 128
F32 = jnp.float32
BF16 = jnp.bfloat16
MIB = 1 << 20


def vmem():
    return pl.BlockSpec(memory_space=pltpu.VMEM)


def smem():
    return pl.BlockSpec(memory_space=pltpu.SMEM)


def three_pieces(value):
    high = value.astype(BF16)
    rest = value - high.astype(F32)
    mid = rest.astype(BF16)
    low = (rest - mid.astype(F32)).astype(BF16)
    return high, mid, low


def rotated_sum(rot, coords):
    depth = coords.shape[0] * coords.shape[1]
    flat = jnp.concatenate([rot[:, part, :] for part in range(3)], axis=1)
    padded = jnp.concatenate([flat, jnp.zeros((5, depth), F32)], axis=0)
    stacked = jnp.concatenate(three_pieces(padded), axis=0)
    product = jnp.dot(stacked, coords.reshape(depth, coords.shape[2]), preferred_element_type=F32)
    return (product[16:19] + product[8:11]) + product[0:3]


def put_block(out_ref, block, value):
    local = value.shape[1]
    out_ref[:, pl.ds(pl.multiple_of(block * local, local), local), :] = value


def assemble_kernel(members, row, rot_ref, *refs):
    blocks, (out_ref, centre_ref) = refs[:-2], refs[-2:]
    for step, ref in enumerate(blocks):
        put_block(out_ref, lax.rem(row[0] // members + step, len(blocks)), ref[...])
    centre = rotated_sum(rot_ref[...], out_ref[...]) * (1.0 / out_ref.shape[1])
    centre_ref[...] = jnp.broadcast_to(centre[None], centre_ref.shape)


def weighted_fit_kernel(members, row, col, inv_ref, centre_ref, rot_ref, own_ref, panel_ref, *refs):
    others, (out_ref, rows_ref, rows_centre_ref, wide_ref, weighted_ref) = refs[:-5], refs[-5:]
    step = pl.program_id(0)
    height, col_width = inv_ref.shape
    width = centre_ref.shape[2]

    @pl.when(step == 0)
    def _():
        for block in range(members):
            for comp in range(3):
                factor = jnp.broadcast_to(centre_ref[block, comp : comp + 1, :], (8, width))
                wide_ref[comp, :, block * width : (block + 1) * width] = factor

    def body(chunk, sums):
        span = pl.ds(pl.multiple_of(chunk * LANES, LANES), LANES)
        value = inv_ref[:, span].reshape(height // 8, 8, LANES)
        return tuple(sums[comp] + value * wide_ref[comp, :, span][None] for comp in range(3))

    zero = jnp.zeros((height // 8, 8, LANES), F32)
    chunks = col_width // LANES
    sums = lax.fori_loop(0, chunks, body, (zero,) * 3, unroll=12 if chunks % 12 == 0 else 1)
    lane = lax.broadcasted_iota(jnp.int32, (height, LANES), 1)
    packed = jnp.zeros((height, LANES), F32)
    for comp in range(3):
        total = jnp.sum(sums[comp].reshape(height, LANES), axis=1, keepdims=True)
        packed = jnp.where(lane == comp, total, packed)
    weighted_ref[pl.ds(pl.multiple_of(step * height, height), height), :] = packed

    @pl.when(step == 0)
    def _():
        at_home = row[0] // members == col[0]

        @pl.when(at_home)
        def _():
            rows_ref[...] = panel_ref[...]

        @pl.when(jnp.logical_not(at_home))
        def _():
            for shift, ref in enumerate((own_ref, *others)):
                put_block(rows_ref, lax.rem(col[0] + shift, len(others) + 1), ref[...])

        rows_centre_ref[...] = rotated_sum(rot_ref[...], rows_ref[...]) * (1.0 / rows_ref.shape[1])

    @pl.when(step == pl.num_programs(0) - 1)
    def _():
        frame_total = rows_ref.shape[1]
        rows = rows_ref[...].reshape(3 * frame_total, width)
        high, mid, low = (
            jnp.dot(rows, piece, preferred_element_type=F32) for piece in three_pieces(weighted_ref[...])
        )
        fits = ((low + mid) + high).T
        entries = [
            fits[comp : comp + 1, part * frame_total : (part + 1) * frame_total]
            for part in range(3)
            for comp in range(3)
        ]
        first = jnp.concatenate(entries[:8], axis=0)
        last = jnp.concatenate([entries[8], jnp.zeros((7, frame_total), F32)], axis=0)
        message = jnp.concatenate([first, last], axis=1)
        out_ref[...] = jnp.broadcast_to(message[None], out_ref.shape)


def add_parts_kernel(parts_ref, out_ref):
    out_ref[...] = jnp.broadcast_to(jnp.sum(parts_ref[...], axis=0)[None], out_ref.shape)


def orthogonalized(message, frame_total):
    fitted = [message[entry : entry + 1, :frame_total] for entry in range(8)]
    fitted.append(message[0:1, frame_total:])
    norm = functools.reduce(lambda a, b: a + b, [value * value for value in fitted])
    scaling = jnp.sqrt(1.0 + norm)
    current = [[fitted[3 * col + row] / scaling for col in range(3)] for row in range(3)]
    for _ in range(POLAR):
        square = [[None] * 3 for _ in range(3)]
        for a in range(3):
            for b in range(a, 3):
                x, y = current[a], current[b]
                square[a][b] = square[b][a] = x[0] * y[0] + x[1] * y[1] + x[2] * y[2]
        cubed = [
            [square[a][0] * current[0][b] + square[a][1] * current[1][b] + square[a][2] * current[2][b] for b in range(3)]
            for a in range(3)
        ]
        current = [[1.5 * current[a][b] - 0.5 * cubed[a][b] for b in range(3)] for a in range(3)]
    return current


def put_deviations(wide_ref, coords_ref, centre, chunk, dev_ref):
    frame_total = coords_ref.shape[1]
    span = slice(chunk * LANES, (chunk + 1) * LANES)
    coords = [coords_ref[part, :, span].astype(F32) for part in range(3)]
    for comp in range(3):
        moved = wide_ref[3 * comp] * coords[0]
        moved = moved + wide_ref[3 * comp + 1] * coords[1]
        moved = moved + wide_ref[3 * comp + 2] * coords[2]
        value = moved - centre[comp : comp + 1, span]
        dev_ref[comp * frame_total : (comp + 1) * frame_total, span] = value.astype(BF16)


def covariance_kernel(members, row, col, fits_ref, rows_ref, rows_centre_ref, centre_ref, *refs):
    panel_refs = refs[:members]
    out_ref, rot_out_ref, wide_ref, rows_dev_ref, dev_ref, tile_ref, sems = refs[members:]
    frame_total = rows_ref.shape[1]
    local = rot_out_ref.shape[2]
    slots, strip, width = tile_ref.shape
    strips = slots // 2
    scale = 1.0 / (3 * frame_total)

    current = orthogonalized(jnp.sum(fits_ref[...], axis=0), frame_total)
    for a in range(3):
        flat = jnp.concatenate(current[a], axis=0)
        kept = flat[:, :local]
        for block in range(1, frame_total // local):
            kept = jnp.where(col[0] == block, flat[:, block * local : (block + 1) * local], kept)
        rot_out_ref[a] = kept
    entries = [current[a][b] for a in range(3) for b in range(3)]
    columns = jnp.concatenate(entries + [jnp.zeros((7, frame_total), F32)], axis=0).T
    for entry in range(9):
        wide_ref[entry] = jnp.broadcast_to(columns[:, entry : entry + 1], (frame_total, LANES))
    centre = rows_centre_ref[...]
    for chunk in range(width // LANES):
        put_deviations(wide_ref, rows_ref, centre, chunk, dev_ref.at[0])
    rows_dev_ref[...] = dev_ref[0].T

    member = lax.rem(row[0], members)

    def write(step, part):
        start = pl.multiple_of((member ^ step) * width, LANES)
        slot = (step % 2) * strips + part
        span = pl.ds(part * strip, strip)
        return pltpu.make_async_copy(tile_ref.at[slot], out_ref.at[span, pl.ds(start, width)], sems.at[slot])

    for step in range(members):
        dev = dev_ref.at[step % 2]
        centre = centre_ref[member ^ step]
        for chunk in range(width // LANES):
            put_deviations(wide_ref, panel_refs[step], centre, chunk, dev)
        for part in range(strips):
            product = jnp.dot(
                rows_dev_ref[part * strip : (part + 1) * strip, :], dev[...], preferred_element_type=F32
            )
            if step >= 2:
                write(step - 2, part).wait()
            tile_ref[(step % 2) * strips + part] = product * scale
            write(step, part).start()
    for step in range(max(members - 2, 0), members):
        for part in range(strips):
            write(step, part).wait()


def per_device(frames, rotations, inverse_cov):
    row_count, col_count = lax.axis_size("row"), lax.axis_size("col")
    members = row_count // col_count
    row = lax.axis_index("row").astype(jnp.int32).reshape(1)
    col = lax.axis_index("col").astype(jnp.int32).reshape(1)
    local, _, width = frames.shape
    frame_total = local * col_count
    col_width = inverse_cov.shape[1]
    coords = jnp.transpose(frames, (1, 0, 2))

    def move(value, source_of, receives=lambda group, col: True):
        pairs = []
        for group in range(col_count):
            for member in range(members):
                for place in range(col_count):
                    if receives(group, place):
                        from_group, from_member, from_col = source_of(group, member, place)
                        source = (from_group * members + from_member) * col_count + from_col
                        pairs.append((source, (group * members + member) * col_count + place))
        return lax.ppermute(value, ("row", "col"), pairs)

    def from_panel_row(value, step):
        return move(value, lambda g, m, c: (c, m, (g + step) % col_count))

    def from_member(value, mask):
        return move(value, lambda g, m, c: (g, m ^ mask, c))

    panel_parts = [from_panel_row(coords, step) for step in range(col_count)]
    others = [
        move(coords, lambda g, m, c, s=step: (g, m, (c + s) % col_count), lambda g, c: g != c)
        for step in range(1, col_count)
    ]
    panel_parts, others = lax.optimization_barrier((panel_parts, others))
    own_block, repeated = pl.pallas_call(
        functools.partial(assemble_kernel, members),
        out_shape=(
            jax.ShapeDtypeStruct((3, frame_total, width), BF16),
            jax.ShapeDtypeStruct((members, 3, width), F32),
        ),
        in_specs=[smem()] + [vmem()] * (1 + col_count),
        out_specs=(vmem(), vmem()),
        name="assemble",
    )(row, rotations, *panel_parts)
    groups = [[group * members + member for member in range(members)] for group in range(col_count)]
    centres = lax.all_to_all(repeated, "row", split_axis=0, concat_axis=0, axis_index_groups=groups, tiled=True)
    _, own_block = lax.optimization_barrier((centres, own_block))
    even_panel = [own_block] + [from_member(own_block, 2 * step) for step in range(1, members // 2)]

    height = 64 if width % 64 == 0 else 8
    message, rows_all, rows_centre = pl.pallas_call(
        functools.partial(weighted_fit_kernel, members),
        grid_spec=pltpu.PrefetchScalarGridSpec(
            num_scalar_prefetch=2,
            grid=(width // height,),
            in_specs=[pl.BlockSpec((height, col_width), lambda i, *_: (i, 0))] + [vmem()] * (3 + col_count),
            out_specs=(vmem(), vmem(), vmem()),
            scratch_shapes=[pltpu.VMEM((3, 8, col_width), F32), pltpu.VMEM((width, LANES), F32)],
        ),
        out_shape=(
            jax.ShapeDtypeStruct((members, 8, 2 * frame_total), F32),
            jax.ShapeDtypeStruct((3, frame_total, width), BF16),
            jax.ShapeDtypeStruct((3, width), F32),
        ),
        compiler_params=pltpu.CompilerParams(vmem_limit_bytes=16 * MIB),
        cost_estimate=pl.CostEstimate(
            flops=6 * width * col_width, bytes_accessed=4 * width * col_width, transcendentals=0
        ),
        name="weighted_fit",
    )(
        row,
        col,
        pltpu.with_memory_space_constraint(inverse_cov, pltpu.HBM),
        centres,
        rotations,
        coords,
        own_block,
        *others,
    )
    parts = lax.all_to_all(message, "row", split_axis=0, concat_axis=0, axis_index_groups=groups, tiled=True)
    summed = pl.pallas_call(
        add_parts_kernel,
        out_shape=jax.ShapeDtypeStruct((col_count * col_count, 8, 2 * frame_total), F32),
        in_specs=[vmem()],
        out_specs=vmem(),
        name="add_parts",
    )(parts)
    _, even_panel = lax.optimization_barrier((summed, even_panel))
    peers = [
        [(group * members + member) * col_count + place for group in range(col_count) for place in range(col_count)]
        for member in range(members)
    ]
    fits = lax.all_to_all(summed, ("row", "col"), split_axis=0, concat_axis=0, axis_index_groups=peers, tiled=True)
    panel = [None] * members
    panel[0::2] = even_panel
    panel[1::2] = [from_member(block, 1) for block in even_panel]

    strips = 4 if width % 64 == 0 else 1
    covariance, transforms = pl.pallas_call(
        functools.partial(covariance_kernel, members),
        grid_spec=pltpu.PrefetchScalarGridSpec(
            num_scalar_prefetch=2,
            grid=(1,),
            in_specs=[vmem()] * (4 + members),
            out_specs=(pl.BlockSpec(memory_space=pl.ANY), vmem()),
            scratch_shapes=[
                pltpu.VMEM((9, frame_total, LANES), F32),
                pltpu.VMEM((width, 3 * frame_total), BF16),
                pltpu.VMEM((2, 3 * frame_total, width), BF16),
                pltpu.VMEM((2 * strips, width // strips, width), F32),
                pltpu.SemaphoreType.DMA((2 * strips,)),
            ],
        ),
        out_shape=(
            jax.ShapeDtypeStruct((width, col_width), F32),
            jax.ShapeDtypeStruct((3, 3, local), F32),
        ),
        compiler_params=pltpu.CompilerParams(vmem_limit_bytes=24 * MIB),
        cost_estimate=pl.CostEstimate(
            flops=6 * frame_total * width * col_width, bytes_accessed=4 * width * col_width, transcendentals=0
        ),
        name="covariance",
    )(row, col, fits, rows_all, rows_centre, centres, *panel)
    return (covariance, transforms)


def solution(mesh):
    placed = (P("col", None, "row"), P(), P("row", "col"))
    return jax.shard_map(
        per_device,
        mesh=mesh,
        in_specs=placed,
        out_specs=(P("row", "col"), P(None, None, "col")),
        check_vma=False,
    )
```

```python
import functools

import jax
import jax.numpy as jnp
from jax import lax
from jax.experimental import pallas as pl
from jax.experimental.pallas import tpu as pltpu
from jax.sharding import PartitionSpec as P

POLAR = 12
LANES = 128
F32 = jnp.float32
BF16 = jnp.bfloat16
MIB = 1 << 20


def vmem():
    return pl.BlockSpec(memory_space=pltpu.VMEM)


def smem():
    return pl.BlockSpec(memory_space=pltpu.SMEM)


def three_pieces(value):
    high = value.astype(BF16)
    rest = value - high.astype(F32)
    mid = rest.astype(BF16)
    low = (rest - mid.astype(F32)).astype(BF16)
    return high, mid, low


def rotated_sum(rot, coords):
    depth = coords.shape[0] * coords.shape[1]
    flat = jnp.concatenate([rot[:, part, :] for part in range(3)], axis=1)
    padded = jnp.concatenate([flat, jnp.zeros((5, depth), F32)], axis=0)
    stacked = jnp.concatenate(three_pieces(padded), axis=0)
    product = jnp.dot(stacked, coords.reshape(depth, coords.shape[2]), preferred_element_type=F32)
    return (product[16:19] + product[8:11]) + product[0:3]


def partial_centre_kernel(frame_total, col, rot_ref, coords_ref, out_ref):
    local = coords_ref.shape[1]
    block = lax.broadcasted_iota(jnp.int32, rot_ref.shape, 2) // local
    rot = jnp.where(block == col[0], rot_ref[...], 0.0)
    coords = jnp.concatenate([coords_ref[...]] * (frame_total // local), axis=1)
    centre = rotated_sum(rot, coords) * (1.0 / frame_total)
    out_ref[...] = jnp.broadcast_to(centre[None], out_ref.shape)


def centre_of(parts_ref, row, col_count):
    total = parts_ref[row * col_count]
    for place in range(1, col_count):
        total = total + parts_ref[row * col_count + place]
    return total


def put_block(out_ref, block, value):
    local = value.shape[1]
    out_ref[:, pl.ds(pl.multiple_of(block * local, local), local), :] = value


def assemble_kernel(members, row, *refs):
    blocks, out_ref = refs[:-1], refs[-1]
    for step, ref in enumerate(blocks):
        put_block(out_ref, lax.rem(row[0] // members + step, len(blocks)), ref[...])


def weighted_fit_kernel(members, row, col, inv_ref, parts_ref, *refs):
    coords_refs, (out_ref, rows_ref, strips_ref, wide_ref, weighted_ref, sems) = refs[:-6], refs[-6:]
    strips, height, col_width = strips_ref.shape
    width = parts_ref.shape[2]

    def fetch(strip):
        rows = pl.ds(pl.multiple_of(strip * height, height), height)
        return pltpu.make_async_copy(inv_ref.at[rows, :], strips_ref.at[strip], sems.at[strip])

    for strip in range(strips):
        fetch(strip).start()
    for block in range(members):
        centre = centre_of(parts_ref, col[0] * members + block, len(coords_refs))
        for comp in range(3):
            factor = jnp.broadcast_to(centre[comp : comp + 1, :], (8, width))
            wide_ref[comp, :, block * width : (block + 1) * width] = factor
    for shift, ref in enumerate(coords_refs):
        put_block(rows_ref, lax.rem(col[0] + shift, len(coords_refs)), ref[...])
    lane = lax.broadcasted_iota(jnp.int32, (height, LANES), 1)
    chunks = col_width // LANES

    def strip_body(strip, carry):
        fetch(strip).wait()

        def body(chunk, sums):
            span = pl.ds(pl.multiple_of(chunk * LANES, LANES), LANES)
            value = strips_ref[strip, :, span].reshape(height // 8, 8, LANES)
            return tuple(sums[comp] + value * wide_ref[comp, :, span][None] for comp in range(3))

        sums = (jnp.zeros((height // 8, 8, LANES), F32),) * 3
        sums = lax.fori_loop(0, chunks, body, sums, unroll=12 if chunks % 12 == 0 else 1)
        packed = jnp.zeros((height, LANES), F32)
        for comp in range(3):
            total = jnp.sum(sums[comp].reshape(height, LANES), axis=1, keepdims=True)
            packed = jnp.where(lane == comp, total, packed)
        weighted_ref[pl.ds(pl.multiple_of(strip * height, height), height), :] = packed
        return carry

    lax.fori_loop(0, strips, strip_body, 0)
    frame_total = rows_ref.shape[1]
    rows = rows_ref[...].reshape(3 * frame_total, width)
    high, mid, low = (jnp.dot(rows, piece, preferred_element_type=F32) for piece in three_pieces(weighted_ref[...]))
    fits = ((low + mid) + high).T
    entries = [
        fits[comp : comp + 1, part * frame_total : (part + 1) * frame_total] for part in range(3) for comp in range(3)
    ]
    first = jnp.concatenate(entries[:8], axis=0)
    last = jnp.concatenate([entries[8], jnp.zeros((7, frame_total), F32)], axis=0)
    message = jnp.concatenate([first, last], axis=1)
    out_ref[...] = jnp.broadcast_to(message[None], out_ref.shape)


def orthogonalized(message, frame_total):
    fitted = [message[entry : entry + 1, :frame_total] for entry in range(8)]
    fitted.append(message[0:1, frame_total:])
    norm = functools.reduce(lambda a, b: a + b, [value * value for value in fitted])
    scaling = jnp.sqrt(1.0 + norm)
    current = [[fitted[3 * col + row] / scaling for col in range(3)] for row in range(3)]
    for _ in range(POLAR):
        square = [[None] * 3 for _ in range(3)]
        for a in range(3):
            for b in range(a, 3):
                x, y = current[a], current[b]
                square[a][b] = square[b][a] = x[0] * y[0] + x[1] * y[1] + x[2] * y[2]
        cubed = [
            [square[a][0] * current[0][b] + square[a][1] * current[1][b] + square[a][2] * current[2][b] for b in range(3)]
            for a in range(3)
        ]
        current = [[1.5 * current[a][b] - 0.5 * cubed[a][b] for b in range(3)] for a in range(3)]
    return current


def put_deviations(wide_ref, coords_ref, centre, chunk, dev_ref):
    frame_total = coords_ref.shape[1]
    span = slice(chunk * LANES, (chunk + 1) * LANES)
    coords = [coords_ref[part, :, span].astype(F32) for part in range(3)]
    for comp in range(3):
        moved = wide_ref[3 * comp] * coords[0]
        moved = moved + wide_ref[3 * comp + 1] * coords[1]
        moved = moved + wide_ref[3 * comp + 2] * coords[2]
        value = moved - centre[comp : comp + 1, span]
        dev_ref[comp * frame_total : (comp + 1) * frame_total, span] = value.astype(BF16)


def put_tile(wide_ref, coords_ref, centre, rows_dev_ref, dev_ref, out_ref):
    width = coords_ref.shape[2]
    scale = 1.0 / (3 * coords_ref.shape[1])
    stride = 2 * LANES if width % (2 * LANES) == 0 else LANES
    for start in range(0, width, stride):
        for chunk in range(start // LANES, (start + stride) // LANES):
            put_deviations(wide_ref, coords_ref, centre, chunk, dev_ref)
        product = jnp.dot(rows_dev_ref[...], dev_ref[:, start : start + stride], preferred_element_type=F32)
        out_ref[:, start : start + stride] = product * scale


def panel_centre(parts_ref, row, col, count, mask, col_count):
    members = 2 * count
    return centre_of(parts_ref, col[0] * members + (lax.rem(row[0], members) ^ mask), col_count)


def first_tiles_kernel(count, row, col, fits_ref, rows_ref, parts_ref, *refs):
    panel_refs = refs[:count]
    out_ref, rot_out_ref, wide_ref, rows_dev_ref, dev_ref = refs[count:]
    frame_total = rows_ref.shape[1]
    local = rot_out_ref.shape[2]

    @pl.when(pl.program_id(0) == 0)
    def _():
        current = orthogonalized(jnp.sum(fits_ref[...], axis=0), frame_total)
        for a in range(3):
            flat = jnp.concatenate(current[a], axis=0)
            kept = flat[:, :local]
            for block in range(1, frame_total // local):
                kept = jnp.where(col[0] == block, flat[:, block * local : (block + 1) * local], kept)
            rot_out_ref[a] = kept
        entries = [current[a][b] for a in range(3) for b in range(3)]
        columns = jnp.concatenate(entries + [jnp.zeros((7, frame_total), F32)], axis=0).T
        for entry in range(9):
            wide_ref[entry] = jnp.broadcast_to(columns[:, entry : entry + 1], (frame_total, LANES))
        centre = centre_of(parts_ref, row[0], frame_total // local)
        for chunk in range(rows_ref.shape[2] // LANES):
            put_deviations(wide_ref, rows_ref, centre, chunk, dev_ref)
        rows_dev_ref[...] = dev_ref[...].T

    for step in range(count):

        @pl.when(pl.program_id(0) == step)
        def _(step=step):
            centre = panel_centre(parts_ref, row, col, count, 2 * step, frame_total // local)
            put_tile(wide_ref, panel_refs[step], centre, rows_dev_ref, dev_ref, out_ref)


def last_tiles_kernel(count, col_count, row, col, before_ref, wide_ref, rows_dev_ref, parts_ref, *refs):
    panel_refs = refs[:count]
    out_ref, dev_ref = refs[count:]
    for step in range(count):

        @pl.when(pl.program_id(0) == step)
        def _(step=step):
            centre = panel_centre(parts_ref, row, col, count, 2 * step + 1, col_count)
            put_tile(wide_ref, panel_refs[step], centre, rows_dev_ref, dev_ref, out_ref)


def per_device(frames, rotations, inverse_cov):
    row_count, col_count = lax.axis_size("row"), lax.axis_size("col")
    members = row_count // col_count
    row = lax.axis_index("row").astype(jnp.int32).reshape(1)
    col = lax.axis_index("col").astype(jnp.int32).reshape(1)
    local, _, width = frames.shape
    frame_total = local * col_count
    device_total = row_count * col_count
    col_width = inverse_cov.shape[1]
    half = members // 2
    coords = jnp.transpose(frames, (1, 0, 2))

    def move(value, source_of, receives=lambda group, col: True):
        pairs = []
        for group in range(col_count):
            for member in range(members):
                for place in range(col_count):
                    if receives(group, place):
                        from_group, from_member, from_col = source_of(group, member, place)
                        source = (from_group * members + from_member) * col_count + from_col
                        pairs.append((source, (group * members + member) * col_count + place))
        return lax.ppermute(value, ("row", "col"), pairs)

    def from_panel_row(value, step):
        return move(value, lambda g, m, c: (c, m, (g + step) % col_count))

    def from_member(value, mask):
        return move(value, lambda g, m, c: (g, m ^ mask, c))

    def limit(mib):
        return pltpu.CompilerParams(vmem_limit_bytes=mib * MIB)

    panel_parts = [from_panel_row(coords, step) for step in range(col_count)]
    others = [move(coords, lambda g, m, c, s=step: (g, m, (c + s) % col_count)) for step in range(1, col_count)]
    repeated = pl.pallas_call(
        functools.partial(partial_centre_kernel, frame_total),
        out_shape=jax.ShapeDtypeStruct((device_total, 3, width), F32),
        in_specs=[smem(), vmem(), vmem()],
        out_specs=vmem(),
        compiler_params=limit(8),
        name="partial_centre",
    )(col, rotations, coords)
    parts = lax.all_to_all(repeated, ("row", "col"), split_axis=0, concat_axis=0, tiled=True)

    _, panel_parts = lax.optimization_barrier((parts, panel_parts))
    own_block = pl.pallas_call(
        functools.partial(assemble_kernel, members),
        out_shape=jax.ShapeDtypeStruct((3, frame_total, width), BF16),
        in_specs=[smem()] + [vmem()] * col_count,
        out_specs=vmem(),
        compiler_params=limit(4),
        name="assemble",
    )(row, *panel_parts)
    even_panel = [own_block] + [from_member(own_block, 2 * step) for step in range(1, members // 2)]

    height = 64 if width % 64 == 0 else 8
    inverse_cov = pltpu.with_memory_space_constraint(inverse_cov, pltpu.HBM)
    message, rows_all = pl.pallas_call(
        functools.partial(weighted_fit_kernel, members),
        in_specs=[smem(), smem(), pl.BlockSpec(memory_space=pl.ANY)] + [vmem()] * (1 + col_count),
        out_specs=(vmem(), vmem()),
        scratch_shapes=[
            pltpu.VMEM((width // height, height, col_width), F32),
            pltpu.VMEM((3, 8, col_width), F32),
            pltpu.VMEM((width, LANES), F32),
            pltpu.SemaphoreType.DMA((width // height,)),
        ],
        out_shape=(
            jax.ShapeDtypeStruct((device_total, 8, 2 * frame_total), F32),
            jax.ShapeDtypeStruct((3, frame_total, width), BF16),
        ),
        compiler_params=limit(28),
        cost_estimate=pl.CostEstimate(
            flops=6 * width * col_width, bytes_accessed=4 * width * col_width, transcendentals=0
        ),
        name="weighted_fit",
    )(row, col, inverse_cov, parts, coords, *others)
    fits = lax.all_to_all(message, ("row", "col"), split_axis=0, concat_axis=0, tiled=True)
    fits, even_panel = lax.optimization_barrier((fits, even_panel))
    odd_panel = [from_member(block, 1) for block in even_panel]

    def tile_spec(odd):
        return pl.BlockSpec((width, width), lambda i, row, *_: (0, lax.rem(row[0], members) ^ (2 * i + odd)))

    tiles_cost = pl.CostEstimate(
        flops=3 * frame_total * width * col_width, bytes_accessed=2 * width * col_width, transcendentals=0
    )
    dev_scratch = pltpu.VMEM((3 * frame_total, width), BF16)
    half_done, transforms, wide, rows_dev = pl.pallas_call(
        functools.partial(first_tiles_kernel, half),
        grid_spec=pltpu.PrefetchScalarGridSpec(
            num_scalar_prefetch=2,
            grid=(half,),
            in_specs=[vmem()] * (3 + half),
            out_specs=(tile_spec(0), vmem(), vmem(), vmem()),
            scratch_shapes=[dev_scratch],
        ),
        out_shape=(
            jax.ShapeDtypeStruct((width, col_width), F32),
            jax.ShapeDtypeStruct((3, 3, local), F32),
            jax.ShapeDtypeStruct((9, frame_total, LANES), F32),
            jax.ShapeDtypeStruct((width, 3 * frame_total), BF16),
        ),
        compiler_params=limit(16),
        cost_estimate=tiles_cost,
        name="steps_and_even_tiles",
    )(row, col, fits, rows_all, parts, *even_panel)
    covariance = pl.pallas_call(
        functools.partial(last_tiles_kernel, half, col_count),
        grid_spec=pltpu.PrefetchScalarGridSpec(
            num_scalar_prefetch=2,
            grid=(half,),
            in_specs=[pl.BlockSpec(memory_space=pl.ANY)] + [vmem()] * (3 + half),
            out_specs=tile_spec(1),
            scratch_shapes=[dev_scratch],
        ),
        out_shape=jax.ShapeDtypeStruct((width, col_width), F32),
        input_output_aliases={2: 0},
        compiler_params=limit(16),
        cost_estimate=tiles_cost,
        name="odd_tiles",
    )(row, col, half_done, wide, rows_dev, parts, *odd_panel)
    return (covariance, transforms)


def solution(mesh):
    placed = (P("col", None, "row"), P(), P("row", "col"))
    return jax.shard_map(
        per_device,
        mesh=mesh,
        in_specs=placed,
        out_specs=(P("row", "col"), P(None, None, "col")),
        check_vma=False,
    )
```

```python
import functools

import jax
import jax.numpy as jnp
from jax import lax
from jax.experimental import pallas as pl
from jax.experimental.pallas import tpu as pltpu
from jax.sharding import PartitionSpec as P

POLAR = 12
LANES = 128
F32 = jnp.float32
BF16 = jnp.bfloat16
MIB = 1 << 20


def vmem():
    return pl.BlockSpec(memory_space=pltpu.VMEM)


def hbm():
    return pl.BlockSpec(memory_space=pl.ANY)


def smem():
    return pl.BlockSpec(memory_space=pltpu.SMEM)


def three_pieces(value):
    high = value.astype(BF16)
    rest = value - high.astype(F32)
    mid = rest.astype(BF16)
    low = (rest - mid.astype(F32)).astype(BF16)
    return high, mid, low


def rotated_sum(rot, coords):
    depth = coords.shape[0] * coords.shape[1]
    flat = jnp.concatenate([rot[:, part, :] for part in range(3)], axis=1)
    padded = jnp.concatenate([flat, jnp.zeros((5, depth), F32)], axis=0)
    stacked = jnp.concatenate(three_pieces(padded), axis=0)
    product = jnp.dot(stacked, coords.reshape(depth, coords.shape[2]), preferred_element_type=F32)
    return (product[16:19] + product[8:11]) + product[0:3]


def fetch_all(sources, targets, sems):
    copies = [pltpu.make_async_copy(source, target, sems.at[k]) for k, (source, target) in enumerate(zip(sources, targets))]
    for copy in copies:
        copy.start()
    for copy in copies:
        copy.wait()


def partial_centre_kernel(frame_total, col, rot_hbm, coords_hbm, out_ref, rot_ref, coords_ref, sems):
    fetch_all((rot_hbm, coords_hbm), (rot_ref, coords_ref), sems)
    local = coords_ref.shape[1]
    block = lax.broadcasted_iota(jnp.int32, rot_ref.shape, 2) // local
    rot = jnp.where(block == col[0], rot_ref[...], 0.0)
    coords = jnp.concatenate([coords_ref[...]] * (frame_total // local), axis=1)
    out_ref[...] = rotated_sum(rot, coords) * (1.0 / frame_total)


def stack_kernel(*refs):
    for index, ref in enumerate(refs[:-1]):
        refs[-1][index] = ref[...]


def sum_kernel(*refs):
    total = refs[0][...]
    for ref in refs[1:-1]:
        total = total + ref[...]
    refs[-1][...] = total


def put_block(out_ref, block, value):
    local = value.shape[1]
    out_ref[:, pl.ds(pl.multiple_of(block * local, local), local), :] = value


def assemble_kernel(members, row, col, rows_ref, *refs):
    far_refs, across_refs, out_ref = refs[: len(refs) // 2], refs[len(refs) // 2 : -1], refs[-1]
    col_count = len(far_refs) + 1
    distance = lax.rem(col[0] + col_count - row[0] // members, col_count)

    @pl.when(distance == 0)
    def _():
        out_ref[...] = rows_ref[...]

    for step, ref in enumerate(far_refs):

        @pl.when(distance == step + 1)
        def _(ref=ref):
            put_block(out_ref, col[0], ref[...])
            for shift, across_ref in enumerate(across_refs):
                put_block(out_ref, lax.rem(col[0] + 1 + shift, col_count), across_ref[...])


def weighted_fit_kernel(members, row, col, inv_ref, rot_hbm, coords_hbm, even_ref, odd_ref, *refs):
    others, (out_ref, rows_ref, rows_centre_ref) = refs[:-9], refs[-9:-6]
    strips_ref, wide_ref, weighted_ref, rot_ref, sems, small_sems = refs[-6:]
    strips, height, col_width = strips_ref.shape
    width = even_ref.shape[2]
    local = coords_hbm.shape[1]

    def fetch(strip):
        rows = pl.ds(pl.multiple_of(strip * height, height), height)
        return pltpu.make_async_copy(inv_ref.at[rows, :], strips_ref.at[strip], sems.at[strip])

    own_rows = rows_ref.at[:, pl.ds(pl.multiple_of(col[0] * local, local), local), :]
    small = [
        pltpu.make_async_copy(rot_hbm, rot_ref, small_sems.at[0]),
        pltpu.make_async_copy(coords_hbm, own_rows, small_sems.at[1]),
    ]
    for copy in small:
        copy.start()
    for strip in range(strips):
        fetch(strip).start()
    member = lax.rem(row[0], members)
    for mask in range(members):
        centre_ref = odd_ref if mask % 2 else even_ref
        start = pl.multiple_of((member ^ mask) * width, LANES)
        for comp in range(3):
            factor = jnp.broadcast_to(centre_ref[mask // 2, comp : comp + 1, :], (8, width))
            wide_ref[comp, :, pl.ds(start, width)] = factor
    for shift, ref in enumerate(others):
        put_block(rows_ref, lax.rem(col[0] + 1 + shift, len(others) + 1), ref[...])
    for copy in small:
        copy.wait()
    rows_centre_ref[...] = rotated_sum(rot_ref[...], rows_ref[...]) * (1.0 / rows_ref.shape[1])
    lane = lax.broadcasted_iota(jnp.int32, (height, LANES), 1)
    chunks = col_width // LANES

    def strip_body(strip, carry):
        fetch(strip).wait()

        def body(chunk, sums):
            span = pl.ds(pl.multiple_of(chunk * LANES, LANES), LANES)
            value = strips_ref[strip, :, span].reshape(height // 8, 8, LANES)
            return tuple(sums[comp] + value * wide_ref[comp, :, span][None] for comp in range(3))

        sums = (jnp.zeros((height // 8, 8, LANES), F32),) * 3
        sums = lax.fori_loop(0, chunks, body, sums, unroll=12 if chunks % 12 == 0 else 1)
        packed = jnp.zeros((height, LANES), F32)
        for comp in range(3):
            total = jnp.sum(sums[comp].reshape(height, LANES), axis=1, keepdims=True)
            packed = jnp.where(lane == comp, total, packed)
        weighted_ref[pl.ds(pl.multiple_of(strip * height, height), height), :] = packed
        return carry

    lax.fori_loop(0, strips, strip_body, 0)
    frame_total = rows_ref.shape[1]
    rows = rows_ref[...].reshape(3 * frame_total, width)
    high, mid, low = (jnp.dot(rows, piece, preferred_element_type=F32) for piece in three_pieces(weighted_ref[...]))
    fits = ((low + mid) + high).T
    entries = [
        fits[comp : comp + 1, part * frame_total : (part + 1) * frame_total] for part in range(3) for comp in range(3)
    ]
    spare = out_ref.shape[2] - 9 * frame_total
    if spare:
        entries.append(jnp.zeros((1, spare), F32))
    message = jnp.concatenate(entries, axis=1)
    out_ref[...] = jnp.broadcast_to(message[None], out_ref.shape)


def orthogonalized(message, frame_total):
    fitted = [message[:, entry * frame_total : (entry + 1) * frame_total] for entry in range(9)]
    norm = functools.reduce(lambda a, b: a + b, [value * value for value in fitted])
    scaling = jnp.sqrt(1.0 + norm)
    current = [[fitted[3 * col + row] / scaling for col in range(3)] for row in range(3)]
    for _ in range(POLAR):
        square = [[None] * 3 for _ in range(3)]
        for a in range(3):
            for b in range(a, 3):
                x, y = current[a], current[b]
                square[a][b] = square[b][a] = x[0] * y[0] + x[1] * y[1] + x[2] * y[2]
        cubed = [
            [square[a][0] * current[0][b] + square[a][1] * current[1][b] + square[a][2] * current[2][b] for b in range(3)]
            for a in range(3)
        ]
        current = [[1.5 * current[a][b] - 0.5 * cubed[a][b] for b in range(3)] for a in range(3)]
    return current


def put_deviations(wide_ref, coords_ref, centre, chunk, dev_ref):
    frame_total = coords_ref.shape[1]
    span = slice(chunk * LANES, (chunk + 1) * LANES)
    coords = [coords_ref[part, :, span].astype(F32) for part in range(3)]
    for comp in range(3):
        moved = wide_ref[3 * comp] * coords[0]
        moved = moved + wide_ref[3 * comp + 1] * coords[1]
        moved = moved + wide_ref[3 * comp + 2] * coords[2]
        value = moved - centre[comp : comp + 1, span]
        dev_ref[comp * frame_total : (comp + 1) * frame_total, span] = value.astype(BF16)


def put_tile(wide_ref, coords_ref, centre, rows_dev_ref, dev_ref, out_ref):
    width = coords_ref.shape[2]
    scale = 1.0 / (3 * coords_ref.shape[1])
    stride = 2 * LANES if width % (2 * LANES) == 0 else LANES
    for start in range(0, width, stride):
        for chunk in range(start // LANES, (start + stride) // LANES):
            put_deviations(wide_ref, coords_ref, centre, chunk, dev_ref)
        product = jnp.dot(rows_dev_ref[...], dev_ref[:, start : start + stride], preferred_element_type=F32)
        out_ref[:, start : start + stride] = product * scale


def put_tiles(masks, wide_ref, even_ref, odd_ref, panel_refs, rows_dev_ref, dev_ref, out_ref):
    for step, mask in enumerate(masks):

        @pl.when(pl.program_id(0) == step)
        def _(step=step, mask=mask):
            centre = (odd_ref if mask % 2 else even_ref)[mask // 2]
            put_tile(wide_ref, panel_refs[step], centre, rows_dev_ref, dev_ref, out_ref)


def first_tiles_kernel(masks, row, col, fits_ref, rows_ref, rows_centre_ref, even_ref, odd_ref, *refs):
    panel_refs = refs[: len(masks)]
    out_ref, rot_out_ref, wide_ref, rows_dev_ref, dev_ref = refs[len(masks) :]
    frame_total = rows_ref.shape[1]
    local = rot_out_ref.shape[2]

    @pl.when(pl.program_id(0) == 0)
    def _():
        current = orthogonalized(jnp.sum(fits_ref[...], axis=0), frame_total)
        for a in range(3):
            flat = jnp.concatenate(current[a], axis=0)
            kept = flat[:, :local]
            for block in range(1, frame_total // local):
                kept = jnp.where(col[0] == block, flat[:, block * local : (block + 1) * local], kept)
            rot_out_ref[a] = kept
        entries = [current[a][b] for a in range(3) for b in range(3)]
        columns = jnp.concatenate(entries + [jnp.zeros((7, frame_total), F32)], axis=0).T
        for entry in range(9):
            wide_ref[entry] = jnp.broadcast_to(columns[:, entry : entry + 1], (frame_total, LANES))
        centre = rows_centre_ref[...]
        for chunk in range(rows_ref.shape[2] // LANES):
            put_deviations(wide_ref, rows_ref, centre, chunk, dev_ref)
        rows_dev_ref[...] = dev_ref[...].T

    put_tiles(masks, wide_ref, even_ref, odd_ref, panel_refs, rows_dev_ref, dev_ref, out_ref)


def more_tiles_kernel(masks, row, before_ref, wide_ref, rows_dev_ref, even_ref, odd_ref, *refs):
    panel_refs, (out_ref, dev_ref) = refs[: len(masks)], refs[len(masks) :]
    put_tiles(masks, wide_ref, even_ref, odd_ref, panel_refs, rows_dev_ref, dev_ref, out_ref)


def per_device(frames, rotations, inverse_cov):
    row_count, col_count = lax.axis_size("row"), lax.axis_size("col")
    members = row_count // col_count
    row = lax.axis_index("row").astype(jnp.int32).reshape(1)
    col = lax.axis_index("col").astype(jnp.int32).reshape(1)
    local, _, width = frames.shape
    frame_total = local * col_count
    device_total = row_count * col_count
    col_width = inverse_cov.shape[1]
    half = members // 2
    coords = jnp.transpose(frames, (1, 0, 2))

    def limit(mib):
        return pltpu.CompilerParams(vmem_limit_bytes=mib * MIB)

    def move(value, source_of, receives=lambda group, col: True):
        pairs = []
        for group in range(col_count):
            for member in range(members):
                for place in range(col_count):
                    if receives(group, place):
                        from_group, from_member, from_col = source_of(group, member, place)
                        source = (from_group * members + from_member) * col_count + from_col
                        pairs.append((source, (group * members + member) * col_count + place))
        return lax.ppermute(value, ("row", "col"), pairs)

    def from_panel_row(value, step):
        return move(value, lambda g, m, c: (c, m, (g + step) % col_count))

    def from_member(value, mask):
        return move(value, lambda g, m, c: (g, m ^ mask, c))

    def limit(mib):
        return pltpu.CompilerParams(vmem_limit_bytes=mib * MIB)

    def after(first, value):
        return lax.optimization_barrier((first, value))[1]

    def small_kernel(kernel, shape, name, *values):
        return pl.pallas_call(
            kernel,
            out_shape=jax.ShapeDtypeStruct(shape, F32),
            in_specs=[vmem()] * len(values),
            out_specs=vmem(),
            compiler_params=limit(4),
            name=name,
        )(*values)

    partial = pl.pallas_call(
        functools.partial(partial_centre_kernel, frame_total),
        out_shape=jax.ShapeDtypeStruct((3, width), F32),
        in_specs=[smem(), hbm(), hbm()],
        out_specs=vmem(),
        scratch_shapes=[
            pltpu.VMEM(rotations.shape, F32),
            pltpu.VMEM(coords.shape, BF16),
            pltpu.SemaphoreType.DMA((2,)),
        ],
        compiler_params=limit(8),
        name="partial_centre",
    )(col, rotations, coords)
    parts = [from_panel_row(partial, step) for step in range(col_count)]

    late_coords = after(partial, coords)
    others = [move(late_coords, lambda g, m, c, s=step: (g, m, (c + s) % col_count)) for step in range(1, col_count)]
    far = [
        move(late_coords, lambda g, m, c, s=step: ((g + s) % col_count, m, c)) for step in range(1, col_count)
    ]

    own_centre = small_kernel(sum_kernel, (3, width), "add_centre", *parts)
    centres = [own_centre] + [from_member(own_centre, 2 * step) for step in range(1, half)]
    centres, others = lax.optimization_barrier((centres, others))
    even_centres = small_kernel(stack_kernel, (half, 3, width), "stack_centres", *centres)
    odd_centres = from_member(even_centres, 1)

    far = after(odd_centres, far)
    distance = lax.rem(col[0] + col_count - row[0] // members, col_count)
    across = []
    for step in range(1, col_count):
        held = far[0]
        if col_count > 2:
            held = lax.select_n(lax.rem(distance + col_count - step, col_count), late_coords, *far)
        across.append(move(held, lambda g, m, c, s=step: (g, m, (c + s) % col_count), lambda g, c: g != c))

    height = 64 if width % 64 == 0 else 8
    message_width = -(-9 * frame_total // LANES) * LANES
    message, rows_all, rows_centre = pl.pallas_call(
        functools.partial(weighted_fit_kernel, members),
        in_specs=[smem(), smem()] + [hbm()] * 3 + [vmem()] * (1 + col_count),
        out_specs=(vmem(), vmem(), vmem()),
        scratch_shapes=[
            pltpu.VMEM((width // height, height, col_width), F32),
            pltpu.VMEM((3, 8, col_width), F32),
            pltpu.VMEM((width, LANES), F32),
            pltpu.VMEM(rotations.shape, F32),
            pltpu.SemaphoreType.DMA((width // height,)),
            pltpu.SemaphoreType.DMA((2,)),
        ],
        out_shape=(
            jax.ShapeDtypeStruct((device_total, 1, message_width), F32),
            jax.ShapeDtypeStruct((3, frame_total, width), BF16),
            jax.ShapeDtypeStruct((3, width), F32),
        ),
        compiler_params=limit(28),
        cost_estimate=pl.CostEstimate(
            flops=6 * width * col_width, bytes_accessed=4 * width * col_width, transcendentals=0
        ),
        name="weighted_fit",
    )(
        row,
        col,
        pltpu.with_memory_space_constraint(inverse_cov, pltpu.HBM),
        rotations,
        coords,
        even_centres,
        odd_centres,
        *others,
    )
    fits = lax.all_to_all(message, ("row", "col"), split_axis=0, concat_axis=0, tiled=True)

    own_block = pl.pallas_call(
        functools.partial(assemble_kernel, members),
        out_shape=jax.ShapeDtypeStruct((3, frame_total, width), BF16),
        in_specs=[smem(), smem()] + [vmem()] * (2 * col_count - 1),
        out_specs=vmem(),
        compiler_params=limit(4),
        name="assemble",
    )(row, col, rows_all, *far, *across)
    panel = [own_block, from_member(own_block, 1)]
    evens = [from_member(own_block, mask) for mask in range(2, members, 2)]

    def tile_spec(masks):
        def index(i, row, *_):
            mask = masks[-1]
            for step, value in enumerate(masks[:-1]):
                mask = jnp.where(i == step, value, mask)
            return (0, lax.rem(row[0], members) ^ mask)

        return pl.BlockSpec((width, width), index)

    def tiles_cost(masks):
        return pl.CostEstimate(
            flops=6 * frame_total * width * width * len(masks),
            bytes_accessed=4 * width * width * len(masks),
            transcendentals=0,
        )

    dev_scratch = pltpu.VMEM((3 * frame_total, width), BF16)
    masks = (0, 1)
    covariance, transforms, wide, rows_dev = pl.pallas_call(
        functools.partial(first_tiles_kernel, masks),
        grid_spec=pltpu.PrefetchScalarGridSpec(
            num_scalar_prefetch=2,
            grid=(len(masks),),
            in_specs=[vmem()] * (5 + len(masks)),
            out_specs=(tile_spec(masks), vmem(), vmem(), vmem()),
            scratch_shapes=[dev_scratch],
        ),
        out_shape=(
            jax.ShapeDtypeStruct((width, col_width), F32),
            jax.ShapeDtypeStruct((3, 3, local), F32),
            jax.ShapeDtypeStruct((9, frame_total, LANES), F32),
            jax.ShapeDtypeStruct((width, 3 * frame_total), BF16),
        ),
        compiler_params=limit(16),
        cost_estimate=tiles_cost(masks),
        name="steps_and_first_tiles",
    )(row, col, fits, rows_all, rows_centre, even_centres, odd_centres, *panel)

    def more_tiles(covariance, masks, blocks, name):
        return pl.pallas_call(
            functools.partial(more_tiles_kernel, masks),
            grid_spec=pltpu.PrefetchScalarGridSpec(
                num_scalar_prefetch=1,
                grid=(len(masks),),
                in_specs=[pl.BlockSpec(memory_space=pl.ANY)] + [vmem()] * (4 + len(masks)),
                out_specs=tile_spec(masks),
                scratch_shapes=[dev_scratch],
            ),
            out_shape=jax.ShapeDtypeStruct((width, col_width), F32),
            input_output_aliases={1: 0},
            compiler_params=limit(16),
            cost_estimate=tiles_cost(masks),
            name=name,
        )(row, covariance, wide, rows_dev, even_centres, odd_centres, *blocks)

    if members > 2:
        evens = after(wide, evens)
        odds = [from_member(block, 1) for block in evens]
        covariance = more_tiles(covariance, tuple(range(2, members, 2)), evens, "even_tiles")
        covariance = more_tiles(covariance, tuple(range(3, members, 2)), odds, "odd_tiles")
    return (covariance, transforms)


def solution(mesh):
    placed = (P("col", None, "row"), P(), P("row", "col"))
    return jax.shard_map(
        per_device,
        mesh=mesh,
        in_specs=placed,
        out_specs=(P("row", "col"), P(None, None, "col")),
        check_vma=False,
    )
```

```python
import functools

import jax
import jax.numpy as jnp
from jax import lax
from jax.experimental import pallas as pl
from jax.experimental.pallas import tpu as pltpu
from jax.sharding import PartitionSpec as P

POLAR = 12
LANES = 128
F32 = jnp.float32
BF16 = jnp.bfloat16
MIB = 1 << 20


def vmem():
    return pl.BlockSpec(memory_space=pltpu.VMEM)


def hbm():
    return pl.BlockSpec(memory_space=pl.ANY)


def smem():
    return pl.BlockSpec(memory_space=pltpu.SMEM)


def three_pieces(value):
    high = value.astype(BF16)
    rest = value - high.astype(F32)
    mid = rest.astype(BF16)
    low = (rest - mid.astype(F32)).astype(BF16)
    return high, mid, low


def rotated_sum(rot, coords):
    depth = coords.shape[0] * coords.shape[1]
    flat = jnp.concatenate([rot[:, part, :] for part in range(3)], axis=1)
    padded = jnp.concatenate([flat, jnp.zeros((5, depth), F32)], axis=0)
    stacked = jnp.concatenate(three_pieces(padded), axis=0)
    product = jnp.dot(stacked, coords.reshape(depth, coords.shape[2]), preferred_element_type=F32)
    return (product[16:19] + product[8:11]) + product[0:3]


def stack_kernel(*refs):
    for index, ref in enumerate(refs[:-1]):
        refs[-1][index] = ref[...]


def put_block(out_ref, block, value):
    local = value.shape[1]
    out_ref[:, pl.ds(pl.multiple_of(block * local, local), local), :] = value


def rows_kernel(col, rot_hbm, coords_hbm, *refs):
    others, (rows_ref, centre_ref, rot_ref, sems) = refs[:-4], refs[-4:]
    local = coords_hbm.shape[1]
    own_rows = rows_ref.at[:, pl.ds(pl.multiple_of(col[0] * local, local), local), :]
    copies = [
        pltpu.make_async_copy(rot_hbm, rot_ref, sems.at[0]),
        pltpu.make_async_copy(coords_hbm, own_rows, sems.at[1]),
    ]
    for copy in copies:
        copy.start()
    for shift, ref in enumerate(others):
        put_block(rows_ref, lax.rem(col[0] + 1 + shift, len(others) + 1), ref[...])
    for copy in copies:
        copy.wait()
    centre_ref[...] = rotated_sum(rot_ref[...], rows_ref[...]) * (1.0 / rows_ref.shape[1])


def assemble_kernel(members, row, col, rot_ref, rows_ref, *refs):
    sources, (out_ref, centre_ref) = refs[:-2], refs[-2:]
    far_refs, across_refs = sources[: len(sources) // 2], sources[len(sources) // 2 :]
    col_count = len(far_refs) + 1
    distance = lax.rem(col[0] + col_count - row[0] // members, col_count)

    @pl.when(distance == 0)
    def _():
        out_ref[...] = rows_ref[...]

    for step, ref in enumerate(far_refs):

        @pl.when(distance == step + 1)
        def _(ref=ref):
            put_block(out_ref, col[0], ref[...])
            for shift, across_ref in enumerate(across_refs):
                put_block(out_ref, lax.rem(col[0] + 1 + shift, col_count), across_ref[...])

    centre_ref[...] = rotated_sum(rot_ref[...], out_ref[...]) * (1.0 / out_ref.shape[1])


def weighted_fit_kernel(members, row, inv_ref, even_ref, odd_ref, rows_ref, out_ref, strips_ref, wide_ref, weighted_ref, sems):
    strips, height, col_width = strips_ref.shape
    width = even_ref.shape[2]

    def fetch(strip):
        rows = pl.ds(pl.multiple_of(strip * height, height), height)
        return pltpu.make_async_copy(inv_ref.at[rows, :], strips_ref.at[strip], sems.at[strip])

    for strip in range(strips):
        fetch(strip).start()
    member = lax.rem(row[0], members)
    for mask in range(members):
        centre_ref = odd_ref if mask % 2 else even_ref
        start = pl.multiple_of((member ^ mask) * width, LANES)
        for comp in range(3):
            factor = jnp.broadcast_to(centre_ref[mask // 2, comp : comp + 1, :], (8, width))
            wide_ref[comp, :, pl.ds(start, width)] = factor
    lane = lax.broadcasted_iota(jnp.int32, (height, LANES), 1)
    chunks = col_width // LANES

    def strip_body(strip, carry):
        fetch(strip).wait()

        def body(chunk, sums):
            span = pl.ds(pl.multiple_of(chunk * LANES, LANES), LANES)
            value = strips_ref[strip, :, span].reshape(height // 8, 8, LANES)
            return tuple(sums[comp] + value * wide_ref[comp, :, span][None] for comp in range(3))

        sums = (jnp.zeros((height // 8, 8, LANES), F32),) * 3
        sums = lax.fori_loop(0, chunks, body, sums, unroll=12 if chunks % 12 == 0 else 1)
        packed = jnp.zeros((height, LANES), F32)
        for comp in range(3):
            total = jnp.sum(sums[comp].reshape(height, LANES), axis=1, keepdims=True)
            packed = jnp.where(lane == comp, total, packed)
        weighted_ref[pl.ds(pl.multiple_of(strip * height, height), height), :] = packed
        return carry

    lax.fori_loop(0, strips, strip_body, 0)
    frame_total = rows_ref.shape[1]
    rows = rows_ref[...].reshape(3 * frame_total, width)
    high, mid, low = (jnp.dot(rows, piece, preferred_element_type=F32) for piece in three_pieces(weighted_ref[...]))
    fits = ((low + mid) + high).T
    entries = [
        fits[comp : comp + 1, part * frame_total : (part + 1) * frame_total] for part in range(3) for comp in range(3)
    ]
    first = jnp.concatenate(entries[:8], axis=0)
    last = jnp.concatenate([entries[8], jnp.zeros((7, frame_total), F32)], axis=0)
    message = jnp.concatenate([first, last], axis=1)
    out_ref[...] = jnp.broadcast_to(message[None], out_ref.shape)


def orthogonalized(message, frame_total):
    fitted = [message[entry : entry + 1, :frame_total] for entry in range(8)]
    fitted.append(message[0:1, frame_total:])
    norm = functools.reduce(lambda a, b: a + b, [value * value for value in fitted])
    scaling = jnp.sqrt(1.0 + norm)
    current = [[fitted[3 * col + row] / scaling for col in range(3)] for row in range(3)]
    for _ in range(POLAR):
        square = [[None] * 3 for _ in range(3)]
        for a in range(3):
            for b in range(a, 3):
                x, y = current[a], current[b]
                square[a][b] = square[b][a] = x[0] * y[0] + x[1] * y[1] + x[2] * y[2]
        cubed = [
            [square[a][0] * current[0][b] + square[a][1] * current[1][b] + square[a][2] * current[2][b] for b in range(3)]
            for a in range(3)
        ]
        current = [[1.5 * current[a][b] - 0.5 * cubed[a][b] for b in range(3)] for a in range(3)]
    return current


def put_deviations(wide_ref, coords_ref, centre, source, dev_ref, target):
    frame_total = coords_ref.shape[1]
    span = slice(source, source + LANES)
    coords = [coords_ref[part, :, span].astype(F32) for part in range(3)]
    for comp in range(3):
        moved = wide_ref[3 * comp] * coords[0]
        moved = moved + wide_ref[3 * comp + 1] * coords[1]
        moved = moved + wide_ref[3 * comp + 2] * coords[2]
        value = moved - centre[comp : comp + 1, span]
        dev_ref[comp * frame_total : (comp + 1) * frame_total, target : target + LANES] = value.astype(BF16)


def put_tile(wide_ref, coords_ref, centre, first, rows_dev_ref, dev_ref, out_ref):
    width = out_ref.shape[1]
    scale = 1.0 / (3 * coords_ref.shape[1])
    for start in range(0, width, LANES):
        put_deviations(wide_ref, coords_ref, centre, first + start, dev_ref, start)
    product = jnp.dot(rows_dev_ref[...], dev_ref[:, :width], preferred_element_type=F32)
    out_ref[...] = product * scale


def put_tiles(wide_ref, centre_ref, panel_refs, rows_dev_ref, dev_ref, out_ref):
    width, pieces = out_ref.shape[1], centre_ref.shape[2] // out_ref.shape[1]
    for step in range(len(panel_refs) * pieces):

        @pl.when(pl.program_id(0) == step)
        def _(block=step // pieces, first=step % pieces * width):
            put_tile(wide_ref, panel_refs[block], centre_ref[block], first, rows_dev_ref, dev_ref, out_ref)


def first_tiles_kernel(half, row, col, fits_ref, rows_ref, rows_centre_ref, centre_ref, *refs):
    panel_refs = refs[:half]
    out_ref, rot_out_ref, wide_ref, rows_dev_ref, dev_ref = refs[half:]
    frame_total = rows_ref.shape[1]
    local = rot_out_ref.shape[2]

    @pl.when(pl.program_id(0) == 0)
    def _():
        current = orthogonalized(jnp.sum(fits_ref[...], axis=0), frame_total)
        for a in range(3):
            flat = jnp.concatenate(current[a], axis=0)
            kept = flat[:, :local]
            for block in range(1, frame_total // local):
                kept = jnp.where(col[0] == block, flat[:, block * local : (block + 1) * local], kept)
            rot_out_ref[a] = kept
        entries = [current[a][b] for a in range(3) for b in range(3)]
        columns = jnp.concatenate(entries + [jnp.zeros((7, frame_total), F32)], axis=0).T
        for entry in range(9):
            wide_ref[entry] = jnp.broadcast_to(columns[:, entry : entry + 1], (frame_total, LANES))
        centre = rows_centre_ref[...]
        for chunk in range(rows_ref.shape[2] // LANES):
            put_deviations(wide_ref, rows_ref, centre, chunk * LANES, dev_ref, chunk * LANES)
        rows_dev_ref[...] = dev_ref[...].T

    put_tiles(wide_ref, centre_ref, panel_refs, rows_dev_ref, dev_ref, out_ref)


def more_tiles_kernel(half, row, before_ref, wide_ref, rows_dev_ref, centre_ref, *refs):
    panel_refs, (out_ref, dev_ref) = refs[:half], refs[half:]
    put_tiles(wide_ref, centre_ref, panel_refs, rows_dev_ref, dev_ref, out_ref)


def per_device(frames, rotations, inverse_cov):
    row_count, col_count = lax.axis_size("row"), lax.axis_size("col")
    members = row_count // col_count
    row = lax.axis_index("row").astype(jnp.int32).reshape(1)
    col = lax.axis_index("col").astype(jnp.int32).reshape(1)
    local, _, width = frames.shape
    frame_total = local * col_count
    device_total = row_count * col_count
    col_width = inverse_cov.shape[1]
    half = members // 2
    coords = jnp.transpose(frames, (1, 0, 2))

    def limit(mib):
        return pltpu.CompilerParams(vmem_limit_bytes=mib * MIB)

    def move(value, source_of, receives=lambda group, col: True):
        pairs = []
        for group in range(col_count):
            for member in range(members):
                for place in range(col_count):
                    if receives(group, place):
                        from_group, from_member, from_col = source_of(group, member, place)
                        source = (from_group * members + from_member) * col_count + from_col
                        pairs.append((source, (group * members + member) * col_count + place))
        return lax.ppermute(value, ("row", "col"), pairs)

    def from_panel_row(value, step):
        return move(value, lambda g, m, c: (c, m, (g + step) % col_count))

    def from_member(value, mask):
        return move(value, lambda g, m, c: (g, m ^ mask, c))

    def limit(mib):
        return pltpu.CompilerParams(vmem_limit_bytes=mib * MIB)

    def after(first, value):
        return lax.optimization_barrier((first, value))[1]

    def small_kernel(kernel, shape, name, *values):
        return pl.pallas_call(
            kernel,
            out_shape=jax.ShapeDtypeStruct(shape, F32),
            in_specs=[vmem()] * len(values),
            out_specs=vmem(),
            compiler_params=limit(4),
            name=name,
        )(*values)

    def in_hbm(value):
        return pltpu.with_memory_space_constraint(value, pltpu.HBM)

    far = [move(coords, lambda g, m, c, s=step: ((g + s) % col_count, m, c)) for step in range(1, col_count)]
    others = [move(coords, lambda g, m, c, s=step: (g, m, (c + s) % col_count)) for step in range(1, col_count)]
    rows_all, rows_centre, rot = pl.pallas_call(
        rows_kernel,
        out_shape=(
            jax.ShapeDtypeStruct((3, frame_total, width), BF16),
            jax.ShapeDtypeStruct((3, width), F32),
            jax.ShapeDtypeStruct(rotations.shape, F32),
        ),
        in_specs=[smem(), hbm(), hbm()] + [vmem()] * (col_count - 1),
        out_specs=(vmem(), vmem(), vmem()),
        scratch_shapes=[pltpu.SemaphoreType.DMA((2,))],
        compiler_params=limit(8),
        name="rows",
    )(col, in_hbm(rotations), in_hbm(coords), *others)

    distance = lax.rem(col[0] + col_count - row[0] // members, col_count)
    across = []
    for step in range(1, col_count):
        held = far[0]
        if col_count > 2:
            held = lax.select_n(lax.rem(distance + col_count - step, col_count), coords, *far)
        across.append(move(held, lambda g, m, c, s=step: (g, m, (c + s) % col_count), lambda g, c: g != c))
    own_block, own_centre = pl.pallas_call(
        functools.partial(assemble_kernel, members),
        out_shape=(
            jax.ShapeDtypeStruct((3, frame_total, width), BF16),
            jax.ShapeDtypeStruct((3, width), F32),
        ),
        in_specs=[smem(), smem()] + [vmem()] * (2 * col_count),
        out_specs=(vmem(), vmem()),
        compiler_params=limit(8),
        name="assemble",
    )(row, col, rot, rows_all, *far, *across)

    centres = [own_centre] + [from_member(own_centre, 2 * step) for step in range(1, half)]
    evens = [own_block] + [from_member(own_block, 2 * step) for step in range(1, half)]
    even_centres = small_kernel(stack_kernel, (half, 3, width), "stack_centres", *centres)
    odd_centres = from_member(even_centres, 1)

    height = 64 if width % 64 == 0 else 8
    message = pl.pallas_call(
        functools.partial(weighted_fit_kernel, members),
        in_specs=[smem(), hbm()] + [vmem()] * 3,
        out_specs=vmem(),
        scratch_shapes=[
            pltpu.VMEM((width // height, height, col_width), F32),
            pltpu.VMEM((3, 8, col_width), F32),
            pltpu.VMEM((width, LANES), F32),
            pltpu.SemaphoreType.DMA((width // height,)),
        ],
        out_shape=jax.ShapeDtypeStruct((device_total, 8, 2 * frame_total), F32),
        compiler_params=limit(28),
        cost_estimate=pl.CostEstimate(
            flops=6 * width * col_width, bytes_accessed=4 * width * col_width, transcendentals=0
        ),
        name="weighted_fit",
    )(row, in_hbm(inverse_cov), even_centres, odd_centres, rows_all)
    fits = lax.all_to_all(message, ("row", "col"), split_axis=0, concat_axis=0, tiled=True)
    evens = after(fits, evens)
    odds = [from_member(block, 1) for block in evens]

    pieces = 2 if width % (2 * LANES) == 0 else 1

    def tile_spec(odd):
        def index(i, row, *_):
            return (0, (lax.rem(row[0], members) ^ (2 * (i // pieces) + odd)) * pieces + lax.rem(i, pieces))

        return pl.BlockSpec((width, width // pieces), index)

    tiles_cost = pl.CostEstimate(
        flops=3 * frame_total * width * col_width, bytes_accessed=2 * width * col_width, transcendentals=0
    )
    dev_scratch = pltpu.VMEM((3 * frame_total, width), BF16)
    covariance, transforms, wide, rows_dev = pl.pallas_call(
        functools.partial(first_tiles_kernel, half),
        grid_spec=pltpu.PrefetchScalarGridSpec(
            num_scalar_prefetch=2,
            grid=(half * pieces,),
            in_specs=[vmem()] * (4 + half),
            out_specs=(tile_spec(0), vmem(), vmem(), vmem()),
            scratch_shapes=[dev_scratch],
        ),
        out_shape=(
            jax.ShapeDtypeStruct((width, col_width), F32),
            jax.ShapeDtypeStruct((3, 3, local), F32),
            jax.ShapeDtypeStruct((9, frame_total, LANES), F32),
            jax.ShapeDtypeStruct((width, 3 * frame_total), BF16),
        ),
        compiler_params=limit(16),
        cost_estimate=tiles_cost,
        name="steps_and_even_tiles",
    )(row, col, fits, rows_all, rows_centre, even_centres, *evens)
    covariance = pl.pallas_call(
        functools.partial(more_tiles_kernel, half),
        grid_spec=pltpu.PrefetchScalarGridSpec(
            num_scalar_prefetch=1,
            grid=(half * pieces,),
            in_specs=[hbm()] + [vmem()] * (3 + half),
            out_specs=tile_spec(1),
            scratch_shapes=[dev_scratch],
        ),
        out_shape=jax.ShapeDtypeStruct((width, col_width), F32),
        input_output_aliases={1: 0},
        compiler_params=limit(16),
        cost_estimate=tiles_cost,
        name="odd_tiles",
    )(row, covariance, wide, rows_dev, odd_centres, *odds)
    return (covariance, transforms)


def solution(mesh):
    placed = (P("col", None, "row"), P(), P("row", "col"))
    return jax.shard_map(
        per_device,
        mesh=mesh,
        in_specs=placed,
        out_specs=(P("row", "col"), P(None, None, "col")),
        check_vma=False,
    )
```

```python
import functools

import jax
import jax.numpy as jnp
from jax import lax
from jax.experimental import pallas as pl
from jax.experimental.pallas import tpu as pltpu
from jax.sharding import PartitionSpec as P

POLAR = 12
LANES = 128
F32 = jnp.float32
BF16 = jnp.bfloat16
MIB = 1 << 20


def vmem():
    return pl.BlockSpec(memory_space=pltpu.VMEM)


def hbm():
    return pl.BlockSpec(memory_space=pl.ANY)


def smem():
    return pl.BlockSpec(memory_space=pltpu.SMEM)


def three_pieces(value):
    high = value.astype(BF16)
    rest = value - high.astype(F32)
    mid = rest.astype(BF16)
    low = (rest - mid.astype(F32)).astype(BF16)
    return high, mid, low


def rotated_sum(rot, coords):
    depth = coords.shape[0] * coords.shape[1]
    flat = jnp.concatenate([rot[:, part, :] for part in range(3)], axis=1)
    padded = jnp.concatenate([flat, jnp.zeros((5, depth), F32)], axis=0)
    stacked = jnp.concatenate(three_pieces(padded), axis=0)
    product = jnp.dot(stacked, coords.reshape(depth, coords.shape[2]), preferred_element_type=F32)
    return (product[16:19] + product[8:11]) + product[0:3]


def stack_kernel(*refs):
    for index, ref in enumerate(refs[:-1]):
        refs[-1][index] = ref[...]


def put_block(out_ref, block, value):
    local = value.shape[1]
    out_ref[:, pl.ds(pl.multiple_of(block * local, local), local), :] = value


def rows_kernel(col, token_ref, rot_hbm, coords_hbm, *refs):
    others, (rows_ref, centre_ref, rot_ref, sems) = refs[:-4], refs[-4:]
    local = coords_hbm.shape[1]
    own_rows = rows_ref.at[:, pl.ds(pl.multiple_of(col[0] * local, local), local), :]
    copies = [
        pltpu.make_async_copy(rot_hbm, rot_ref, sems.at[0]),
        pltpu.make_async_copy(coords_hbm, own_rows, sems.at[1]),
    ]
    for copy in copies:
        copy.start()
    for shift, ref in enumerate(others):
        put_block(rows_ref, lax.rem(col[0] + 1 + shift, len(others) + 1), ref[...])
    for copy in copies:
        copy.wait()
    centre_ref[...] = rotated_sum(rot_ref[...], rows_ref[...]) * (1.0 / rows_ref.shape[1])


def assemble_kernel(members, row, col, rot_ref, rows_ref, *refs):
    sources, (out_ref, centre_ref) = refs[:-2], refs[-2:]
    far_refs, across_refs = sources[: len(sources) // 2], sources[len(sources) // 2 :]
    col_count = len(far_refs) + 1
    distance = lax.rem(col[0] + col_count - row[0] // members, col_count)

    @pl.when(distance == 0)
    def _():
        out_ref[...] = rows_ref[...]

    for step, ref in enumerate(far_refs):

        @pl.when(distance == step + 1)
        def _(ref=ref):
            put_block(out_ref, col[0], ref[...])
            for shift, across_ref in enumerate(across_refs):
                put_block(out_ref, lax.rem(col[0] + 1 + shift, col_count), across_ref[...])

    centre_ref[...] = rotated_sum(rot_ref[...], out_ref[...]) * (1.0 / out_ref.shape[1])


def fetch_kernel(source_ref, target_ref, token_ref, sems):
    height = source_ref.shape[0] // sems.shape[0]
    copies = []
    for strip in range(sems.shape[0]):
        span = pl.ds(strip * height, height)
        copies.append(pltpu.make_async_copy(source_ref.at[span, :], target_ref.at[span, :], sems.at[strip]))
        copies[-1].start()
    for copy in copies:
        copy.wait()
    token_ref[...] = jnp.zeros_like(token_ref)


def weighted_fit_kernel(members, height, row, inv_ref, even_ref, odd_ref, rows_ref, out_ref, wide_ref, weighted_ref):
    width = even_ref.shape[2]
    member = lax.rem(row[0], members)
    for mask in range(members):
        centre_ref = odd_ref if mask % 2 else even_ref
        for comp in range(3):
            factor = jnp.broadcast_to(centre_ref[mask // 2, comp : comp + 1, :], (8, width))
            wide_ref[comp, :, mask * width : (mask + 1) * width] = factor
    lane = lax.broadcasted_iota(jnp.int32, (height, LANES), 1)

    def strip_body(strip, carry):
        strip_rows = pl.ds(pl.multiple_of(strip * height, height), height)

        def body(mask, sums):
            block = member ^ mask
            for start in range(0, width, LANES):
                span = pl.ds(pl.multiple_of(block * width + start, LANES), LANES)
                value = inv_ref[strip_rows, span].reshape(height // 8, 8, LANES)
                span = pl.ds(pl.multiple_of(mask * width + start, LANES), LANES)
                sums = tuple(sums[comp] + value * wide_ref[comp, :, span][None] for comp in range(3))
            return sums

        sums = (jnp.zeros((height // 8, 8, LANES), F32),) * 3
        sums = lax.fori_loop(0, members, body, sums)
        packed = jnp.zeros((height, LANES), F32)
        for comp in range(3):
            total = jnp.sum(sums[comp].reshape(height, LANES), axis=1, keepdims=True)
            packed = jnp.where(lane == comp, total, packed)
        weighted_ref[strip_rows, :] = packed
        return carry

    lax.fori_loop(0, width // height, strip_body, 0)
    frame_total = rows_ref.shape[1]
    rows = rows_ref[...].reshape(3 * frame_total, width)
    high, mid, low = (jnp.dot(rows, piece, preferred_element_type=F32) for piece in three_pieces(weighted_ref[...]))
    fits = ((low + mid) + high).T
    entries = [
        fits[comp : comp + 1, part * frame_total : (part + 1) * frame_total] for part in range(3) for comp in range(3)
    ]
    first = jnp.concatenate(entries[:8], axis=0)
    last = jnp.concatenate([entries[8], jnp.zeros((7, frame_total), F32)], axis=0)
    message = jnp.concatenate([first, last], axis=1)
    out_ref[...] = jnp.broadcast_to(message[None], out_ref.shape)


def orthogonalized(message, frame_total):
    fitted = [message[entry : entry + 1, :frame_total] for entry in range(8)]
    fitted.append(message[0:1, frame_total:])
    norm = functools.reduce(lambda a, b: a + b, [value * value for value in fitted])
    scaling = jnp.sqrt(1.0 + norm)
    current = [[fitted[3 * col + row] / scaling for col in range(3)] for row in range(3)]
    for _ in range(POLAR):
        square = [[None] * 3 for _ in range(3)]
        for a in range(3):
            for b in range(a, 3):
                x, y = current[a], current[b]
                square[a][b] = square[b][a] = x[0] * y[0] + x[1] * y[1] + x[2] * y[2]
        cubed = [
            [square[a][0] * current[0][b] + square[a][1] * current[1][b] + square[a][2] * current[2][b] for b in range(3)]
            for a in range(3)
        ]
        current = [[1.5 * current[a][b] - 0.5 * cubed[a][b] for b in range(3)] for a in range(3)]
    return current


def put_deviations(wide_ref, coords_ref, centre_ref, dev_ref):
    frame_total, width = coords_ref.shape[1:]
    for start in range(0, width, LANES):
        span = slice(start, start + LANES)
        coords = [coords_ref[part, :, span].astype(F32) for part in range(3)]
        for comp in range(3):
            moved = wide_ref[3 * comp] * coords[0]
            moved = moved + wide_ref[3 * comp + 1] * coords[1]
            moved = moved + wide_ref[3 * comp + 2] * coords[2]
            value = moved - centre_ref[comp : comp + 1, span]
            dev_ref[comp * frame_total : (comp + 1) * frame_total, span] = value.astype(BF16)


def clear_spare(dev_ref, frame_total):
    depth, width = dev_ref.shape[1:]
    if depth > 3 * frame_total:
        dev_ref[:, 3 * frame_total :, :] = jnp.zeros((2, depth - 3 * frame_total, width), BF16)


def put_tiles(wide_ref, centre_ref, panel_refs, rows_dev_ref, dev_ref, out_ref):
    scale = 1.0 / (3 * wide_ref.shape[1])
    for step in range(len(panel_refs)):

        @pl.when(pl.program_id(0) == step)
        def _(step=step):
            product = jnp.dot(rows_dev_ref[...], dev_ref[step % 2], preferred_element_type=F32)
            if step + 1 < len(panel_refs):
                later = dev_ref.at[(step + 1) % 2]
                put_deviations(wide_ref, panel_refs[step + 1], centre_ref.at[step + 1], later)
            out_ref[...] = product * scale


def first_tiles_kernel(half, row, col, fits_ref, rows_ref, rows_centre_ref, centre_ref, *refs):
    panel_refs = refs[:half]
    out_ref, rot_out_ref, wide_ref, rows_dev_ref, dev_ref = refs[half:]
    frame_total = rows_ref.shape[1]
    local = rot_out_ref.shape[2]

    @pl.when(pl.program_id(0) == 0)
    def _():
        current = orthogonalized(jnp.sum(fits_ref[...], axis=0), frame_total)
        for a in range(3):
            flat = jnp.concatenate(current[a], axis=0)
            kept = flat[:, :local]
            for block in range(1, frame_total // local):
                kept = jnp.where(col[0] == block, flat[:, block * local : (block + 1) * local], kept)
            rot_out_ref[a] = kept
        entries = [current[a][b] for a in range(3) for b in range(3)]
        columns = jnp.concatenate(entries + [jnp.zeros((7, frame_total), F32)], axis=0).T
        for entry in range(9):
            wide_ref[entry] = jnp.broadcast_to(columns[:, entry : entry + 1], (frame_total, LANES))
        clear_spare(dev_ref, frame_total)
        put_deviations(wide_ref, rows_ref, rows_centre_ref, dev_ref.at[1])
        rows_dev_ref[...] = dev_ref[1].T
        put_deviations(wide_ref, panel_refs[0], centre_ref.at[0], dev_ref.at[0])

    put_tiles(wide_ref, centre_ref, panel_refs, rows_dev_ref, dev_ref, out_ref)


def more_tiles_kernel(half, row, before_ref, wide_ref, rows_dev_ref, centre_ref, *refs):
    panel_refs, (out_ref, dev_ref) = refs[:half], refs[half:]

    @pl.when(pl.program_id(0) == 0)
    def _():
        clear_spare(dev_ref, wide_ref.shape[1])
        put_deviations(wide_ref, panel_refs[0], centre_ref.at[0], dev_ref.at[0])

    put_tiles(wide_ref, centre_ref, panel_refs, rows_dev_ref, dev_ref, out_ref)


def per_device(frames, rotations, inverse_cov):
    row_count, col_count = lax.axis_size("row"), lax.axis_size("col")
    members = row_count // col_count
    row = lax.axis_index("row").astype(jnp.int32).reshape(1)
    col = lax.axis_index("col").astype(jnp.int32).reshape(1)
    local, _, width = frames.shape
    frame_total = local * col_count
    device_total = row_count * col_count
    col_width = inverse_cov.shape[1]
    half = members // 2
    coords = jnp.transpose(frames, (1, 0, 2))

    def limit(mib):
        return pltpu.CompilerParams(vmem_limit_bytes=mib * MIB)

    def move(value, source_of, receives=lambda group, col: True):
        pairs = []
        for group in range(col_count):
            for member in range(members):
                for place in range(col_count):
                    if receives(group, place):
                        from_group, from_member, from_col = source_of(group, member, place)
                        source = (from_group * members + from_member) * col_count + from_col
                        pairs.append((source, (group * members + member) * col_count + place))
        return lax.ppermute(value, ("row", "col"), pairs)

    def from_panel_row(value, step):
        return move(value, lambda g, m, c: (c, m, (g + step) % col_count))

    def from_member(value, mask):
        return move(value, lambda g, m, c: (g, m ^ mask, c))

    def limit(mib):
        return pltpu.CompilerParams(vmem_limit_bytes=mib * MIB)

    def after(first, value):
        return lax.optimization_barrier((first, value))[1]

    def small_kernel(kernel, shape, name, *values):
        return pl.pallas_call(
            kernel,
            out_shape=jax.ShapeDtypeStruct(shape, F32),
            in_specs=[vmem()] * len(values),
            out_specs=vmem(),
            compiler_params=limit(4),
            name=name,
        )(*values)

    def in_hbm(value):
        return pltpu.with_memory_space_constraint(value, pltpu.HBM)

    far = [move(coords, lambda g, m, c, s=step: ((g + s) % col_count, m, c)) for step in range(1, col_count)]
    others = [move(coords, lambda g, m, c, s=step: (g, m, (c + s) % col_count)) for step in range(1, col_count)]
    inverse_here, token = pl.pallas_call(
        fetch_kernel,
        out_shape=(jax.ShapeDtypeStruct(inverse_cov.shape, F32), jax.ShapeDtypeStruct((8, LANES), F32)),
        in_specs=[hbm()],
        out_specs=(vmem(), vmem()),
        scratch_shapes=[pltpu.SemaphoreType.DMA((12,))],
        compiler_params=limit(4),
        cost_estimate=pl.CostEstimate(flops=0, bytes_accessed=4 * width * col_width, transcendentals=0),
        name="fetch_inverse",
    )(in_hbm(inverse_cov))
    rows_all, rows_centre, rot = pl.pallas_call(
        rows_kernel,
        out_shape=(
            jax.ShapeDtypeStruct((3, frame_total, width), BF16),
            jax.ShapeDtypeStruct((3, width), F32),
            jax.ShapeDtypeStruct(rotations.shape, F32),
        ),
        in_specs=[smem(), vmem(), hbm(), hbm()] + [vmem()] * (col_count - 1),
        out_specs=(vmem(), vmem(), vmem()),
        scratch_shapes=[pltpu.SemaphoreType.DMA((2,))],
        compiler_params=limit(8),
        name="rows",
    )(col, token, in_hbm(rotations), in_hbm(coords), *others)

    distance = lax.rem(col[0] + col_count - row[0] // members, col_count)
    across = []
    for step in range(1, col_count):
        held = far[0]
        if col_count > 2:
            held = lax.select_n(lax.rem(distance + col_count - step, col_count), coords, *far)
        across.append(move(held, lambda g, m, c, s=step: (g, m, (c + s) % col_count), lambda g, c: g != c))
    own_block, own_centre = pl.pallas_call(
        functools.partial(assemble_kernel, members),
        out_shape=(
            jax.ShapeDtypeStruct((3, frame_total, width), BF16),
            jax.ShapeDtypeStruct((3, width), F32),
        ),
        in_specs=[smem(), smem()] + [vmem()] * (2 * col_count),
        out_specs=(vmem(), vmem()),
        compiler_params=limit(8),
        name="assemble",
    )(row, col, rot, rows_all, *far, *across)

    centres = [own_centre] + [from_member(own_centre, 2 * step) for step in range(1, half)]
    even_centres = small_kernel(stack_kernel, (half, 3, width), "stack_centres", *centres)
    odd_centres = from_member(even_centres, 1)
    own_block = after(odd_centres, own_block)
    evens = [own_block] + [from_member(own_block, 2 * step) for step in range(1, half)]

    height = 64 if width % 64 == 0 else 8
    message = pl.pallas_call(
        functools.partial(weighted_fit_kernel, members, height),
        in_specs=[smem()] + [vmem()] * 4,
        out_specs=vmem(),
        scratch_shapes=[pltpu.VMEM((3, 8, col_width), F32), pltpu.VMEM((width, LANES), F32)],
        out_shape=jax.ShapeDtypeStruct((device_total, 8, 2 * frame_total), F32),
        compiler_params=limit(8),
        cost_estimate=pl.CostEstimate(
            flops=6 * width * col_width, bytes_accessed=4 * width * col_width, transcendentals=0
        ),
        name="weighted_fit",
    )(row, inverse_here, even_centres, odd_centres, rows_all)
    fits = lax.all_to_all(message, ("row", "col"), split_axis=0, concat_axis=0, tiled=True)
    evens = after(fits, evens)
    odds = [from_member(block, 1) for block in evens]

    depth = -(-3 * frame_total // 256) * 256

    def tile_spec(odd):
        def index(i, row, *_):
            return (0, lax.rem(row[0], members) ^ (2 * i + odd))

        return pl.BlockSpec((width, width), index)

    tiles_cost = pl.CostEstimate(
        flops=3 * frame_total * width * col_width, bytes_accessed=2 * width * col_width, transcendentals=0
    )
    dev_scratch = pltpu.VMEM((2, depth, width), BF16)
    covariance, transforms, wide, rows_dev = pl.pallas_call(
        functools.partial(first_tiles_kernel, half),
        grid_spec=pltpu.PrefetchScalarGridSpec(
            num_scalar_prefetch=2,
            grid=(half,),
            in_specs=[vmem()] * (4 + half),
            out_specs=(tile_spec(0), vmem(), vmem(), vmem()),
            scratch_shapes=[dev_scratch],
        ),
        out_shape=(
            jax.ShapeDtypeStruct((width, col_width), F32),
            jax.ShapeDtypeStruct((3, 3, local), F32),
            jax.ShapeDtypeStruct((9, frame_total, LANES), F32),
            jax.ShapeDtypeStruct((width, depth), BF16),
        ),
        compiler_params=limit(16),
        cost_estimate=tiles_cost,
        name="steps_and_even_tiles",
    )(row, col, fits, rows_all, rows_centre, even_centres, *evens)
    covariance = pl.pallas_call(
        functools.partial(more_tiles_kernel, half),
        grid_spec=pltpu.PrefetchScalarGridSpec(
            num_scalar_prefetch=1,
            grid=(half,),
            in_specs=[hbm()] + [vmem()] * (3 + half),
            out_specs=tile_spec(1),
            scratch_shapes=[dev_scratch],
        ),
        out_shape=jax.ShapeDtypeStruct((width, col_width), F32),
        input_output_aliases={1: 0},
        compiler_params=limit(16),
        cost_estimate=tiles_cost,
        name="odd_tiles",
    )(row, covariance, wide, rows_dev, odd_centres, *odds)
    return (covariance, transforms)


def solution(mesh):
    placed = (P("col", None, "row"), P(), P("row", "col"))
    return jax.shard_map(
        per_device,
        mesh=mesh,
        in_specs=placed,
        out_specs=(P("row", "col"), P(None, None, "col")),
        check_vma=False,
    )
```

```python
import functools

import jax
import jax.numpy as jnp
from jax import lax
from jax.experimental import pallas as pl
from jax.experimental.pallas import tpu as pltpu
from jax.sharding import PartitionSpec as P

POLAR = 12
LANES = 128
F32 = jnp.float32
BF16 = jnp.bfloat16
MIB = 1 << 20


def vmem():
    return pl.BlockSpec(memory_space=pltpu.VMEM)


def hbm():
    return pl.BlockSpec(memory_space=pl.ANY)


def smem():
    return pl.BlockSpec(memory_space=pltpu.SMEM)


def three_pieces(value):
    high = value.astype(BF16)
    rest = value - high.astype(F32)
    mid = rest.astype(BF16)
    low = (rest - mid.astype(F32)).astype(BF16)
    return high, mid, low


def rotated_sum(rot, coords):
    depth = coords.shape[0] * coords.shape[1]
    flat = jnp.concatenate([rot[:, part, :] for part in range(3)], axis=1)
    padded = jnp.concatenate([flat, jnp.zeros((5, depth), F32)], axis=0)
    stacked = jnp.concatenate(three_pieces(padded), axis=0)
    product = jnp.dot(stacked, coords.reshape(depth, coords.shape[2]), preferred_element_type=F32)
    return (product[16:19] + product[8:11]) + product[0:3]


def partial_centre_kernel(frame_total, col, rot_hbm, coords_hbm, out_ref, coords_ref, rot_ref, sems):
    copies = [
        pltpu.make_async_copy(rot_hbm, rot_ref, sems.at[0]),
        pltpu.make_async_copy(coords_hbm, coords_ref, sems.at[1]),
    ]
    for copy in copies:
        copy.start()
    for copy in copies:
        copy.wait()
    local = coords_ref.shape[1]
    block = lax.broadcasted_iota(jnp.int32, rot_ref.shape, 2) // local
    rot = jnp.where(block == col[0], rot_ref[...], 0.0)
    coords = jnp.concatenate([coords_ref[...]] * (frame_total // local), axis=1)
    centre = rotated_sum(rot, coords) * (1.0 / frame_total)
    flat = jnp.concatenate([centre[comp : comp + 1, :] for comp in range(3)], axis=1)
    out_ref[...] = jnp.broadcast_to(flat[None], out_ref.shape)


def put_centre(parts_ref, row, col_count, centre_ref):
    total = parts_ref[row * col_count]
    for place in range(1, col_count):
        total = total + parts_ref[row * col_count + place]
    width = centre_ref.shape[1]
    for comp in range(3):
        centre_ref[comp : comp + 1, :] = total[:, comp * width : (comp + 1) * width]


def put_block(out_ref, block, value):
    local = value.shape[1]
    out_ref[:, pl.ds(pl.multiple_of(block * local, local), local), :] = value


def assemble_kernel(members, row, col, rows_ref, *refs):
    sources, out_ref = refs[:-1], refs[-1]
    far_refs, across_refs = sources[: len(sources) // 2], sources[len(sources) // 2 :]
    col_count = len(far_refs) + 1
    distance = lax.rem(col[0] + col_count - row[0] // members, col_count)

    @pl.when(distance == 0)
    def _():
        out_ref[...] = rows_ref[...]

    for step, ref in enumerate(far_refs):

        @pl.when(distance == step + 1)
        def _(ref=ref):
            put_block(out_ref, col[0], ref[...])
            for shift, across_ref in enumerate(across_refs):
                put_block(out_ref, lax.rem(col[0] + 1 + shift, col_count), across_ref[...])


def fetch_kernel(source_ref, target_ref, sems):
    height = source_ref.shape[0] // sems.shape[0]
    copies = []
    for strip in range(sems.shape[0]):
        span = pl.ds(strip * height, height)
        copies.append(pltpu.make_async_copy(source_ref.at[span, :], target_ref.at[span, :], sems.at[strip]))
        copies[-1].start()
    for copy in copies:
        copy.wait()


def weighted_kernel(members, col_count, height, row, col, inv_ref, parts_ref, out_ref, even_ref, odd_ref, rows_centre_ref, wide_ref):
    width = even_ref.shape[2]
    member = lax.rem(row[0], members)
    for mask in range(members):
        centre_ref = (odd_ref if mask % 2 else even_ref).at[mask // 2]
        put_centre(parts_ref, col[0] * members + (member ^ mask), col_count, centre_ref)
        for comp in range(3):
            factor = jnp.broadcast_to(centre_ref[comp : comp + 1, :], (8, width))
            wide_ref[comp, :, mask * width : (mask + 1) * width] = factor
    put_centre(parts_ref, row[0], col_count, rows_centre_ref)
    lane = lax.broadcasted_iota(jnp.int32, (height, LANES), 1)

    def strip_body(strip, carry):
        strip_rows = pl.ds(pl.multiple_of(strip * height, height), height)
        sums = [jnp.zeros((height // 8, 8, LANES), F32)] * 3
        for mask in range(members):
            block = member ^ mask
            for start in range(0, width, LANES):
                span = pl.ds(pl.multiple_of(block * width + start, LANES), LANES)
                value = inv_ref[strip_rows, span].reshape(height // 8, 8, LANES)
                place = mask * width + start
                for comp in range(3):
                    sums[comp] = sums[comp] + value * wide_ref[comp, :, place : place + LANES][None]
        packed = jnp.zeros((height, LANES), F32)
        for comp in range(3):
            total = jnp.sum(sums[comp].reshape(height, LANES), axis=1, keepdims=True)
            packed = jnp.where(lane == comp, total, packed)
        out_ref[strip_rows, :] = packed
        return carry

    lax.fori_loop(0, inv_ref.shape[0] // height, strip_body, 0)


def fit_kernel(col, weighted_ref, own_ref, *refs):
    others, (out_ref, rows_ref) = refs[:-2], refs[-2:]
    for shift, ref in enumerate((own_ref, *others)):
        put_block(rows_ref, lax.rem(col[0] + shift, len(others) + 1), ref[...])
    frame_total, width = rows_ref.shape[1:]
    rows = rows_ref[...].reshape(3 * frame_total, width)
    high, mid, low = (jnp.dot(rows, piece, preferred_element_type=F32) for piece in three_pieces(weighted_ref[...]))
    fits = ((low + mid) + high).T
    entries = [
        fits[comp : comp + 1, part * frame_total : (part + 1) * frame_total] for part in range(3) for comp in range(3)
    ]
    first = jnp.concatenate(entries[:8], axis=0)
    last = jnp.concatenate([entries[8], jnp.zeros((7, frame_total), F32)], axis=0)
    message = jnp.concatenate([first, last], axis=1)
    out_ref[...] = jnp.broadcast_to(message[None], out_ref.shape)


def orthogonalized(message, frame_total):
    fitted = [message[entry : entry + 1, :frame_total] for entry in range(8)]
    fitted.append(message[0:1, frame_total:])
    norm = functools.reduce(lambda a, b: a + b, [value * value for value in fitted])
    scaling = jnp.sqrt(1.0 + norm)
    current = [[fitted[3 * col + row] / scaling for col in range(3)] for row in range(3)]
    for _ in range(POLAR):
        square = [[None] * 3 for _ in range(3)]
        for a in range(3):
            for b in range(a, 3):
                x, y = current[a], current[b]
                square[a][b] = square[b][a] = x[0] * y[0] + x[1] * y[1] + x[2] * y[2]
        cubed = [
            [square[a][0] * current[0][b] + square[a][1] * current[1][b] + square[a][2] * current[2][b] for b in range(3)]
            for a in range(3)
        ]
        current = [[1.5 * current[a][b] - 0.5 * cubed[a][b] for b in range(3)] for a in range(3)]
    return current


def put_deviations(wide_ref, coords_ref, centre_ref, first, dev_ref):
    frame_total = coords_ref.shape[1]
    for start in range(0, dev_ref.shape[1], LANES):
        span = slice(first + start, first + start + LANES)
        coords = [coords_ref[part, :, span].astype(F32) for part in range(3)]
        for comp in range(3):
            moved = wide_ref[3 * comp] * coords[0]
            moved = moved + wide_ref[3 * comp + 1] * coords[1]
            moved = moved + wide_ref[3 * comp + 2] * coords[2]
            value = moved - centre_ref[comp : comp + 1, span]
            dev_ref[comp * frame_total : (comp + 1) * frame_total, start : start + LANES] = value.astype(BF16)


def put_tiles(masks, row, wide_ref, centre_ref, panel_refs, rows_dev_ref, dev_ref, tile_ref, sems, out_ref):
    slots, _, tile = tile_ref.shape
    width = centre_ref.shape[2]
    members = out_ref.shape[1] // width
    scale = 1.0 / (3 * wide_ref.shape[1])
    writes = []
    for step, mask in enumerate(masks):
        block = lax.rem(row[0], members) ^ mask
        for first in range(0, width, tile):
            count = len(writes)
            dev = dev_ref.at[count % 2]
            put_deviations(wide_ref, panel_refs[step], centre_ref.at[step], first, dev)
            product = jnp.dot(rows_dev_ref[...], dev[...], preferred_element_type=F32)
            if count >= slots:
                writes[count - slots].wait()
            tile_ref[count % slots] = product * scale
            target = out_ref.at[:, pl.ds(pl.multiple_of(block * width + first, LANES), tile)]
            writes.append(pltpu.make_async_copy(tile_ref.at[count % slots], target, sems.at[count % slots]))
            writes[-1].start()
    for write in writes[-slots:]:
        write.wait()


def first_tiles_kernel(masks, row, col, fits_ref, rows_ref, rows_centre_ref, centre_ref, *refs):
    panel_refs = refs[: len(masks)]
    out_ref, rot_out_ref, wide_ref, rows_dev_ref, rows_ref_t, dev_ref, tile_ref, sems = refs[len(masks) :]
    frame_total = rows_ref.shape[1]
    local = rot_out_ref.shape[2]
    current = orthogonalized(jnp.sum(fits_ref[...], axis=0), frame_total)
    for a in range(3):
        flat = jnp.concatenate(current[a], axis=0)
        kept = flat[:, :local]
        for block in range(1, frame_total // local):
            kept = jnp.where(col[0] == block, flat[:, block * local : (block + 1) * local], kept)
        rot_out_ref[a] = kept
    entries = [current[a][b] for a in range(3) for b in range(3)]
    columns = jnp.concatenate(entries + [jnp.zeros((7, frame_total), F32)], axis=0).T
    for entry in range(9):
        wide_ref[entry] = jnp.broadcast_to(columns[:, entry : entry + 1], (frame_total, LANES))
    put_deviations(wide_ref, rows_ref, rows_centre_ref, 0, rows_ref_t)
    rows_dev_ref[...] = rows_ref_t[...].T
    put_tiles(masks, row, wide_ref, centre_ref, panel_refs, rows_dev_ref, dev_ref, tile_ref, sems, out_ref)


def more_tiles_kernel(masks, row, before_ref, wide_ref, rows_dev_ref, centre_ref, *refs):
    panel_refs, (out_ref, dev_ref, tile_ref, sems) = refs[: len(masks)], refs[len(masks) :]
    put_tiles(masks, row, wide_ref, centre_ref, panel_refs, rows_dev_ref, dev_ref, tile_ref, sems, out_ref)


def per_device(frames, rotations, inverse_cov):
    row_count, col_count = lax.axis_size("row"), lax.axis_size("col")
    members = row_count // col_count
    row = lax.axis_index("row").astype(jnp.int32).reshape(1)
    col = lax.axis_index("col").astype(jnp.int32).reshape(1)
    local, _, width = frames.shape
    frame_total = local * col_count
    device_total = row_count * col_count
    col_width = inverse_cov.shape[1]
    half = members // 2
    coords = jnp.transpose(frames, (1, 0, 2))

    def limit(mib):
        return pltpu.CompilerParams(vmem_limit_bytes=mib * MIB)

    def move(value, source_of, receives=lambda group, col: True):
        pairs = []
        for group in range(col_count):
            for member in range(members):
                for place in range(col_count):
                    if receives(group, place):
                        from_group, from_member, from_col = source_of(group, member, place)
                        source = (from_group * members + from_member) * col_count + from_col
                        pairs.append((source, (group * members + member) * col_count + place))
        return lax.ppermute(value, ("row", "col"), pairs)

    def from_panel_row(value, step):
        return move(value, lambda g, m, c: (c, m, (g + step) % col_count))

    def from_member(value, mask):
        return move(value, lambda g, m, c: (g, m ^ mask, c))

    def limit(mib):
        return pltpu.CompilerParams(vmem_limit_bytes=mib * MIB)

    def in_hbm(value):
        return pltpu.with_memory_space_constraint(value, pltpu.HBM)

    repeated, coords_here = pl.pallas_call(
        functools.partial(partial_centre_kernel, frame_total),
        out_shape=(
            jax.ShapeDtypeStruct((device_total, 1, 3 * width), F32),
            jax.ShapeDtypeStruct(coords.shape, BF16),
        ),
        in_specs=[smem(), hbm(), hbm()],
        out_specs=(vmem(), vmem()),
        scratch_shapes=[pltpu.VMEM(rotations.shape, F32), pltpu.SemaphoreType.DMA((2,))],
        compiler_params=limit(8),
        name="partial_centre",
    )(col, in_hbm(rotations), in_hbm(coords))
    parts = lax.all_to_all(repeated, ("row", "col"), split_axis=0, concat_axis=0, tiled=True)

    far = [move(coords_here, lambda g, m, c, s=step: ((g + s) % col_count, m, c)) for step in range(1, col_count)]
    others = [
        move(coords_here, lambda g, m, c, s=step: (g, m, (c + s) % col_count)) for step in range(1, col_count)
    ]
    inverse_here = pl.pallas_call(
        fetch_kernel,
        out_shape=jax.ShapeDtypeStruct(inverse_cov.shape, F32),
        in_specs=[hbm()],
        out_specs=vmem(),
        scratch_shapes=[pltpu.SemaphoreType.DMA((12,))],
        compiler_params=limit(4),
        cost_estimate=pl.CostEstimate(flops=0, bytes_accessed=4 * width * col_width, transcendentals=0),
        name="fetch_inverse",
    )(in_hbm(inverse_cov))

    height = 64 if width % 64 == 0 else 8
    weighted, even_centres, odd_centres, rows_centre = pl.pallas_call(
        functools.partial(weighted_kernel, members, col_count, height),
        out_shape=(
            jax.ShapeDtypeStruct((width, LANES), F32),
            jax.ShapeDtypeStruct((half, 3, width), F32),
            jax.ShapeDtypeStruct((half, 3, width), F32),
            jax.ShapeDtypeStruct((3, width), F32),
        ),
        in_specs=[smem(), smem(), vmem(), vmem()],
        out_specs=(vmem(),) * 4,
        scratch_shapes=[pltpu.VMEM((3, 8, col_width), F32)],
        compiler_params=limit(8),
        cost_estimate=pl.CostEstimate(
            flops=6 * width * col_width, bytes_accessed=4 * width * col_width, transcendentals=0
        ),
        name="weighted",
    )(row, col, inverse_here, parts)
    message, rows_all = pl.pallas_call(
        fit_kernel,
        out_shape=(
            jax.ShapeDtypeStruct((device_total, 8, 2 * frame_total), F32),
            jax.ShapeDtypeStruct((3, frame_total, width), BF16),
        ),
        in_specs=[smem()] + [vmem()] * (1 + col_count),
        out_specs=(vmem(), vmem()),
        compiler_params=limit(8),
        name="fit",
    )(col, weighted, coords_here, *others)

    distance = lax.rem(col[0] + col_count - row[0] // members, col_count)
    across = []
    for step in range(1, col_count):
        held = far[0]
        if col_count > 2:
            held = lax.select_n(lax.rem(distance + col_count - step, col_count), coords_here, *far)
        across.append(move(held, lambda g, m, c, s=step: (g, m, (c + s) % col_count), lambda g, c: g != c))
    own_block = pl.pallas_call(
        functools.partial(assemble_kernel, members),
        out_shape=jax.ShapeDtypeStruct((3, frame_total, width), BF16),
        in_specs=[smem(), smem()] + [vmem()] * (2 * col_count - 1),
        out_specs=vmem(),
        compiler_params=limit(8),
        name="assemble",
    )(row, col, rows_all, *far, *across)
    evens = [own_block] + [from_member(own_block, 2 * step) for step in range(1, half)]
    fits = lax.all_to_all(message, ("row", "col"), split_axis=0, concat_axis=0, tiled=True)
    fits, evens = lax.optimization_barrier((fits, evens))
    odds = [from_member(block, 1) for block in evens]

    depth = 3 * frame_total
    tile = 2 * LANES if width % (2 * LANES) == 0 else LANES
    tile_scratch = [
        pltpu.VMEM((2, depth, tile), BF16),
        pltpu.VMEM((4, width, tile), F32),
        pltpu.SemaphoreType.DMA((4,)),
    ]
    tiles_cost = pl.CostEstimate(
        flops=3 * frame_total * width * col_width, bytes_accessed=2 * width * col_width, transcendentals=0
    )
    covariance, transforms, wide, rows_dev = pl.pallas_call(
        functools.partial(first_tiles_kernel, tuple(range(0, members, 2))),
        in_specs=[smem(), smem()] + [vmem()] * (4 + half),
        out_specs=(hbm(), vmem(), vmem(), vmem()),
        scratch_shapes=[pltpu.VMEM((depth, width), BF16)] + tile_scratch,
        out_shape=(
            jax.ShapeDtypeStruct((width, col_width), F32),
            jax.ShapeDtypeStruct((3, 3, local), F32),
            jax.ShapeDtypeStruct((9, frame_total, LANES), F32),
            jax.ShapeDtypeStruct((width, depth), BF16),
        ),
        compiler_params=limit(16),
        cost_estimate=tiles_cost,
        name="steps_and_even_tiles",
    )(row, col, fits, rows_all, rows_centre, even_centres, *evens)
    covariance = pl.pallas_call(
        functools.partial(more_tiles_kernel, tuple(range(1, members, 2))),
        in_specs=[smem(), hbm()] + [vmem()] * (3 + half),
        out_specs=hbm(),
        scratch_shapes=tile_scratch,
        out_shape=jax.ShapeDtypeStruct((width, col_width), F32),
        input_output_aliases={1: 0},
        compiler_params=limit(16),
        cost_estimate=tiles_cost,
        name="odd_tiles",
    )(row, covariance, wide, rows_dev, odd_centres, *odds)
    return (covariance, transforms)


def solution(mesh):
    placed = (P("col", None, "row"), P(), P("row", "col"))
    return jax.shard_map(
        per_device,
        mesh=mesh,
        in_specs=placed,
        out_specs=(P("row", "col"), P(None, None, "col")),
        check_vma=False,
    )
```

```python
import functools

import jax
import jax.numpy as jnp
from jax import lax
from jax.experimental import pallas as pl
from jax.experimental.pallas import tpu as pltpu
from jax.sharding import PartitionSpec as P

POLAR = 12
LANES = 128
F32 = jnp.float32
BF16 = jnp.bfloat16
MIB = 1 << 20


def vmem():
    return pl.BlockSpec(memory_space=pltpu.VMEM)


def hbm():
    return pl.BlockSpec(memory_space=pl.ANY)


def smem():
    return pl.BlockSpec(memory_space=pltpu.SMEM)


def three_pieces(value):
    high = value.astype(BF16)
    rest = value - high.astype(F32)
    mid = rest.astype(BF16)
    low = (rest - mid.astype(F32)).astype(BF16)
    return high, mid, low


def rotated_sum(rot, coords):
    depth = coords.shape[0] * coords.shape[1]
    flat = jnp.concatenate([rot[:, part, :] for part in range(3)], axis=1)
    padded = jnp.concatenate([flat, jnp.zeros((5, depth), F32)], axis=0)
    stacked = jnp.concatenate(three_pieces(padded), axis=0)
    product = jnp.dot(stacked, coords.reshape(depth, coords.shape[2]), preferred_element_type=F32)
    return (product[16:19] + product[8:11]) + product[0:3]


def put_block(out_ref, block, value):
    local = value.shape[1]
    out_ref[:, pl.ds(pl.multiple_of(block * local, local), local), :] = value


def rows_kernel(col, rot_hbm, coords_hbm, *refs):
    others, (rows_ref, centre_ref, rot_ref, sems) = refs[:-4], refs[-4:]
    local = coords_hbm.shape[1]
    own_rows = rows_ref.at[:, pl.ds(pl.multiple_of(col[0] * local, local), local), :]
    copies = [
        pltpu.make_async_copy(rot_hbm, rot_ref, sems.at[0]),
        pltpu.make_async_copy(coords_hbm, own_rows, sems.at[1]),
    ]
    for copy in copies:
        copy.start()
    for shift, ref in enumerate(others):
        put_block(rows_ref, lax.rem(col[0] + 1 + shift, len(others) + 1), ref[...])
    for copy in copies:
        copy.wait()
    centre = rotated_sum(rot_ref[...], rows_ref[...]) * (1.0 / rows_ref.shape[1])
    flat = jnp.concatenate([centre[comp : comp + 1, :] for comp in range(3)], axis=1)
    centre_ref[...] = jnp.broadcast_to(flat[None], centre_ref.shape)


def pick_kernel(members, step, row, col, rows_ref, *refs):
    far_refs, out_ref = refs[:-1], refs[-1]
    col_count, local = len(far_refs) + 1, out_ref.shape[1]
    index = lax.rem(col[0] + 2 * col_count - row[0] // members - step, col_count)

    @pl.when(index == 0)
    def _():
        out_ref[...] = rows_ref[:, pl.ds(pl.multiple_of(col[0] * local, local), local), :]

    for shift, ref in enumerate(far_refs):

        @pl.when(index == shift + 1)
        def _(ref=ref):
            out_ref[...] = ref[...]


def assemble_kernel(members, row, col, centres_ref, rows_ref, *refs):
    sources, out_ref = refs[:-1], refs[-1]
    far_refs, across_refs = sources[: len(sources) // 2], sources[len(sources) // 2 :]
    col_count = len(far_refs) + 1
    distance = lax.rem(col[0] + col_count - row[0] // members, col_count)

    @pl.when(distance == 0)
    def _():
        out_ref[...] = rows_ref[...]

    for step, ref in enumerate(far_refs):

        @pl.when(distance == step + 1)
        def _(ref=ref):
            put_block(out_ref, col[0], ref[...])
            for shift, across_ref in enumerate(across_refs):
                put_block(out_ref, lax.rem(col[0] + 1 + shift, col_count), across_ref[...])


def weighted_fit_kernel(members, row, col, inv_ref, centres_ref, rows_ref, out_ref, strips_ref, wide_ref, weighted_ref, sems):
    strips, height, col_width = strips_ref.shape
    width = rows_ref.shape[2]

    def fetch(strip):
        rows = pl.ds(pl.multiple_of(strip * height, height), height)
        return pltpu.make_async_copy(inv_ref.at[rows, :], strips_ref.at[strip], sems.at[strip])

    for strip in range(strips):
        fetch(strip).start()
    for block in range(members):
        centre = centres_ref[col[0] * members + block]
        for comp in range(3):
            factor = jnp.broadcast_to(centre[:, comp * width : (comp + 1) * width], (8, width))
            wide_ref[comp, :, block * width : (block + 1) * width] = factor
    lane = lax.broadcasted_iota(jnp.int32, (height, LANES), 1)
    chunks = col_width // LANES

    def strip_body(strip, carry):
        fetch(strip).wait()

        def body(chunk, sums):
            span = pl.ds(pl.multiple_of(chunk * LANES, LANES), LANES)
            value = strips_ref[strip, :, span].reshape(height // 8, 8, LANES)
            return tuple(sums[comp] + value * wide_ref[comp, :, span][None] for comp in range(3))

        sums = (jnp.zeros((height // 8, 8, LANES), F32),) * 3
        sums = lax.fori_loop(0, chunks, body, sums, unroll=12 if chunks % 12 == 0 else 1)
        packed = jnp.zeros((height, LANES), F32)
        for comp in range(3):
            total = jnp.sum(sums[comp].reshape(height, LANES), axis=1, keepdims=True)
            packed = jnp.where(lane == comp, total, packed)
        weighted_ref[pl.ds(pl.multiple_of(strip * height, height), height), :] = packed
        return carry

    lax.fori_loop(0, strips, strip_body, 0)
    frame_total = rows_ref.shape[1]
    rows = rows_ref[...].reshape(3 * frame_total, width)
    high, mid, low = (jnp.dot(rows, piece, preferred_element_type=F32) for piece in three_pieces(weighted_ref[...]))
    fits = ((low + mid) + high).T
    entries = [
        fits[comp : comp + 1, part * frame_total : (part + 1) * frame_total] for part in range(3) for comp in range(3)
    ]
    first = jnp.concatenate(entries[:8], axis=0)
    last = jnp.concatenate([entries[8], jnp.zeros((7, frame_total), F32)], axis=0)
    message = jnp.concatenate([first, last], axis=1)
    out_ref[...] = jnp.broadcast_to(message[None], out_ref.shape)


def orthogonalized(message, frame_total):
    fitted = [message[entry : entry + 1, :frame_total] for entry in range(8)]
    fitted.append(message[0:1, frame_total:])
    norm = functools.reduce(lambda a, b: a + b, [value * value for value in fitted])
    scaling = jnp.sqrt(1.0 + norm)
    current = [[fitted[3 * col + row] / scaling for col in range(3)] for row in range(3)]
    for _ in range(POLAR):
        square = [[None] * 3 for _ in range(3)]
        for a in range(3):
            for b in range(a, 3):
                x, y = current[a], current[b]
                square[a][b] = square[b][a] = x[0] * y[0] + x[1] * y[1] + x[2] * y[2]
        cubed = [
            [square[a][0] * current[0][b] + square[a][1] * current[1][b] + square[a][2] * current[2][b] for b in range(3)]
            for a in range(3)
        ]
        current = [[1.5 * current[a][b] - 0.5 * cubed[a][b] for b in range(3)] for a in range(3)]
    return current


def put_deviations(wide_ref, coords_ref, centres_ref, row, chunk, dev_ref):
    frame_total, width = coords_ref.shape[1:]
    span = slice(chunk * LANES, (chunk + 1) * LANES)
    coords = [coords_ref[part, :, span].astype(F32) for part in range(3)]
    for comp in range(3):
        moved = wide_ref[3 * comp] * coords[0]
        moved = moved + wide_ref[3 * comp + 1] * coords[1]
        moved = moved + wide_ref[3 * comp + 2] * coords[2]
        start = comp * width + chunk * LANES
        value = moved - centres_ref[row, :, start : start + LANES]
        dev_ref[comp * frame_total : (comp + 1) * frame_total, span] = value.astype(BF16)


def put_tile(wide_ref, coords_ref, centres_ref, row, rows_dev_ref, dev_ref, out_ref):
    width = coords_ref.shape[2]
    scale = 1.0 / (3 * coords_ref.shape[1])
    stride = 2 * LANES if width % (2 * LANES) == 0 else LANES
    for start in range(0, width, stride):
        for chunk in range(start // LANES, (start + stride) // LANES):
            put_deviations(wide_ref, coords_ref, centres_ref, row, chunk, dev_ref)
        product = jnp.dot(rows_dev_ref[...], dev_ref[:, start : start + stride], preferred_element_type=F32)
        out_ref[:, start : start + stride] = product * scale


def first_tiles_kernel(count, row, col, fits_ref, rows_ref, centres_ref, *refs):
    panel_refs = refs[:count]
    out_ref, rot_out_ref, wide_ref, rows_dev_ref, dev_ref = refs[count:]
    frame_total = rows_ref.shape[1]
    local = rot_out_ref.shape[2]

    @pl.when(pl.program_id(0) == 0)
    def _():
        current = orthogonalized(jnp.sum(fits_ref[...], axis=0), frame_total)
        for a in range(3):
            flat = jnp.concatenate(current[a], axis=0)
            kept = flat[:, :local]
            for block in range(1, frame_total // local):
                kept = jnp.where(col[0] == block, flat[:, block * local : (block + 1) * local], kept)
            rot_out_ref[a] = kept
        entries = [current[a][b] for a in range(3) for b in range(3)]
        columns = jnp.concatenate(entries + [jnp.zeros((7, frame_total), F32)], axis=0).T
        for entry in range(9):
            wide_ref[entry] = jnp.broadcast_to(columns[:, entry : entry + 1], (frame_total, LANES))
        for chunk in range(rows_ref.shape[2] // LANES):
            put_deviations(wide_ref, rows_ref, centres_ref, row[0], chunk, dev_ref)
        rows_dev_ref[...] = dev_ref[...].T

    for step in range(count):

        @pl.when(pl.program_id(0) == step)
        def _(step=step):
            block = col[0] * 2 * count + (lax.rem(row[0], 2 * count) ^ (2 * step))
            put_tile(wide_ref, panel_refs[step], centres_ref, block, rows_dev_ref, dev_ref, out_ref)


def last_tiles_kernel(count, row, col, before_ref, wide_ref, rows_dev_ref, centres_ref, *refs):
    panel_refs = refs[:count]
    out_ref, dev_ref = refs[count:]
    for step in range(count):

        @pl.when(pl.program_id(0) == step)
        def _(step=step):
            block = col[0] * 2 * count + (lax.rem(row[0], 2 * count) ^ (2 * step + 1))
            put_tile(wide_ref, panel_refs[step], centres_ref, block, rows_dev_ref, dev_ref, out_ref)


def per_device(frames, rotations, inverse_cov):
    row_count, col_count = lax.axis_size("row"), lax.axis_size("col")
    members = row_count // col_count
    row = lax.axis_index("row").astype(jnp.int32).reshape(1)
    col = lax.axis_index("col").astype(jnp.int32).reshape(1)
    local, _, width = frames.shape
    frame_total = local * col_count
    device_total = row_count * col_count
    col_width = inverse_cov.shape[1]
    half = members // 2
    coords = jnp.transpose(frames, (1, 0, 2))

    def limit(mib):
        return pltpu.CompilerParams(vmem_limit_bytes=mib * MIB)

    def move(value, source_of, receives=lambda group, col: True):
        pairs = []
        for group in range(col_count):
            for member in range(members):
                for place in range(col_count):
                    if receives(group, place):
                        from_group, from_member, from_col = source_of(group, member, place)
                        source = (from_group * members + from_member) * col_count + from_col
                        pairs.append((source, (group * members + member) * col_count + place))
        return lax.ppermute(value, ("row", "col"), pairs)

    def from_panel_row(value, step):
        return move(value, lambda g, m, c: (c, m, (g + step) % col_count))

    def from_member(value, mask):
        return move(value, lambda g, m, c: (g, m ^ mask, c))

    def limit(mib):
        return pltpu.CompilerParams(vmem_limit_bytes=mib * MIB)

    def in_hbm(value):
        return pltpu.with_memory_space_constraint(value, pltpu.HBM)

    far = [move(coords, lambda g, m, c, s=step: ((g + s) % col_count, m, c)) for step in range(1, col_count)]
    others = [move(coords, lambda g, m, c, s=step: (g, m, (c + s) % col_count)) for step in range(1, col_count)]
    rows_all, repeated = pl.pallas_call(
        rows_kernel,
        out_shape=(
            jax.ShapeDtypeStruct((3, frame_total, width), BF16),
            jax.ShapeDtypeStruct((row_count, 1, 3 * width), F32),
        ),
        in_specs=[smem(), hbm(), hbm()] + [vmem()] * (col_count - 1),
        out_specs=(vmem(), vmem()),
        scratch_shapes=[pltpu.VMEM(rotations.shape, F32), pltpu.SemaphoreType.DMA((2,))],
        compiler_params=limit(8),
        name="rows",
    )(col, in_hbm(rotations), in_hbm(coords), *others)
    centres = lax.all_to_all(repeated, "row", split_axis=0, concat_axis=0, tiled=True)

    across = []
    for step in range(1, col_count):
        held = pl.pallas_call(
            functools.partial(pick_kernel, members, step),
            out_shape=jax.ShapeDtypeStruct((3, local, width), BF16),
            in_specs=[smem(), smem()] + [vmem()] * col_count,
            out_specs=vmem(),
            compiler_params=limit(4),
            name="pick",
        )(row, col, rows_all, *far)
        across.append(move(held, lambda g, m, c, s=step: (g, m, (c + s) % col_count), lambda g, c: g != c))
    own_block = pl.pallas_call(
        functools.partial(assemble_kernel, members),
        out_shape=jax.ShapeDtypeStruct((3, frame_total, width), BF16),
        in_specs=[smem(), smem()] + [vmem()] * (2 * col_count),
        out_specs=vmem(),
        compiler_params=limit(8),
        name="assemble",
    )(row, col, centres, rows_all, *far, *across)
    evens = [own_block] + [from_member(own_block, 2 * step) for step in range(1, half)]

    height = 64 if width % 64 == 0 else 8
    message = pl.pallas_call(
        functools.partial(weighted_fit_kernel, members),
        in_specs=[smem(), smem(), hbm(), vmem(), vmem()],
        out_specs=vmem(),
        scratch_shapes=[
            pltpu.VMEM((width // height, height, col_width), F32),
            pltpu.VMEM((3, 8, col_width), F32),
            pltpu.VMEM((width, LANES), F32),
            pltpu.SemaphoreType.DMA((width // height,)),
        ],
        out_shape=jax.ShapeDtypeStruct((device_total, 8, 2 * frame_total), F32),
        compiler_params=limit(28),
        cost_estimate=pl.CostEstimate(
            flops=6 * width * col_width, bytes_accessed=4 * width * col_width, transcendentals=0
        ),
        name="weighted_fit",
    )(row, col, in_hbm(inverse_cov), centres, rows_all)
    fits = lax.all_to_all(message, ("row", "col"), split_axis=0, concat_axis=0, tiled=True)
    fits, evens = lax.optimization_barrier((fits, evens))
    odds = [from_member(block, 1) for block in evens]

    def tile_spec(odd):
        return pl.BlockSpec((width, width), lambda i, row, *_: (0, lax.rem(row[0], members) ^ (2 * i + odd)))

    tiles_cost = pl.CostEstimate(
        flops=3 * frame_total * width * col_width, bytes_accessed=2 * width * col_width, transcendentals=0
    )
    dev_scratch = pltpu.VMEM((3 * frame_total, width), BF16)
    half_done, transforms, wide, rows_dev = pl.pallas_call(
        functools.partial(first_tiles_kernel, half),
        grid_spec=pltpu.PrefetchScalarGridSpec(
            num_scalar_prefetch=2,
            grid=(half,),
            in_specs=[vmem()] * (3 + half),
            out_specs=(tile_spec(0), vmem(), vmem(), vmem()),
            scratch_shapes=[dev_scratch],
        ),
        out_shape=(
            jax.ShapeDtypeStruct((width, col_width), F32),
            jax.ShapeDtypeStruct((3, 3, local), F32),
            jax.ShapeDtypeStruct((9, frame_total, LANES), F32),
            jax.ShapeDtypeStruct((width, 3 * frame_total), BF16),
        ),
        compiler_params=limit(16),
        cost_estimate=tiles_cost,
        name="steps_and_even_tiles",
    )(row, col, fits, rows_all, centres, *evens)
    covariance = pl.pallas_call(
        functools.partial(last_tiles_kernel, half),
        grid_spec=pltpu.PrefetchScalarGridSpec(
            num_scalar_prefetch=2,
            grid=(half,),
            in_specs=[pl.BlockSpec(memory_space=pl.ANY)] + [vmem()] * (3 + half),
            out_specs=tile_spec(1),
            scratch_shapes=[dev_scratch],
        ),
        out_shape=jax.ShapeDtypeStruct((width, col_width), F32),
        input_output_aliases={2: 0},
        compiler_params=limit(16),
        cost_estimate=tiles_cost,
        name="odd_tiles",
    )(row, col, half_done, wide, rows_dev, centres, *odds)
    return (covariance, transforms)


def solution(mesh):
    placed = (P("col", None, "row"), P(), P("row", "col"))
    return jax.shard_map(
        per_device,
        mesh=mesh,
        in_specs=placed,
        out_specs=(P("row", "col"), P(None, None, "col")),
        check_vma=False,
    )
```

```python
import functools

import jax
import jax.numpy as jnp
from jax import lax
from jax.experimental import pallas as pl
from jax.experimental.pallas import tpu as pltpu
from jax.sharding import PartitionSpec as P

POLAR = 12
LANES = 128
F32 = jnp.float32
BF16 = jnp.bfloat16
MIB = 1 << 20


def vmem():
    return pl.BlockSpec(memory_space=pltpu.VMEM)


def hbm():
    return pl.BlockSpec(memory_space=pl.ANY)


def smem():
    return pl.BlockSpec(memory_space=pltpu.SMEM)


def three_pieces(value):
    high = value.astype(BF16)
    rest = value - high.astype(F32)
    mid = rest.astype(BF16)
    low = (rest - mid.astype(F32)).astype(BF16)
    return high, mid, low


def rotated_sum(rot, coords):
    depth = coords.shape[0] * coords.shape[1]
    flat = jnp.concatenate([rot[:, part, :] for part in range(3)], axis=1)
    padded = jnp.concatenate([flat, jnp.zeros((5, depth), F32)], axis=0)
    stacked = jnp.concatenate(three_pieces(padded), axis=0)
    product = jnp.dot(stacked, coords.reshape(depth, coords.shape[2]), preferred_element_type=F32)
    return (product[16:19] + product[8:11]) + product[0:3]


def put_block(out_ref, block, value):
    local = value.shape[1]
    out_ref[:, pl.ds(pl.multiple_of(block * local, local), local), :] = value


def load_kernel(rot_hbm, coords_hbm, rot_ref, coords_ref, sems):
    copies = [
        pltpu.make_async_copy(rot_hbm, rot_ref, sems.at[0]),
        pltpu.make_async_copy(coords_hbm, coords_ref, sems.at[1]),
    ]
    for copy in copies:
        copy.start()
    for copy in copies:
        copy.wait()


def rows_kernel(col, rot_ref, *refs):
    blocks, (rows_ref, centre_ref) = refs[:-2], refs[-2:]
    for shift, ref in enumerate(blocks):
        put_block(rows_ref, lax.rem(col[0] + shift, len(blocks)), ref[...])
    centre = rotated_sum(rot_ref[...], rows_ref[...]) * (1.0 / rows_ref.shape[1])
    flat = jnp.concatenate([centre[comp : comp + 1, :] for comp in range(3)], axis=1)
    centre_ref[...] = jnp.broadcast_to(flat[None], centre_ref.shape)


def assemble_kernel(members, row, col, centres_ref, rows_ref, *refs):
    far_refs, out_ref = refs[:-1], refs[-1]
    group = row[0] // members

    @pl.when(group == col[0])
    def _():
        out_ref[...] = rows_ref[...]

    @pl.when(group != col[0])
    def _():
        for shift, ref in enumerate(far_refs):
            put_block(out_ref, lax.rem(group + shift, len(far_refs)), ref[...])


def weighted_fit_kernel(members, row, col, inv_ref, centres_ref, rows_ref, out_ref, strips_ref, wide_ref, weighted_ref, sems):
    strips, height, col_width = strips_ref.shape
    width = rows_ref.shape[2]

    def fetch(strip):
        rows = pl.ds(pl.multiple_of(strip * height, height), height)
        return pltpu.make_async_copy(inv_ref.at[rows, :], strips_ref.at[strip], sems.at[strip])

    for strip in range(strips):
        fetch(strip).start()
    for block in range(members):
        centre = centres_ref[col[0] * members + block]
        for comp in range(3):
            factor = jnp.broadcast_to(centre[:, comp * width : (comp + 1) * width], (8, width))
            wide_ref[comp, :, block * width : (block + 1) * width] = factor
    lane = lax.broadcasted_iota(jnp.int32, (height, LANES), 1)
    chunks = col_width // LANES

    def strip_body(strip, carry):
        fetch(strip).wait()

        def body(chunk, sums):
            span = pl.ds(pl.multiple_of(chunk * LANES, LANES), LANES)
            value = strips_ref[strip, :, span].reshape(height // 8, 8, LANES)
            return tuple(sums[comp] + value * wide_ref[comp, :, span][None] for comp in range(3))

        sums = (jnp.zeros((height // 8, 8, LANES), F32),) * 3
        sums = lax.fori_loop(0, chunks, body, sums, unroll=12 if chunks % 12 == 0 else 1)
        packed = jnp.zeros((height, LANES), F32)
        for comp in range(3):
            total = jnp.sum(sums[comp].reshape(height, LANES), axis=1, keepdims=True)
            packed = jnp.where(lane == comp, total, packed)
        weighted_ref[pl.ds(pl.multiple_of(strip * height, height), height), :] = packed
        return carry

    lax.fori_loop(0, strips, strip_body, 0)
    frame_total = rows_ref.shape[1]
    rows = rows_ref[...].reshape(3 * frame_total, width)
    high, mid, low = (jnp.dot(rows, piece, preferred_element_type=F32) for piece in three_pieces(weighted_ref[...]))
    fits = ((low + mid) + high).T
    entries = [
        fits[comp : comp + 1, part * frame_total : (part + 1) * frame_total] for part in range(3) for comp in range(3)
    ]
    first = jnp.concatenate(entries[:8], axis=0)
    last = jnp.concatenate([entries[8], jnp.zeros((7, frame_total), F32)], axis=0)
    message = jnp.concatenate([first, last], axis=1)
    out_ref[...] = jnp.broadcast_to(message[None], out_ref.shape)


def orthogonalized(message, frame_total):
    fitted = [message[entry : entry + 1, :frame_total] for entry in range(8)]
    fitted.append(message[0:1, frame_total:])
    norm = functools.reduce(lambda a, b: a + b, [value * value for value in fitted])
    scaling = jnp.sqrt(1.0 + norm)
    current = [[fitted[3 * col + row] / scaling for col in range(3)] for row in range(3)]
    for _ in range(POLAR):
        square = [[None] * 3 for _ in range(3)]
        for a in range(3):
            for b in range(a, 3):
                x, y = current[a], current[b]
                square[a][b] = square[b][a] = x[0] * y[0] + x[1] * y[1] + x[2] * y[2]
        cubed = [
            [square[a][0] * current[0][b] + square[a][1] * current[1][b] + square[a][2] * current[2][b] for b in range(3)]
            for a in range(3)
        ]
        current = [[1.5 * current[a][b] - 0.5 * cubed[a][b] for b in range(3)] for a in range(3)]
    return current


def put_deviations(wide_ref, coords_ref, centres_ref, row, chunk, dev_ref):
    frame_total, width = coords_ref.shape[1:]
    span = slice(chunk * LANES, (chunk + 1) * LANES)
    coords = [coords_ref[part, :, span].astype(F32) for part in range(3)]
    for comp in range(3):
        moved = wide_ref[3 * comp] * coords[0]
        moved = moved + wide_ref[3 * comp + 1] * coords[1]
        moved = moved + wide_ref[3 * comp + 2] * coords[2]
        start = comp * width + chunk * LANES
        value = moved - centres_ref[row, :, start : start + LANES]
        dev_ref[comp * frame_total : (comp + 1) * frame_total, span] = value.astype(BF16)


def put_tile(wide_ref, coords_ref, centres_ref, row, rows_dev_ref, dev_ref, out_ref):
    width = coords_ref.shape[2]
    scale = 1.0 / (3 * coords_ref.shape[1])
    stride = 2 * LANES if width % (2 * LANES) == 0 else LANES
    for start in range(0, width, stride):
        for chunk in range(start // LANES, (start + stride) // LANES):
            put_deviations(wide_ref, coords_ref, centres_ref, row, chunk, dev_ref)
        span = slice(start, start + stride)
        for first in range(0, rows_dev_ref.shape[0], LANES):
            strip = slice(first, first + LANES)
            product = jnp.dot(rows_dev_ref[strip, :], dev_ref[:, span], preferred_element_type=F32)
            out_ref[strip, span] = product * scale


def first_tiles_kernel(count, row, col, fits_ref, rows_ref, centres_ref, *refs):
    panel_refs = refs[:count]
    out_ref, rot_out_ref, wide_ref, rows_dev_ref, dev_ref = refs[count:]
    frame_total = rows_ref.shape[1]
    local = rot_out_ref.shape[2]

    @pl.when(pl.program_id(0) == 0)
    def _():
        current = orthogonalized(jnp.sum(fits_ref[...], axis=0), frame_total)
        for a in range(3):
            flat = jnp.concatenate(current[a], axis=0)
            kept = flat[:, :local]
            for block in range(1, frame_total // local):
                kept = jnp.where(col[0] == block, flat[:, block * local : (block + 1) * local], kept)
            rot_out_ref[a] = kept
        entries = [current[a][b] for a in range(3) for b in range(3)]
        columns = jnp.concatenate(entries + [jnp.zeros((7, frame_total), F32)], axis=0).T
        for entry in range(9):
            wide_ref[entry] = jnp.broadcast_to(columns[:, entry : entry + 1], (frame_total, LANES))
        for chunk in range(rows_ref.shape[2] // LANES):
            put_deviations(wide_ref, rows_ref, centres_ref, row[0], chunk, dev_ref)
        rows_dev_ref[...] = dev_ref[...].T

    for step in range(count):

        @pl.when(pl.program_id(0) == step)
        def _(step=step):
            block = col[0] * 2 * count + (lax.rem(row[0], 2 * count) ^ (2 * step))
            put_tile(wide_ref, panel_refs[step], centres_ref, block, rows_dev_ref, dev_ref, out_ref)


def last_tiles_kernel(count, row, col, before_ref, wide_ref, rows_dev_ref, centres_ref, *refs):
    panel_refs = refs[:count]
    out_ref, dev_ref = refs[count:]
    for step in range(count):

        @pl.when(pl.program_id(0) == step)
        def _(step=step):
            block = col[0] * 2 * count + (lax.rem(row[0], 2 * count) ^ (2 * step + 1))
            put_tile(wide_ref, panel_refs[step], centres_ref, block, rows_dev_ref, dev_ref, out_ref)


def per_device(frames, rotations, inverse_cov):
    row_count, col_count = lax.axis_size("row"), lax.axis_size("col")
    members = row_count // col_count
    row = lax.axis_index("row").astype(jnp.int32).reshape(1)
    col = lax.axis_index("col").astype(jnp.int32).reshape(1)
    local, _, width = frames.shape
    frame_total = local * col_count
    device_total = row_count * col_count
    col_width = inverse_cov.shape[1]
    half = members // 2
    coords = jnp.transpose(frames, (1, 0, 2))

    def limit(mib):
        return pltpu.CompilerParams(vmem_limit_bytes=mib * MIB)

    def move(value, source_of, receives=lambda group, col: True):
        pairs = []
        for group in range(col_count):
            for member in range(members):
                for place in range(col_count):
                    if receives(group, place):
                        from_group, from_member, from_col = source_of(group, member, place)
                        source = (from_group * members + from_member) * col_count + from_col
                        pairs.append((source, (group * members + member) * col_count + place))
        return lax.ppermute(value, ("row", "col"), pairs)

    def from_panel_row(value, step):
        return move(value, lambda g, m, c: (c, m, (g + step) % col_count))

    def from_member(value, mask):
        return move(value, lambda g, m, c: (g, m ^ mask, c))

    def limit(mib):
        return pltpu.CompilerParams(vmem_limit_bytes=mib * MIB)

    def in_hbm(value):
        return pltpu.with_memory_space_constraint(value, pltpu.HBM)

    others = [move(coords, lambda g, m, c, s=step: (g, m, (c + s) % col_count)) for step in range(1, col_count)]
    far = [
        move(coords, lambda g, m, c, s=step: (c, m, (g + s) % col_count), lambda g, c: g != c)
        for step in range(col_count)
    ]
    rot_here, coords_here = pl.pallas_call(
        load_kernel,
        out_shape=(jax.ShapeDtypeStruct(rotations.shape, F32), jax.ShapeDtypeStruct(coords.shape, BF16)),
        in_specs=[hbm(), hbm()],
        out_specs=(vmem(), vmem()),
        scratch_shapes=[pltpu.SemaphoreType.DMA((2,))],
        compiler_params=limit(4),
        name="load",
    )(in_hbm(rotations), in_hbm(coords))
    rows_all, repeated = pl.pallas_call(
        rows_kernel,
        out_shape=(
            jax.ShapeDtypeStruct((3, frame_total, width), BF16),
            jax.ShapeDtypeStruct((row_count, 1, 3 * width), F32),
        ),
        in_specs=[smem()] + [vmem()] * (1 + col_count),
        out_specs=(vmem(), vmem()),
        compiler_params=limit(8),
        name="rows",
    )(col, rot_here, coords_here, *others)
    centres = lax.all_to_all(repeated, "row", split_axis=0, concat_axis=0, tiled=True)

    own_block = pl.pallas_call(
        functools.partial(assemble_kernel, members),
        out_shape=jax.ShapeDtypeStruct((3, frame_total, width), BF16),
        in_specs=[smem(), smem()] + [vmem()] * (2 + col_count),
        out_specs=vmem(),
        compiler_params=limit(8),
        name="assemble",
    )(row, col, centres, rows_all, *far)
    evens = [own_block] + [from_member(own_block, 2 * step) for step in range(1, half)]

    height = 64 if width % 64 == 0 else 8
    message = pl.pallas_call(
        functools.partial(weighted_fit_kernel, members),
        in_specs=[smem(), smem(), hbm(), vmem(), vmem()],
        out_specs=vmem(),
        scratch_shapes=[
            pltpu.VMEM((width // height, height, col_width), F32),
            pltpu.VMEM((3, 8, col_width), F32),
            pltpu.VMEM((width, LANES), F32),
            pltpu.SemaphoreType.DMA((width // height,)),
        ],
        out_shape=jax.ShapeDtypeStruct((device_total, 8, 2 * frame_total), F32),
        compiler_params=limit(28),
        cost_estimate=pl.CostEstimate(
            flops=6 * width * col_width, bytes_accessed=4 * width * col_width, transcendentals=0
        ),
        name="weighted_fit",
    )(row, col, in_hbm(inverse_cov), centres, rows_all)
    fits = lax.all_to_all(message, ("row", "col"), split_axis=0, concat_axis=0, tiled=True)
    fits, evens = lax.optimization_barrier((fits, evens))
    odds = [from_member(block, 1) for block in evens]

    def tile_spec(odd):
        return pl.BlockSpec((width, width), lambda i, row, *_: (0, lax.rem(row[0], members) ^ (2 * i + odd)))

    tiles_cost = pl.CostEstimate(
        flops=3 * frame_total * width * col_width, bytes_accessed=2 * width * col_width, transcendentals=0
    )
    dev_scratch = pltpu.VMEM((3 * frame_total, width), BF16)
    half_done, transforms, wide, rows_dev = pl.pallas_call(
        functools.partial(first_tiles_kernel, half),
        grid_spec=pltpu.PrefetchScalarGridSpec(
            num_scalar_prefetch=2,
            grid=(half,),
            in_specs=[vmem()] * (3 + half),
            out_specs=(tile_spec(0), vmem(), vmem(), vmem()),
            scratch_shapes=[dev_scratch],
        ),
        out_shape=(
            jax.ShapeDtypeStruct((width, col_width), F32),
            jax.ShapeDtypeStruct((3, 3, local), F32),
            jax.ShapeDtypeStruct((9, frame_total, LANES), F32),
            jax.ShapeDtypeStruct((width, 3 * frame_total), BF16),
        ),
        compiler_params=limit(16),
        cost_estimate=tiles_cost,
        name="steps_and_even_tiles",
    )(row, col, fits, rows_all, centres, *evens)
    covariance = pl.pallas_call(
        functools.partial(last_tiles_kernel, half),
        grid_spec=pltpu.PrefetchScalarGridSpec(
            num_scalar_prefetch=2,
            grid=(half,),
            in_specs=[pl.BlockSpec(memory_space=pl.ANY)] + [vmem()] * (3 + half),
            out_specs=tile_spec(1),
            scratch_shapes=[dev_scratch],
        ),
        out_shape=jax.ShapeDtypeStruct((width, col_width), F32),
        input_output_aliases={2: 0},
        compiler_params=limit(16),
        cost_estimate=tiles_cost,
        name="odd_tiles",
    )(row, col, half_done, wide, rows_dev, centres, *odds)
    return (covariance, transforms)


def solution(mesh):
    placed = (P("col", None, "row"), P(), P("row", "col"))
    return jax.shard_map(
        per_device,
        mesh=mesh,
        in_specs=placed,
        out_specs=(P("row", "col"), P(None, None, "col")),
        check_vma=False,
    )
```

```python
import functools

import jax
import jax.numpy as jnp
from jax import lax
from jax.experimental import pallas as pl
from jax.experimental.pallas import tpu as pltpu
from jax.sharding import PartitionSpec as P

POLAR = 12
LANES = 128
F32 = jnp.float32
BF16 = jnp.bfloat16
MIB = 1 << 20


def vmem():
    return pl.BlockSpec(memory_space=pltpu.VMEM)


def hbm():
    return pl.BlockSpec(memory_space=pl.ANY)


def smem():
    return pl.BlockSpec(memory_space=pltpu.SMEM)


def three_pieces(value):
    high = value.astype(BF16)
    rest = value - high.astype(F32)
    mid = rest.astype(BF16)
    low = (rest - mid.astype(F32)).astype(BF16)
    return high, mid, low


def rotated_sum(rot, coords):
    depth = coords.shape[0] * coords.shape[1]
    flat = jnp.concatenate([rot[:, part, :] for part in range(3)], axis=1)
    padded = jnp.concatenate([flat, jnp.zeros((5, depth), F32)], axis=0)
    stacked = jnp.concatenate(three_pieces(padded), axis=0)
    product = jnp.dot(stacked, coords.reshape(depth, coords.shape[2]), preferred_element_type=F32)
    return (product[16:19] + product[8:11]) + product[0:3]


def put_block(out_ref, block, value):
    local = value.shape[1]
    out_ref[:, pl.ds(pl.multiple_of(block * local, local), local), :] = value


def load_kernel(rot_hbm, coords_hbm, rot_ref, coords_ref, sems):
    copies = [
        pltpu.make_async_copy(rot_hbm, rot_ref, sems.at[0]),
        pltpu.make_async_copy(coords_hbm, coords_ref, sems.at[1]),
    ]
    for copy in copies:
        copy.start()
    for copy in copies:
        copy.wait()


def rows_kernel(col, rot_ref, *refs):
    blocks, (rows_ref, centre_ref) = refs[:-2], refs[-2:]
    for shift, ref in enumerate(blocks):
        put_block(rows_ref, lax.rem(col[0] + shift, len(blocks)), ref[...])
    centre = rotated_sum(rot_ref[...], rows_ref[...]) * (1.0 / rows_ref.shape[1])
    flat = jnp.concatenate([centre[comp : comp + 1, :] for comp in range(3)], axis=1)
    centre_ref[...] = jnp.broadcast_to(flat[None], centre_ref.shape)


def assemble_kernel(members, row, col, rows_ref, *refs):
    sources, out_ref = refs[:-1], refs[-1]
    far_refs, across_refs = sources[: len(sources) // 2], sources[len(sources) // 2 :]
    col_count = len(far_refs) + 1
    distance = lax.rem(col[0] + col_count - row[0] // members, col_count)

    @pl.when(distance == 0)
    def _():
        out_ref[...] = rows_ref[...]

    for step, ref in enumerate(far_refs):

        @pl.when(distance == step + 1)
        def _(ref=ref):
            put_block(out_ref, col[0], ref[...])
            for shift, across_ref in enumerate(across_refs):
                put_block(out_ref, lax.rem(col[0] + 1 + shift, col_count), across_ref[...])


def weighted_fit_kernel(members, row, col, inv_ref, centres_ref, rows_ref, out_ref, strips_ref, wide_ref, weighted_ref, sems):
    strips, height, col_width = strips_ref.shape
    width = rows_ref.shape[2]

    def fetch(strip):
        rows = pl.ds(pl.multiple_of(strip * height, height), height)
        return pltpu.make_async_copy(inv_ref.at[rows, :], strips_ref.at[strip], sems.at[strip])

    for strip in range(strips):
        fetch(strip).start()
    for block in range(members):
        centre = centres_ref[col[0] * members + block]
        for comp in range(3):
            factor = jnp.broadcast_to(centre[:, comp * width : (comp + 1) * width], (8, width))
            wide_ref[comp, :, block * width : (block + 1) * width] = factor
    lane = lax.broadcasted_iota(jnp.int32, (height, LANES), 1)
    chunks = col_width // LANES

    def strip_body(strip, carry):
        fetch(strip).wait()

        def body(chunk, sums):
            span = pl.ds(pl.multiple_of(chunk * LANES, LANES), LANES)
            value = strips_ref[strip, :, span].reshape(height // 8, 8, LANES)
            return tuple(sums[comp] + value * wide_ref[comp, :, span][None] for comp in range(3))

        sums = (jnp.zeros((height // 8, 8, LANES), F32),) * 3
        sums = lax.fori_loop(0, chunks, body, sums, unroll=12 if chunks % 12 == 0 else 1)
        packed = jnp.zeros((height, LANES), F32)
        for comp in range(3):
            total = jnp.sum(sums[comp].reshape(height, LANES), axis=1, keepdims=True)
            packed = jnp.where(lane == comp, total, packed)
        weighted_ref[pl.ds(pl.multiple_of(strip * height, height), height), :] = packed
        return carry

    lax.fori_loop(0, strips, strip_body, 0)
    frame_total = rows_ref.shape[1]
    rows = rows_ref[...].reshape(3 * frame_total, width)
    high, mid, low = (jnp.dot(rows, piece, preferred_element_type=F32) for piece in three_pieces(weighted_ref[...]))
    fits = ((low + mid) + high).T
    entries = [
        fits[comp : comp + 1, part * frame_total : (part + 1) * frame_total] for part in range(3) for comp in range(3)
    ]
    first = jnp.concatenate(entries[:8], axis=0)
    last = jnp.concatenate([entries[8], jnp.zeros((7, frame_total), F32)], axis=0)
    message = jnp.concatenate([first, last], axis=1)
    out_ref[...] = jnp.broadcast_to(message[None], out_ref.shape)


def orthogonalized(message, frame_total):
    fitted = [message[entry : entry + 1, :frame_total] for entry in range(8)]
    fitted.append(message[0:1, frame_total:])
    norm = functools.reduce(lambda a, b: a + b, [value * value for value in fitted])
    scaling = jnp.sqrt(1.0 + norm)
    current = [[fitted[3 * col + row] / scaling for col in range(3)] for row in range(3)]
    for _ in range(POLAR):
        square = [[None] * 3 for _ in range(3)]
        for a in range(3):
            for b in range(a, 3):
                x, y = current[a], current[b]
                square[a][b] = square[b][a] = x[0] * y[0] + x[1] * y[1] + x[2] * y[2]
        cubed = [
            [square[a][0] * current[0][b] + square[a][1] * current[1][b] + square[a][2] * current[2][b] for b in range(3)]
            for a in range(3)
        ]
        current = [[1.5 * current[a][b] - 0.5 * cubed[a][b] for b in range(3)] for a in range(3)]
    return current


def put_deviations(wide_ref, coords_ref, centres_ref, row, chunk, dev_ref):
    frame_total, width = coords_ref.shape[1:]
    span = slice(chunk * LANES, (chunk + 1) * LANES)
    coords = [coords_ref[part, :, span].astype(F32) for part in range(3)]
    for comp in range(3):
        moved = wide_ref[3 * comp] * coords[0]
        moved = moved + wide_ref[3 * comp + 1] * coords[1]
        moved = moved + wide_ref[3 * comp + 2] * coords[2]
        start = comp * width + chunk * LANES
        value = moved - centres_ref[row, :, start : start + LANES]
        dev_ref[comp * frame_total : (comp + 1) * frame_total, span] = value.astype(BF16)


def put_tile(wide_ref, coords_ref, centres_ref, row, rows_dev_ref, dev_ref, out_ref):
    width = coords_ref.shape[2]
    scale = 1.0 / (3 * coords_ref.shape[1])
    stride = 2 * LANES if width % (2 * LANES) == 0 else LANES
    for start in range(0, width, stride):
        for chunk in range(start // LANES, (start + stride) // LANES):
            put_deviations(wide_ref, coords_ref, centres_ref, row, chunk, dev_ref)
        product = jnp.dot(rows_dev_ref[...], dev_ref[:, start : start + stride], preferred_element_type=F32)
        out_ref[:, start : start + stride] = product * scale


def first_tiles_kernel(count, row, col, fits_ref, rows_ref, centres_ref, *refs):
    panel_refs = refs[:count]
    out_ref, rot_out_ref, wide_ref, rows_dev_ref, dev_ref = refs[count:]
    frame_total = rows_ref.shape[1]
    local = rot_out_ref.shape[2]

    @pl.when(pl.program_id(0) == 0)
    def _():
        current = orthogonalized(jnp.sum(fits_ref[...], axis=0), frame_total)
        for a in range(3):
            flat = jnp.concatenate(current[a], axis=0)
            kept = flat[:, :local]
            for block in range(1, frame_total // local):
                kept = jnp.where(col[0] == block, flat[:, block * local : (block + 1) * local], kept)
            rot_out_ref[a] = kept
        entries = [current[a][b] for a in range(3) for b in range(3)]
        columns = jnp.concatenate(entries + [jnp.zeros((7, frame_total), F32)], axis=0).T
        for entry in range(9):
            wide_ref[entry] = jnp.broadcast_to(columns[:, entry : entry + 1], (frame_total, LANES))
        for chunk in range(rows_ref.shape[2] // LANES):
            put_deviations(wide_ref, rows_ref, centres_ref, row[0], chunk, dev_ref)
        rows_dev_ref[...] = dev_ref[...].T

    for step in range(count):

        @pl.when(pl.program_id(0) == step)
        def _(step=step):
            block = col[0] * 2 * count + (lax.rem(row[0], 2 * count) ^ (2 * step))
            put_tile(wide_ref, panel_refs[step], centres_ref, block, rows_dev_ref, dev_ref, out_ref)


def last_tiles_kernel(count, row, col, before_ref, wide_ref, rows_dev_ref, centres_ref, *refs):
    panel_refs = refs[:count]
    out_ref, dev_ref = refs[count:]
    for step in range(count):

        @pl.when(pl.program_id(0) == step)
        def _(step=step):
            block = col[0] * 2 * count + (lax.rem(row[0], 2 * count) ^ (2 * step + 1))
            put_tile(wide_ref, panel_refs[step], centres_ref, block, rows_dev_ref, dev_ref, out_ref)


def per_device(frames, rotations, inverse_cov):
    row_count, col_count = lax.axis_size("row"), lax.axis_size("col")
    members = row_count // col_count
    row = lax.axis_index("row").astype(jnp.int32).reshape(1)
    col = lax.axis_index("col").astype(jnp.int32).reshape(1)
    local, _, width = frames.shape
    frame_total = local * col_count
    device_total = row_count * col_count
    col_width = inverse_cov.shape[1]
    half = members // 2
    coords = jnp.transpose(frames, (1, 0, 2))

    def limit(mib):
        return pltpu.CompilerParams(vmem_limit_bytes=mib * MIB)

    def move(value, source_of, receives=lambda group, col: True):
        pairs = []
        for group in range(col_count):
            for member in range(members):
                for place in range(col_count):
                    if receives(group, place):
                        from_group, from_member, from_col = source_of(group, member, place)
                        source = (from_group * members + from_member) * col_count + from_col
                        pairs.append((source, (group * members + member) * col_count + place))
        return lax.ppermute(value, ("row", "col"), pairs)

    def from_panel_row(value, step):
        return move(value, lambda g, m, c: (c, m, (g + step) % col_count))

    def from_member(value, mask):
        return move(value, lambda g, m, c: (g, m ^ mask, c))

    def limit(mib):
        return pltpu.CompilerParams(vmem_limit_bytes=mib * MIB)

    def in_hbm(value):
        return pltpu.with_memory_space_constraint(value, pltpu.HBM)

    far = [move(coords, lambda g, m, c, s=step: ((g + s) % col_count, m, c)) for step in range(1, col_count)]
    others = [move(coords, lambda g, m, c, s=step: (g, m, (c + s) % col_count)) for step in range(1, col_count)]
    rot_here, coords_here = pl.pallas_call(
        load_kernel,
        out_shape=(jax.ShapeDtypeStruct(rotations.shape, F32), jax.ShapeDtypeStruct(coords.shape, BF16)),
        in_specs=[hbm(), hbm()],
        out_specs=(vmem(), vmem()),
        scratch_shapes=[pltpu.SemaphoreType.DMA((2,))],
        compiler_params=limit(4),
        name="load",
    )(in_hbm(rotations), in_hbm(coords))
    rows_all, repeated = pl.pallas_call(
        rows_kernel,
        out_shape=(
            jax.ShapeDtypeStruct((3, frame_total, width), BF16),
            jax.ShapeDtypeStruct((row_count, 1, 3 * width), F32),
        ),
        in_specs=[smem()] + [vmem()] * (1 + col_count),
        out_specs=(vmem(), vmem()),
        compiler_params=limit(8),
        name="rows",
    )(col, rot_here, coords_here, *others)
    centres = lax.all_to_all(repeated, "row", split_axis=0, concat_axis=0, tiled=True)

    distance = lax.rem(col[0] + col_count - row[0] // members, col_count)
    across = []
    for step in range(1, col_count):
        held = far[0]
        if col_count > 2:
            held = lax.select_n(lax.rem(distance + col_count - step, col_count), coords, *far)
        across.append(move(held, lambda g, m, c, s=step: (g, m, (c + s) % col_count), lambda g, c: g != c))
    own_block = pl.pallas_call(
        functools.partial(assemble_kernel, members),
        out_shape=jax.ShapeDtypeStruct((3, frame_total, width), BF16),
        in_specs=[smem(), smem()] + [vmem()] * (2 * col_count - 1),
        out_specs=vmem(),
        compiler_params=limit(8),
        name="assemble",
    )(row, col, rows_all, *far, *across)
    evens = [own_block] + [from_member(own_block, 2 * step) for step in range(1, half)]

    height = 64 if width % 64 == 0 else 8
    message = pl.pallas_call(
        functools.partial(weighted_fit_kernel, members),
        in_specs=[smem(), smem(), hbm(), vmem(), vmem()],
        out_specs=vmem(),
        scratch_shapes=[
            pltpu.VMEM((width // height, height, col_width), F32),
            pltpu.VMEM((3, 8, col_width), F32),
            pltpu.VMEM((width, LANES), F32),
            pltpu.SemaphoreType.DMA((width // height,)),
        ],
        out_shape=jax.ShapeDtypeStruct((device_total, 8, 2 * frame_total), F32),
        compiler_params=limit(28),
        cost_estimate=pl.CostEstimate(
            flops=6 * width * col_width, bytes_accessed=4 * width * col_width, transcendentals=0
        ),
        name="weighted_fit",
    )(row, col, in_hbm(inverse_cov), centres, rows_all)
    fits = lax.all_to_all(message, ("row", "col"), split_axis=0, concat_axis=0, tiled=True)
    fits, evens = lax.optimization_barrier((fits, evens))
    odds = [from_member(block, 1) for block in evens]

    def tile_spec(odd):
        return pl.BlockSpec((width, width), lambda i, row, *_: (0, lax.rem(row[0], members) ^ (2 * i + odd)))

    tiles_cost = pl.CostEstimate(
        flops=3 * frame_total * width * col_width, bytes_accessed=2 * width * col_width, transcendentals=0
    )
    dev_scratch = pltpu.VMEM((3 * frame_total, width), BF16)
    half_done, transforms, wide, rows_dev = pl.pallas_call(
        functools.partial(first_tiles_kernel, half),
        grid_spec=pltpu.PrefetchScalarGridSpec(
            num_scalar_prefetch=2,
            grid=(half,),
            in_specs=[vmem()] * (3 + half),
            out_specs=(tile_spec(0), vmem(), vmem(), vmem()),
            scratch_shapes=[dev_scratch],
        ),
        out_shape=(
            jax.ShapeDtypeStruct((width, col_width), F32),
            jax.ShapeDtypeStruct((3, 3, local), F32),
            jax.ShapeDtypeStruct((9, frame_total, LANES), F32),
            jax.ShapeDtypeStruct((width, 3 * frame_total), BF16),
        ),
        compiler_params=limit(16),
        cost_estimate=tiles_cost,
        name="steps_and_even_tiles",
    )(row, col, fits, rows_all, centres, *evens)
    covariance = pl.pallas_call(
        functools.partial(last_tiles_kernel, half),
        grid_spec=pltpu.PrefetchScalarGridSpec(
            num_scalar_prefetch=2,
            grid=(half,),
            in_specs=[pl.BlockSpec(memory_space=pl.ANY)] + [vmem()] * (3 + half),
            out_specs=tile_spec(1),
            scratch_shapes=[dev_scratch],
        ),
        out_shape=jax.ShapeDtypeStruct((width, col_width), F32),
        input_output_aliases={2: 0},
        compiler_params=limit(16),
        cost_estimate=tiles_cost,
        name="odd_tiles",
    )(row, col, half_done, wide, rows_dev, centres, *odds)
    return (covariance, transforms)


def solution(mesh):
    placed = (P("col", None, "row"), P(), P("row", "col"))
    return jax.shard_map(
        per_device,
        mesh=mesh,
        in_specs=placed,
        out_specs=(P("row", "col"), P(None, None, "col")),
        check_vma=False,
    )
```

```python
import functools

import jax
import jax.numpy as jnp
from jax import lax
from jax.experimental import pallas as pl
from jax.experimental.pallas import tpu as pltpu
from jax.sharding import PartitionSpec as P

POLAR = 12
LANES = 128
F32 = jnp.float32
BF16 = jnp.bfloat16
MIB = 1 << 20


def vmem():
    return pl.BlockSpec(memory_space=pltpu.VMEM)


def hbm():
    return pl.BlockSpec(memory_space=pl.ANY)


def smem():
    return pl.BlockSpec(memory_space=pltpu.SMEM)


def three_pieces(value):
    high = value.astype(BF16)
    rest = value - high.astype(F32)
    mid = rest.astype(BF16)
    low = (rest - mid.astype(F32)).astype(BF16)
    return high, mid, low


def rotated_sum(rot, coords):
    depth = coords.shape[0] * coords.shape[1]
    flat = jnp.concatenate([rot[:, part, :] for part in range(3)], axis=1)
    padded = jnp.concatenate([flat, jnp.zeros((5, depth), F32)], axis=0)
    stacked = jnp.concatenate(three_pieces(padded), axis=0)
    product = jnp.dot(stacked, coords.reshape(depth, coords.shape[2]), preferred_element_type=F32)
    return (product[16:19] + product[8:11]) + product[0:3]


def put_block(out_ref, block, value):
    local = value.shape[1]
    out_ref[:, pl.ds(pl.multiple_of(block * local, local), local), :] = value


def load_kernel(rot_hbm, coords_hbm, rot_ref, coords_ref, sems):
    copies = [
        pltpu.make_async_copy(rot_hbm, rot_ref, sems.at[0]),
        pltpu.make_async_copy(coords_hbm, coords_ref, sems.at[1]),
    ]
    for copy in copies:
        copy.start()
    for copy in copies:
        copy.wait()


def rows_kernel(col_count, col, rot_ref, *refs):
    blocks, (rows_ref, centre_ref) = refs[:col_count], refs[-2:]
    for shift, ref in enumerate(blocks):
        put_block(rows_ref, lax.rem(col[0] + shift, len(blocks)), ref[...])
    centre = rotated_sum(rot_ref[...], rows_ref[...]) * (1.0 / rows_ref.shape[1])
    flat = jnp.concatenate([centre[comp : comp + 1, :] for comp in range(3)], axis=1)
    centre_ref[...] = jnp.broadcast_to(flat[None], centre_ref.shape)


def assemble_kernel(members, row, col, rows_ref, *refs):
    sources, out_ref = refs[:-1], refs[-1]
    far_refs, across_refs = sources[: len(sources) // 2], sources[len(sources) // 2 :]
    col_count = len(far_refs) + 1
    distance = lax.rem(col[0] + col_count - row[0] // members, col_count)

    @pl.when(distance == 0)
    def _():
        out_ref[...] = rows_ref[...]

    for step, ref in enumerate(far_refs):

        @pl.when(distance == step + 1)
        def _(ref=ref):
            put_block(out_ref, col[0], ref[...])
            for shift, across_ref in enumerate(across_refs):
                put_block(out_ref, lax.rem(col[0] + 1 + shift, col_count), across_ref[...])


def weighted_fit_kernel(members, row, col, inv_ref, centres_ref, rows_ref, out_ref, strips_ref, wide_ref, weighted_ref, sems):
    strips, height, col_width = strips_ref.shape
    width = rows_ref.shape[2]

    def fetch(strip):
        rows = pl.ds(pl.multiple_of(strip * height, height), height)
        return pltpu.make_async_copy(inv_ref.at[rows, :], strips_ref.at[strip], sems.at[strip])

    for strip in range(strips):
        fetch(strip).start()
    for block in range(members):
        centre = centres_ref[col[0] * members + block]
        for comp in range(3):
            factor = jnp.broadcast_to(centre[:, comp * width : (comp + 1) * width], (8, width))
            wide_ref[comp, :, block * width : (block + 1) * width] = factor
    lane = lax.broadcasted_iota(jnp.int32, (height, LANES), 1)
    chunks = col_width // LANES

    def strip_body(strip, carry):
        fetch(strip).wait()

        def body(chunk, sums):
            span = pl.ds(pl.multiple_of(chunk * LANES, LANES), LANES)
            value = strips_ref[strip, :, span].reshape(height // 8, 8, LANES)
            return tuple(sums[comp] + value * wide_ref[comp, :, span][None] for comp in range(3))

        sums = (jnp.zeros((height // 8, 8, LANES), F32),) * 3
        sums = lax.fori_loop(0, chunks, body, sums, unroll=12 if chunks % 12 == 0 else 1)
        packed = jnp.zeros((height, LANES), F32)
        for comp in range(3):
            total = jnp.sum(sums[comp].reshape(height, LANES), axis=1, keepdims=True)
            packed = jnp.where(lane == comp, total, packed)
        weighted_ref[pl.ds(pl.multiple_of(strip * height, height), height), :] = packed
        return carry

    lax.fori_loop(0, strips, strip_body, 0)
    frame_total = rows_ref.shape[1]
    rows = rows_ref[...].reshape(3 * frame_total, width)
    high, mid, low = (jnp.dot(rows, piece, preferred_element_type=F32) for piece in three_pieces(weighted_ref[...]))
    fits = ((low + mid) + high).T
    entries = [
        fits[comp : comp + 1, part * frame_total : (part + 1) * frame_total] for part in range(3) for comp in range(3)
    ]
    first = jnp.concatenate(entries[:8], axis=0)
    last = jnp.concatenate([entries[8], jnp.zeros((7, frame_total), F32)], axis=0)
    message = jnp.concatenate([first, last], axis=1)
    out_ref[...] = jnp.broadcast_to(message[None], out_ref.shape)


def orthogonalized(message, frame_total):
    fitted = [message[entry : entry + 1, :frame_total] for entry in range(8)]
    fitted.append(message[0:1, frame_total:])
    norm = functools.reduce(lambda a, b: a + b, [value * value for value in fitted])
    scaling = jnp.sqrt(1.0 + norm)
    current = [[fitted[3 * col + row] / scaling for col in range(3)] for row in range(3)]
    for _ in range(POLAR):
        square = [[None] * 3 for _ in range(3)]
        for a in range(3):
            for b in range(a, 3):
                x, y = current[a], current[b]
                square[a][b] = square[b][a] = x[0] * y[0] + x[1] * y[1] + x[2] * y[2]
        cubed = [
            [square[a][0] * current[0][b] + square[a][1] * current[1][b] + square[a][2] * current[2][b] for b in range(3)]
            for a in range(3)
        ]
        current = [[1.5 * current[a][b] - 0.5 * cubed[a][b] for b in range(3)] for a in range(3)]
    return current


def put_deviations(wide_ref, coords_ref, centres_ref, row, chunk, dev_ref):
    frame_total, width = coords_ref.shape[1:]
    span = slice(chunk * LANES, (chunk + 1) * LANES)
    coords = [coords_ref[part, :, span].astype(F32) for part in range(3)]
    for comp in range(3):
        moved = wide_ref[3 * comp] * coords[0]
        moved = moved + wide_ref[3 * comp + 1] * coords[1]
        moved = moved + wide_ref[3 * comp + 2] * coords[2]
        start = comp * width + chunk * LANES
        value = moved - centres_ref[row, :, start : start + LANES]
        dev_ref[comp * frame_total : (comp + 1) * frame_total, span] = value.astype(BF16)


def put_tile(wide_ref, coords_ref, centres_ref, row, rows_dev_ref, dev_ref, out_ref):
    width = coords_ref.shape[2]
    scale = 1.0 / (3 * coords_ref.shape[1])
    stride = 2 * LANES if width % (2 * LANES) == 0 else LANES
    for start in range(0, width, stride):
        for chunk in range(start // LANES, (start + stride) // LANES):
            put_deviations(wide_ref, coords_ref, centres_ref, row, chunk, dev_ref)
        product = jnp.dot(rows_dev_ref[...], dev_ref[:, start : start + stride], preferred_element_type=F32)
        out_ref[:, start : start + stride] = product * scale


def first_tiles_kernel(count, row, col, fits_ref, rows_ref, centres_ref, *refs):
    panel_refs = refs[:count]
    out_ref, rot_out_ref, wide_ref, rows_dev_ref, dev_ref = refs[count:]
    frame_total = rows_ref.shape[1]
    local = rot_out_ref.shape[2]

    @pl.when(pl.program_id(0) == 0)
    def _():
        current = orthogonalized(jnp.sum(fits_ref[...], axis=0), frame_total)
        for a in range(3):
            flat = jnp.concatenate(current[a], axis=0)
            kept = flat[:, :local]
            for block in range(1, frame_total // local):
                kept = jnp.where(col[0] == block, flat[:, block * local : (block + 1) * local], kept)
            rot_out_ref[a] = kept
        entries = [current[a][b] for a in range(3) for b in range(3)]
        columns = jnp.concatenate(entries + [jnp.zeros((7, frame_total), F32)], axis=0).T
        for entry in range(9):
            wide_ref[entry] = jnp.broadcast_to(columns[:, entry : entry + 1], (frame_total, LANES))
        for chunk in range(rows_ref.shape[2] // LANES):
            put_deviations(wide_ref, rows_ref, centres_ref, row[0], chunk, dev_ref)
        rows_dev_ref[...] = dev_ref[...].T

    for step in range(count):

        @pl.when(pl.program_id(0) == step)
        def _(step=step):
            block = col[0] * 2 * count + (lax.rem(row[0], 2 * count) ^ (2 * step))
            put_tile(wide_ref, panel_refs[step], centres_ref, block, rows_dev_ref, dev_ref, out_ref)


def last_tiles_kernel(count, row, col, before_ref, wide_ref, rows_dev_ref, centres_ref, *refs):
    panel_refs = refs[:count]
    out_ref, dev_ref = refs[count:]
    for step in range(count):

        @pl.when(pl.program_id(0) == step)
        def _(step=step):
            block = col[0] * 2 * count + (lax.rem(row[0], 2 * count) ^ (2 * step + 1))
            put_tile(wide_ref, panel_refs[step], centres_ref, block, rows_dev_ref, dev_ref, out_ref)


def per_device(frames, rotations, inverse_cov):
    row_count, col_count = lax.axis_size("row"), lax.axis_size("col")
    members = row_count // col_count
    row = lax.axis_index("row").astype(jnp.int32).reshape(1)
    col = lax.axis_index("col").astype(jnp.int32).reshape(1)
    local, _, width = frames.shape
    frame_total = local * col_count
    device_total = row_count * col_count
    col_width = inverse_cov.shape[1]
    half = members // 2
    coords = jnp.transpose(frames, (1, 0, 2))

    def limit(mib):
        return pltpu.CompilerParams(vmem_limit_bytes=mib * MIB)

    def move(value, source_of, receives=lambda group, col: True):
        pairs = []
        for group in range(col_count):
            for member in range(members):
                for place in range(col_count):
                    if receives(group, place):
                        from_group, from_member, from_col = source_of(group, member, place)
                        source = (from_group * members + from_member) * col_count + from_col
                        pairs.append((source, (group * members + member) * col_count + place))
        return lax.ppermute(value, ("row", "col"), pairs)

    def from_panel_row(value, step):
        return move(value, lambda g, m, c: (c, m, (g + step) % col_count))

    def from_member(value, mask):
        return move(value, lambda g, m, c: (g, m ^ mask, c))

    def limit(mib):
        return pltpu.CompilerParams(vmem_limit_bytes=mib * MIB)

    def in_hbm(value):
        return pltpu.with_memory_space_constraint(value, pltpu.HBM)

    far = [move(coords, lambda g, m, c, s=step: ((g + s) % col_count, m, c)) for step in range(1, col_count)]
    others = [move(coords, lambda g, m, c, s=step: (g, m, (c + s) % col_count)) for step in range(1, col_count)]
    rot_here, coords_here = pl.pallas_call(
        load_kernel,
        out_shape=(jax.ShapeDtypeStruct(rotations.shape, F32), jax.ShapeDtypeStruct(coords.shape, BF16)),
        in_specs=[hbm(), hbm()],
        out_specs=(vmem(), vmem()),
        scratch_shapes=[pltpu.SemaphoreType.DMA((2,))],
        compiler_params=limit(4),
        name="load",
    )(in_hbm(rotations), in_hbm(coords))
    rows_all, repeated = pl.pallas_call(
        functools.partial(rows_kernel, col_count),
        out_shape=(
            jax.ShapeDtypeStruct((3, frame_total, width), BF16),
            jax.ShapeDtypeStruct((row_count, 1, 3 * width), F32),
        ),
        in_specs=[smem()] + [vmem()] * (2 * col_count),
        out_specs=(vmem(), vmem()),
        compiler_params=limit(8),
        name="rows",
    )(col, rot_here, coords_here, *others, *far)
    centres = lax.all_to_all(repeated, "row", split_axis=0, concat_axis=0, tiled=True)

    distance = lax.rem(col[0] + col_count - row[0] // members, col_count)
    across = []
    for step in range(1, col_count):
        held = far[0]
        if col_count > 2:
            held = lax.select_n(lax.rem(distance + col_count - step, col_count), coords, *far)
        across.append(move(held, lambda g, m, c, s=step: (g, m, (c + s) % col_count), lambda g, c: g != c))
    own_block = pl.pallas_call(
        functools.partial(assemble_kernel, members),
        out_shape=jax.ShapeDtypeStruct((3, frame_total, width), BF16),
        in_specs=[smem(), smem()] + [vmem()] * (2 * col_count - 1),
        out_specs=vmem(),
        compiler_params=limit(8),
        name="assemble",
    )(row, col, rows_all, *far, *across)
    evens = [own_block] + [from_member(own_block, 2 * step) for step in range(1, half)]

    height = 64 if width % 64 == 0 else 8
    message = pl.pallas_call(
        functools.partial(weighted_fit_kernel, members),
        in_specs=[smem(), smem(), hbm(), vmem(), vmem()],
        out_specs=vmem(),
        scratch_shapes=[
            pltpu.VMEM((width // height, height, col_width), F32),
            pltpu.VMEM((3, 8, col_width), F32),
            pltpu.VMEM((width, LANES), F32),
            pltpu.SemaphoreType.DMA((width // height,)),
        ],
        out_shape=jax.ShapeDtypeStruct((device_total, 8, 2 * frame_total), F32),
        compiler_params=limit(28),
        cost_estimate=pl.CostEstimate(
            flops=6 * width * col_width, bytes_accessed=4 * width * col_width, transcendentals=0
        ),
        name="weighted_fit",
    )(row, col, in_hbm(inverse_cov), centres, rows_all)
    fits = lax.all_to_all(message, ("row", "col"), split_axis=0, concat_axis=0, tiled=True)
    fits, evens = lax.optimization_barrier((fits, evens))
    odds = [from_member(block, 1) for block in evens]

    def tile_spec(odd):
        return pl.BlockSpec((width, width), lambda i, row, *_: (0, lax.rem(row[0], members) ^ (2 * i + odd)))

    tiles_cost = pl.CostEstimate(
        flops=3 * frame_total * width * col_width, bytes_accessed=2 * width * col_width, transcendentals=0
    )
    dev_scratch = pltpu.VMEM((3 * frame_total, width), BF16)
    half_done, transforms, wide, rows_dev = pl.pallas_call(
        functools.partial(first_tiles_kernel, half),
        grid_spec=pltpu.PrefetchScalarGridSpec(
            num_scalar_prefetch=2,
            grid=(half,),
            in_specs=[vmem()] * (3 + half),
            out_specs=(tile_spec(0), vmem(), vmem(), vmem()),
            scratch_shapes=[dev_scratch],
        ),
        out_shape=(
            jax.ShapeDtypeStruct((width, col_width), F32),
            jax.ShapeDtypeStruct((3, 3, local), F32),
            jax.ShapeDtypeStruct((9, frame_total, LANES), F32),
            jax.ShapeDtypeStruct((width, 3 * frame_total), BF16),
        ),
        compiler_params=limit(16),
        cost_estimate=tiles_cost,
        name="steps_and_even_tiles",
    )(row, col, fits, rows_all, centres, *evens)
    covariance = pl.pallas_call(
        functools.partial(last_tiles_kernel, half),
        grid_spec=pltpu.PrefetchScalarGridSpec(
            num_scalar_prefetch=2,
            grid=(half,),
            in_specs=[pl.BlockSpec(memory_space=pl.ANY)] + [vmem()] * (3 + half),
            out_specs=tile_spec(1),
            scratch_shapes=[dev_scratch],
        ),
        out_shape=jax.ShapeDtypeStruct((width, col_width), F32),
        input_output_aliases={2: 0},
        compiler_params=limit(16),
        cost_estimate=tiles_cost,
        name="odd_tiles",
    )(row, col, half_done, wide, rows_dev, centres, *odds)
    return (covariance, transforms)


def solution(mesh):
    placed = (P("col", None, "row"), P(), P("row", "col"))
    return jax.shard_map(
        per_device,
        mesh=mesh,
        in_specs=placed,
        out_specs=(P("row", "col"), P(None, None, "col")),
        check_vma=False,
    )
```

```python
import functools

import jax
import jax.numpy as jnp
from jax import lax
from jax.experimental import pallas as pl
from jax.experimental.pallas import tpu as pltpu
from jax.sharding import PartitionSpec as P

POLAR = 12
LANES = 128
F32 = jnp.float32
BF16 = jnp.bfloat16
MIB = 1 << 20


def vmem():
    return pl.BlockSpec(memory_space=pltpu.VMEM)


def hbm():
    return pl.BlockSpec(memory_space=pl.ANY)


def smem():
    return pl.BlockSpec(memory_space=pltpu.SMEM)


def three_pieces(value):
    high = value.astype(BF16)
    rest = value - high.astype(F32)
    mid = rest.astype(BF16)
    low = (rest - mid.astype(F32)).astype(BF16)
    return high, mid, low


def rotated_sum(rot, coords):
    depth = coords.shape[0] * coords.shape[1]
    flat = jnp.concatenate([rot[:, part, :] for part in range(3)], axis=1)
    padded = jnp.concatenate([flat, jnp.zeros((5, depth), F32)], axis=0)
    stacked = jnp.concatenate(three_pieces(padded), axis=0)
    product = jnp.dot(stacked, coords.reshape(depth, coords.shape[2]), preferred_element_type=F32)
    return (product[16:19] + product[8:11]) + product[0:3]


def put_block(out_ref, block, value):
    local = value.shape[1]
    out_ref[:, pl.ds(pl.multiple_of(block * local, local), local), :] = value


def load_kernel(rot_hbm, coords_hbm, rot_ref, coords_ref, sems):
    copies = [
        pltpu.make_async_copy(rot_hbm, rot_ref, sems.at[0]),
        pltpu.make_async_copy(coords_hbm, coords_ref, sems.at[1]),
    ]
    for copy in copies:
        copy.start()
    for copy in copies:
        copy.wait()


def rows_kernel(col, rot_ref, *refs):
    blocks, (rows_ref, centre_ref) = refs[:-2], refs[-2:]
    for shift, ref in enumerate(blocks):
        put_block(rows_ref, lax.rem(col[0] + shift, len(blocks)), ref[...])
    centre = rotated_sum(rot_ref[...], rows_ref[...]) * (1.0 / rows_ref.shape[1])
    flat = jnp.concatenate([centre[comp : comp + 1, :] for comp in range(3)], axis=1)
    centre_ref[...] = jnp.broadcast_to(flat[None], centre_ref.shape)


def assemble_kernel(members, row, col, rows_ref, *refs):
    far_refs, out_ref = refs[:-1], refs[-1]
    group = row[0] // members

    @pl.when(group == col[0])
    def _():
        out_ref[...] = rows_ref[...]

    @pl.when(group != col[0])
    def _():
        for shift, ref in enumerate(far_refs):
            put_block(out_ref, lax.rem(group + shift, len(far_refs)), ref[...])


def weighted_fit_kernel(members, row, col, inv_ref, centres_ref, rows_ref, out_ref, strips_ref, wide_ref, weighted_ref, sems):
    strips, height, col_width = strips_ref.shape
    width = rows_ref.shape[2]

    def fetch(strip):
        rows = pl.ds(pl.multiple_of(strip * height, height), height)
        return pltpu.make_async_copy(inv_ref.at[rows, :], strips_ref.at[strip], sems.at[strip])

    for strip in range(strips):
        fetch(strip).start()
    for block in range(members):
        centre = centres_ref[col[0] * members + block]
        for comp in range(3):
            factor = jnp.broadcast_to(centre[:, comp * width : (comp + 1) * width], (8, width))
            wide_ref[comp, :, block * width : (block + 1) * width] = factor
    lane = lax.broadcasted_iota(jnp.int32, (height, LANES), 1)
    chunks = col_width // LANES

    def strip_body(strip, carry):
        fetch(strip).wait()

        def body(chunk, sums):
            span = pl.ds(pl.multiple_of(chunk * LANES, LANES), LANES)
            value = strips_ref[strip, :, span].reshape(height // 8, 8, LANES)
            return tuple(sums[comp] + value * wide_ref[comp, :, span][None] for comp in range(3))

        sums = (jnp.zeros((height // 8, 8, LANES), F32),) * 3
        sums = lax.fori_loop(0, chunks, body, sums, unroll=12 if chunks % 12 == 0 else 1)
        packed = jnp.zeros((height, LANES), F32)
        for comp in range(3):
            total = jnp.sum(sums[comp].reshape(height, LANES), axis=1, keepdims=True)
            packed = jnp.where(lane == comp, total, packed)
        weighted_ref[pl.ds(pl.multiple_of(strip * height, height), height), :] = packed
        return carry

    lax.fori_loop(0, strips, strip_body, 0)
    frame_total = rows_ref.shape[1]
    rows = rows_ref[...].reshape(3 * frame_total, width)
    high, mid, low = (jnp.dot(rows, piece, preferred_element_type=F32) for piece in three_pieces(weighted_ref[...]))
    fits = ((low + mid) + high).T
    entries = [
        fits[comp : comp + 1, part * frame_total : (part + 1) * frame_total] for part in range(3) for comp in range(3)
    ]
    first = jnp.concatenate(entries[:8], axis=0)
    last = jnp.concatenate([entries[8], jnp.zeros((7, frame_total), F32)], axis=0)
    message = jnp.concatenate([first, last], axis=1)
    out_ref[...] = jnp.broadcast_to(message[None], out_ref.shape)


def orthogonalized(message, frame_total):
    fitted = [message[entry : entry + 1, :frame_total] for entry in range(8)]
    fitted.append(message[0:1, frame_total:])
    norm = functools.reduce(lambda a, b: a + b, [value * value for value in fitted])
    scaling = jnp.sqrt(1.0 + norm)
    current = [[fitted[3 * col + row] / scaling for col in range(3)] for row in range(3)]
    for _ in range(POLAR):
        square = [[None] * 3 for _ in range(3)]
        for a in range(3):
            for b in range(a, 3):
                x, y = current[a], current[b]
                square[a][b] = square[b][a] = x[0] * y[0] + x[1] * y[1] + x[2] * y[2]
        cubed = [
            [square[a][0] * current[0][b] + square[a][1] * current[1][b] + square[a][2] * current[2][b] for b in range(3)]
            for a in range(3)
        ]
        current = [[1.5 * current[a][b] - 0.5 * cubed[a][b] for b in range(3)] for a in range(3)]
    return current


def put_deviations(wide_ref, coords_ref, centres_ref, row, chunk, dev_ref):
    frame_total, width = coords_ref.shape[1:]
    span = slice(chunk * LANES, (chunk + 1) * LANES)
    coords = [coords_ref[part, :, span].astype(F32) for part in range(3)]
    for comp in range(3):
        moved = wide_ref[3 * comp] * coords[0]
        moved = moved + wide_ref[3 * comp + 1] * coords[1]
        moved = moved + wide_ref[3 * comp + 2] * coords[2]
        start = comp * width + chunk * LANES
        value = moved - centres_ref[row, :, start : start + LANES]
        dev_ref[comp * frame_total : (comp + 1) * frame_total, span] = value.astype(BF16)


def put_tile(wide_ref, coords_ref, centres_ref, row, rows_dev_ref, dev_ref, out_ref):
    width = coords_ref.shape[2]
    scale = 1.0 / (3 * coords_ref.shape[1])
    stride = 2 * LANES if width % (2 * LANES) == 0 else LANES
    for start in range(0, width, stride):
        for chunk in range(start // LANES, (start + stride) // LANES):
            put_deviations(wide_ref, coords_ref, centres_ref, row, chunk, dev_ref)
        product = jnp.dot(rows_dev_ref[...], dev_ref[:, start : start + stride], preferred_element_type=F32)
        out_ref[:, start : start + stride] = product * scale


def first_tiles_kernel(count, row, col, fits_ref, rows_ref, centres_ref, *refs):
    panel_refs = refs[:count]
    out_ref, rot_out_ref, wide_ref, rows_dev_ref, dev_ref = refs[count:]
    frame_total = rows_ref.shape[1]
    local = rot_out_ref.shape[2]

    @pl.when(pl.program_id(0) == 0)
    def _():
        current = orthogonalized(jnp.sum(fits_ref[...], axis=0), frame_total)
        for a in range(3):
            flat = jnp.concatenate(current[a], axis=0)
            kept = flat[:, :local]
            for block in range(1, frame_total // local):
                kept = jnp.where(col[0] == block, flat[:, block * local : (block + 1) * local], kept)
            rot_out_ref[a] = kept
        entries = [current[a][b] for a in range(3) for b in range(3)]
        columns = jnp.concatenate(entries + [jnp.zeros((7, frame_total), F32)], axis=0).T
        for entry in range(9):
            wide_ref[entry] = jnp.broadcast_to(columns[:, entry : entry + 1], (frame_total, LANES))
        for chunk in range(rows_ref.shape[2] // LANES):
            put_deviations(wide_ref, rows_ref, centres_ref, row[0], chunk, dev_ref)
        rows_dev_ref[...] = dev_ref[...].T

    for step in range(count):

        @pl.when(pl.program_id(0) == step)
        def _(step=step):
            block = col[0] * 2 * count + (lax.rem(row[0], 2 * count) ^ (2 * step))
            put_tile(wide_ref, panel_refs[step], centres_ref, block, rows_dev_ref, dev_ref, out_ref)


def last_tiles_kernel(count, row, col, before_ref, wide_ref, rows_dev_ref, centres_ref, *refs):
    panel_refs = refs[:count]
    out_ref, dev_ref = refs[count:]
    for step in range(count):

        @pl.when(pl.program_id(0) == step)
        def _(step=step):
            block = col[0] * 2 * count + (lax.rem(row[0], 2 * count) ^ (2 * step + 1))
            put_tile(wide_ref, panel_refs[step], centres_ref, block, rows_dev_ref, dev_ref, out_ref)


def per_device(frames, rotations, inverse_cov):
    row_count, col_count = lax.axis_size("row"), lax.axis_size("col")
    members = row_count // col_count
    row = lax.axis_index("row").astype(jnp.int32).reshape(1)
    col = lax.axis_index("col").astype(jnp.int32).reshape(1)
    local, _, width = frames.shape
    frame_total = local * col_count
    device_total = row_count * col_count
    col_width = inverse_cov.shape[1]
    half = members // 2
    coords = jnp.transpose(frames, (1, 0, 2))

    def limit(mib):
        return pltpu.CompilerParams(vmem_limit_bytes=mib * MIB)

    def move(value, source_of, receives=lambda group, col: True):
        pairs = []
        for group in range(col_count):
            for member in range(members):
                for place in range(col_count):
                    if receives(group, place):
                        from_group, from_member, from_col = source_of(group, member, place)
                        source = (from_group * members + from_member) * col_count + from_col
                        pairs.append((source, (group * members + member) * col_count + place))
        return lax.ppermute(value, ("row", "col"), pairs)

    def from_panel_row(value, step):
        return move(value, lambda g, m, c: (c, m, (g + step) % col_count))

    def from_member(value, mask):
        return move(value, lambda g, m, c: (g, m ^ mask, c))

    def limit(mib):
        return pltpu.CompilerParams(vmem_limit_bytes=mib * MIB)

    def in_hbm(value):
        return pltpu.with_memory_space_constraint(value, pltpu.HBM)

    others = [move(coords, lambda g, m, c, s=step: (g, m, (c + s) % col_count)) for step in range(1, col_count)]
    far = [
        move(coords, lambda g, m, c, s=step: (c, m, (g + s) % col_count), lambda g, c: g != c)
        for step in range(col_count)
    ]
    rot_here, coords_here = pl.pallas_call(
        load_kernel,
        out_shape=(jax.ShapeDtypeStruct(rotations.shape, F32), jax.ShapeDtypeStruct(coords.shape, BF16)),
        in_specs=[hbm(), hbm()],
        out_specs=(vmem(), vmem()),
        scratch_shapes=[pltpu.SemaphoreType.DMA((2,))],
        compiler_params=limit(4),
        name="load",
    )(in_hbm(rotations), in_hbm(coords))
    rows_all, repeated = pl.pallas_call(
        rows_kernel,
        out_shape=(
            jax.ShapeDtypeStruct((3, frame_total, width), BF16),
            jax.ShapeDtypeStruct((row_count, 1, 3 * width), F32),
        ),
        in_specs=[smem()] + [vmem()] * (1 + col_count),
        out_specs=(vmem(), vmem()),
        compiler_params=limit(8),
        name="rows",
    )(col, rot_here, coords_here, *others)
    centres = lax.all_to_all(repeated, "row", split_axis=0, concat_axis=0, tiled=True)

    own_block = pl.pallas_call(
        functools.partial(assemble_kernel, members),
        out_shape=jax.ShapeDtypeStruct((3, frame_total, width), BF16),
        in_specs=[smem(), smem()] + [vmem()] * (1 + col_count),
        out_specs=vmem(),
        compiler_params=limit(8),
        cost_estimate=pl.CostEstimate(flops=0, bytes_accessed=100 * MIB, transcendentals=0),
        name="assemble",
    )(row, col, rows_all, *far)
    evens = [own_block] + [from_member(own_block, 2 * step) for step in range(1, half)]

    height = 64 if width % 64 == 0 else 8
    message = pl.pallas_call(
        functools.partial(weighted_fit_kernel, members),
        in_specs=[smem(), smem(), hbm(), vmem(), vmem()],
        out_specs=vmem(),
        scratch_shapes=[
            pltpu.VMEM((width // height, height, col_width), F32),
            pltpu.VMEM((3, 8, col_width), F32),
            pltpu.VMEM((width, LANES), F32),
            pltpu.SemaphoreType.DMA((width // height,)),
        ],
        out_shape=jax.ShapeDtypeStruct((device_total, 8, 2 * frame_total), F32),
        compiler_params=limit(28),
        cost_estimate=pl.CostEstimate(
            flops=6 * width * col_width, bytes_accessed=4 * width * col_width, transcendentals=0
        ),
        name="weighted_fit",
    )(row, col, in_hbm(inverse_cov), centres, rows_all)
    fits = lax.all_to_all(message, ("row", "col"), split_axis=0, concat_axis=0, tiled=True)
    fits, evens = lax.optimization_barrier((fits, evens))
    odds = [from_member(block, 1) for block in evens]

    def tile_spec(odd):
        return pl.BlockSpec((width, width), lambda i, row, *_: (0, lax.rem(row[0], members) ^ (2 * i + odd)))

    tiles_cost = pl.CostEstimate(
        flops=3 * frame_total * width * col_width, bytes_accessed=2 * width * col_width, transcendentals=0
    )
    dev_scratch = pltpu.VMEM((3 * frame_total, width), BF16)
    half_done, transforms, wide, rows_dev = pl.pallas_call(
        functools.partial(first_tiles_kernel, half),
        grid_spec=pltpu.PrefetchScalarGridSpec(
            num_scalar_prefetch=2,
            grid=(half,),
            in_specs=[vmem()] * (3 + half),
            out_specs=(tile_spec(0), vmem(), vmem(), vmem()),
            scratch_shapes=[dev_scratch],
        ),
        out_shape=(
            jax.ShapeDtypeStruct((width, col_width), F32),
            jax.ShapeDtypeStruct((3, 3, local), F32),
            jax.ShapeDtypeStruct((9, frame_total, LANES), F32),
            jax.ShapeDtypeStruct((width, 3 * frame_total), BF16),
        ),
        compiler_params=limit(16),
        cost_estimate=tiles_cost,
        name="steps_and_even_tiles",
    )(row, col, fits, rows_all, centres, *evens)
    covariance = pl.pallas_call(
        functools.partial(last_tiles_kernel, half),
        grid_spec=pltpu.PrefetchScalarGridSpec(
            num_scalar_prefetch=2,
            grid=(half,),
            in_specs=[pl.BlockSpec(memory_space=pl.ANY)] + [vmem()] * (3 + half),
            out_specs=tile_spec(1),
            scratch_shapes=[dev_scratch],
        ),
        out_shape=jax.ShapeDtypeStruct((width, col_width), F32),
        input_output_aliases={2: 0},
        compiler_params=limit(16),
        cost_estimate=tiles_cost,
        name="odd_tiles",
    )(row, col, half_done, wide, rows_dev, centres, *odds)
    return (covariance, transforms)


def solution(mesh):
    placed = (P("col", None, "row"), P(), P("row", "col"))
    return jax.shard_map(
        per_device,
        mesh=mesh,
        in_specs=placed,
        out_specs=(P("row", "col"), P(None, None, "col")),
        check_vma=False,
    )
```

```python
import functools

import jax
import jax.numpy as jnp
from jax import lax
from jax.experimental import pallas as pl
from jax.experimental.pallas import tpu as pltpu
from jax.sharding import PartitionSpec as P

POLAR = 12
LANES = 128
F32 = jnp.float32
BF16 = jnp.bfloat16
MIB = 1 << 20


def vmem():
    return pl.BlockSpec(memory_space=pltpu.VMEM)


def hbm():
    return pl.BlockSpec(memory_space=pl.ANY)


def smem():
    return pl.BlockSpec(memory_space=pltpu.SMEM)


def three_pieces(value):
    high = value.astype(BF16)
    rest = value - high.astype(F32)
    mid = rest.astype(BF16)
    low = (rest - mid.astype(F32)).astype(BF16)
    return high, mid, low


def rotated_sum(rot, coords):
    depth = coords.shape[0] * coords.shape[1]
    flat = jnp.concatenate([rot[:, part, :] for part in range(3)], axis=1)
    padded = jnp.concatenate([flat, jnp.zeros((5, depth), F32)], axis=0)
    stacked = jnp.concatenate(three_pieces(padded), axis=0)
    product = jnp.dot(stacked, coords.reshape(depth, coords.shape[2]), preferred_element_type=F32)
    return (product[16:19] + product[8:11]) + product[0:3]


def put_block(out_ref, block, value):
    local = value.shape[1]
    out_ref[:, pl.ds(pl.multiple_of(block * local, local), local), :] = value


def load_kernel(rot_hbm, coords_hbm, rot_ref, coords_ref, sems):
    copies = [
        pltpu.make_async_copy(rot_hbm, rot_ref, sems.at[0]),
        pltpu.make_async_copy(coords_hbm, coords_ref, sems.at[1]),
    ]
    for copy in copies:
        copy.start()
    for copy in copies:
        copy.wait()


def rows_kernel(col, rot_ref, *refs):
    blocks, (rows_ref, centre_ref) = refs[:-2], refs[-2:]
    for shift, ref in enumerate(blocks):
        put_block(rows_ref, lax.rem(col[0] + shift, len(blocks)), ref[...])
    centre = rotated_sum(rot_ref[...], rows_ref[...]) * (1.0 / rows_ref.shape[1])
    flat = jnp.concatenate([centre[comp : comp + 1, :] for comp in range(3)], axis=1)
    centre_ref[...] = jnp.broadcast_to(flat[None], centre_ref.shape)


def assemble_kernel(members, row, col, rows_ref, *refs):
    sources, out_ref = refs[:-1], refs[-1]
    far_refs, across_refs = sources[: len(sources) // 2], sources[len(sources) // 2 :]
    col_count = len(far_refs) + 1
    distance = lax.rem(col[0] + col_count - row[0] // members, col_count)

    @pl.when(distance == 0)
    def _():
        out_ref[...] = rows_ref[...]

    for step, ref in enumerate(far_refs):

        @pl.when(distance == step + 1)
        def _(ref=ref):
            put_block(out_ref, col[0], ref[...])
            for shift, across_ref in enumerate(across_refs):
                put_block(out_ref, lax.rem(col[0] + 1 + shift, col_count), across_ref[...])


def weighted_fit_kernel(members, row, col, inv_ref, centres_ref, rows_ref, out_ref, strips_ref, wide_ref, weighted_ref, sems):
    strips, height, col_width = strips_ref.shape
    width = rows_ref.shape[2]

    def fetch(strip):
        rows = pl.ds(pl.multiple_of(strip * height, height), height)
        return pltpu.make_async_copy(inv_ref.at[rows, :], strips_ref.at[strip], sems.at[strip])

    for strip in range(strips):
        fetch(strip).start()
    for block in range(members):
        centre = centres_ref[col[0] * members + block]
        for comp in range(3):
            factor = jnp.broadcast_to(centre[:, comp * width : (comp + 1) * width], (8, width))
            wide_ref[comp, :, block * width : (block + 1) * width] = factor
    lane = lax.broadcasted_iota(jnp.int32, (height, LANES), 1)
    chunks = col_width // LANES

    def strip_body(strip, carry):
        fetch(strip).wait()

        def body(chunk, sums):
            span = pl.ds(pl.multiple_of(chunk * LANES, LANES), LANES)
            value = strips_ref[strip, :, span].reshape(height // 8, 8, LANES)
            return tuple(sums[comp] + value * wide_ref[comp, :, span][None] for comp in range(3))

        sums = (jnp.zeros((height // 8, 8, LANES), F32),) * 3
        sums = lax.fori_loop(0, chunks, body, sums, unroll=12 if chunks % 12 == 0 else 1)
        packed = jnp.zeros((height, LANES), F32)
        for comp in range(3):
            total = jnp.sum(sums[comp].reshape(height, LANES), axis=1, keepdims=True)
            packed = jnp.where(lane == comp, total, packed)
        weighted_ref[pl.ds(pl.multiple_of(strip * height, height), height), :] = packed
        return carry

    lax.fori_loop(0, strips, strip_body, 0)
    frame_total = rows_ref.shape[1]
    rows = rows_ref[...].reshape(3 * frame_total, width)
    high, mid, low = (jnp.dot(rows, piece, preferred_element_type=F32) for piece in three_pieces(weighted_ref[...]))
    fits = ((low + mid) + high).T
    entries = [
        fits[comp : comp + 1, part * frame_total : (part + 1) * frame_total] for part in range(3) for comp in range(3)
    ]
    first = jnp.concatenate(entries[:8], axis=0)
    last = jnp.concatenate([entries[8], jnp.zeros((7, frame_total), F32)], axis=0)
    message = jnp.concatenate([first, last], axis=1)
    out_ref[...] = jnp.broadcast_to(message[None], out_ref.shape)


def orthogonalized(message, frame_total):
    fitted = [message[entry : entry + 1, :frame_total] for entry in range(8)]
    fitted.append(message[0:1, frame_total:])
    norm = functools.reduce(lambda a, b: a + b, [value * value for value in fitted])
    scaling = jnp.sqrt(1.0 + norm)
    current = [[fitted[3 * col + row] / scaling for col in range(3)] for row in range(3)]
    for _ in range(POLAR):
        square = [[None] * 3 for _ in range(3)]
        for a in range(3):
            for b in range(a, 3):
                x, y = current[a], current[b]
                square[a][b] = square[b][a] = x[0] * y[0] + x[1] * y[1] + x[2] * y[2]
        cubed = [
            [square[a][0] * current[0][b] + square[a][1] * current[1][b] + square[a][2] * current[2][b] for b in range(3)]
            for a in range(3)
        ]
        current = [[1.5 * current[a][b] - 0.5 * cubed[a][b] for b in range(3)] for a in range(3)]
    return current


def put_deviations(wide_ref, coords_ref, centres_ref, row, chunk, dev_ref):
    frame_total, width = coords_ref.shape[1:]
    span = slice(chunk * LANES, (chunk + 1) * LANES)
    coords = [coords_ref[part, :, span].astype(F32) for part in range(3)]
    for comp in range(3):
        moved = wide_ref[3 * comp] * coords[0]
        moved = moved + wide_ref[3 * comp + 1] * coords[1]
        moved = moved + wide_ref[3 * comp + 2] * coords[2]
        start = comp * width + chunk * LANES
        value = moved - centres_ref[row, :, start : start + LANES]
        dev_ref[comp * frame_total : (comp + 1) * frame_total, span] = value.astype(BF16)


def put_tile(wide_ref, coords_ref, centres_ref, row, rows_dev_ref, dev_ref, out_ref):
    width = coords_ref.shape[2]
    scale = 1.0 / (3 * coords_ref.shape[1])
    stride = 2 * LANES if width % (2 * LANES) == 0 else LANES
    for start in range(0, width, stride):
        for chunk in range(start // LANES, (start + stride) // LANES):
            put_deviations(wide_ref, coords_ref, centres_ref, row, chunk, dev_ref)
        product = jnp.dot(rows_dev_ref[...], dev_ref[:, start : start + stride], preferred_element_type=F32)
        out_ref[:, start : start + stride] = product * scale


def covariance_kernel(members, row, col, fits_ref, rows_ref, centres_ref, *refs):
    panel_refs = refs[:members]
    out_ref, rot_out_ref, wide_ref, rows_dev_ref, dev_ref = refs[members:]
    frame_total = rows_ref.shape[1]
    local = rot_out_ref.shape[2]

    @pl.when(pl.program_id(0) == 0)
    def _():
        current = orthogonalized(jnp.sum(fits_ref[...], axis=0), frame_total)
        for a in range(3):
            flat = jnp.concatenate(current[a], axis=0)
            kept = flat[:, :local]
            for block in range(1, frame_total // local):
                kept = jnp.where(col[0] == block, flat[:, block * local : (block + 1) * local], kept)
            rot_out_ref[a] = kept
        entries = [current[a][b] for a in range(3) for b in range(3)]
        columns = jnp.concatenate(entries + [jnp.zeros((7, frame_total), F32)], axis=0).T
        for entry in range(9):
            wide_ref[entry] = jnp.broadcast_to(columns[:, entry : entry + 1], (frame_total, LANES))
        for chunk in range(rows_ref.shape[2] // LANES):
            put_deviations(wide_ref, rows_ref, centres_ref, row[0], chunk, dev_ref)
        rows_dev_ref[...] = dev_ref[...].T

    for step in range(members):

        @pl.when(pl.program_id(0) == step)
        def _(step=step):
            block = col[0] * members + (lax.rem(row[0], members) ^ step)
            put_tile(wide_ref, panel_refs[step], centres_ref, block, rows_dev_ref, dev_ref, out_ref)


def per_device(frames, rotations, inverse_cov):
    row_count, col_count = lax.axis_size("row"), lax.axis_size("col")
    members = row_count // col_count
    row = lax.axis_index("row").astype(jnp.int32).reshape(1)
    col = lax.axis_index("col").astype(jnp.int32).reshape(1)
    local, _, width = frames.shape
    frame_total = local * col_count
    device_total = row_count * col_count
    col_width = inverse_cov.shape[1]
    half = members // 2
    coords = jnp.transpose(frames, (1, 0, 2))

    def limit(mib):
        return pltpu.CompilerParams(vmem_limit_bytes=mib * MIB)

    def move(value, source_of, receives=lambda group, col: True):
        pairs = []
        for group in range(col_count):
            for member in range(members):
                for place in range(col_count):
                    if receives(group, place):
                        from_group, from_member, from_col = source_of(group, member, place)
                        source = (from_group * members + from_member) * col_count + from_col
                        pairs.append((source, (group * members + member) * col_count + place))
        return lax.ppermute(value, ("row", "col"), pairs)

    def from_panel_row(value, step):
        return move(value, lambda g, m, c: (c, m, (g + step) % col_count))

    def from_member(value, mask):
        return move(value, lambda g, m, c: (g, m ^ mask, c))

    def limit(mib):
        return pltpu.CompilerParams(vmem_limit_bytes=mib * MIB)

    def in_hbm(value):
        return pltpu.with_memory_space_constraint(value, pltpu.HBM)

    far = [move(coords, lambda g, m, c, s=step: ((g + s) % col_count, m, c)) for step in range(1, col_count)]
    others = [move(coords, lambda g, m, c, s=step: (g, m, (c + s) % col_count)) for step in range(1, col_count)]
    rot_here, coords_here = pl.pallas_call(
        load_kernel,
        out_shape=(jax.ShapeDtypeStruct(rotations.shape, F32), jax.ShapeDtypeStruct(coords.shape, BF16)),
        in_specs=[hbm(), hbm()],
        out_specs=(vmem(), vmem()),
        scratch_shapes=[pltpu.SemaphoreType.DMA((2,))],
        compiler_params=limit(4),
        name="load",
    )(in_hbm(rotations), in_hbm(coords))
    rows_all, repeated = pl.pallas_call(
        rows_kernel,
        out_shape=(
            jax.ShapeDtypeStruct((3, frame_total, width), BF16),
            jax.ShapeDtypeStruct((row_count, 1, 3 * width), F32),
        ),
        in_specs=[smem()] + [vmem()] * (1 + col_count),
        out_specs=(vmem(), vmem()),
        compiler_params=limit(8),
        name="rows",
    )(col, rot_here, coords_here, *others)
    centres = lax.all_to_all(repeated, "row", split_axis=0, concat_axis=0, tiled=True)

    distance = lax.rem(col[0] + col_count - row[0] // members, col_count)
    across = []
    for step in range(1, col_count):
        held = far[0]
        if col_count > 2:
            held = lax.select_n(lax.rem(distance + col_count - step, col_count), coords, *far)
        across.append(move(held, lambda g, m, c, s=step: (g, m, (c + s) % col_count), lambda g, c: g != c))
    own_block = pl.pallas_call(
        functools.partial(assemble_kernel, members),
        out_shape=jax.ShapeDtypeStruct((3, frame_total, width), BF16),
        in_specs=[smem(), smem()] + [vmem()] * (2 * col_count - 1),
        out_specs=vmem(),
        compiler_params=limit(8),
        name="assemble",
    )(row, col, rows_all, *far, *across)
    evens = [own_block] + [from_member(own_block, 2 * step) for step in range(1, half)]

    height = 64 if width % 64 == 0 else 8
    message = pl.pallas_call(
        functools.partial(weighted_fit_kernel, members),
        in_specs=[smem(), smem(), hbm(), vmem(), vmem()],
        out_specs=vmem(),
        scratch_shapes=[
            pltpu.VMEM((width // height, height, col_width), F32),
            pltpu.VMEM((3, 8, col_width), F32),
            pltpu.VMEM((width, LANES), F32),
            pltpu.SemaphoreType.DMA((width // height,)),
        ],
        out_shape=jax.ShapeDtypeStruct((device_total, 8, 2 * frame_total), F32),
        compiler_params=limit(28),
        cost_estimate=pl.CostEstimate(
            flops=6 * width * col_width, bytes_accessed=4 * width * col_width, transcendentals=0
        ),
        name="weighted_fit",
    )(row, col, in_hbm(inverse_cov), centres, rows_all)
    fits = lax.all_to_all(message, ("row", "col"), split_axis=0, concat_axis=0, tiled=True)
    panel = [None] * members
    panel[0::2] = evens
    panel[1::2] = [from_member(block, 1) for block in evens]

    covariance, transforms = pl.pallas_call(
        functools.partial(covariance_kernel, members),
        grid_spec=pltpu.PrefetchScalarGridSpec(
            num_scalar_prefetch=2,
            grid=(members,),
            in_specs=[vmem()] * (3 + members),
            out_specs=(
                pl.BlockSpec((width, width), lambda i, row, col: (0, lax.rem(row[0], members) ^ i)),
                vmem(),
            ),
            scratch_shapes=[
                pltpu.VMEM((9, frame_total, LANES), F32),
                pltpu.VMEM((width, 3 * frame_total), BF16),
                pltpu.VMEM((3 * frame_total, width), BF16),
            ],
        ),
        out_shape=(
            jax.ShapeDtypeStruct((width, col_width), F32),
            jax.ShapeDtypeStruct((3, 3, local), F32),
        ),
        compiler_params=limit(16),
        cost_estimate=pl.CostEstimate(
            flops=6 * frame_total * width * col_width, bytes_accessed=4 * width * col_width, transcendentals=0
        ),
        name="covariance",
    )(row, col, fits, rows_all, centres, *panel)
    return (covariance, transforms)


def solution(mesh):
    placed = (P("col", None, "row"), P(), P("row", "col"))
    return jax.shard_map(
        per_device,
        mesh=mesh,
        in_specs=placed,
        out_specs=(P("row", "col"), P(None, None, "col")),
        check_vma=False,
    )
```

```python
import functools

import jax
import jax.numpy as jnp
from jax import lax
from jax.experimental import pallas as pl
from jax.experimental.pallas import tpu as pltpu
from jax.sharding import PartitionSpec as P

POLAR = 12
LANES = 128
F32 = jnp.float32
BF16 = jnp.bfloat16
MIB = 1 << 20


def vmem():
    return pl.BlockSpec(memory_space=pltpu.VMEM)


def hbm():
    return pl.BlockSpec(memory_space=pl.ANY)


def smem():
    return pl.BlockSpec(memory_space=pltpu.SMEM)


def three_pieces(value):
    high = value.astype(BF16)
    rest = value - high.astype(F32)
    mid = rest.astype(BF16)
    low = (rest - mid.astype(F32)).astype(BF16)
    return high, mid, low


def rotated_sum(rot, coords):
    depth = coords.shape[0] * coords.shape[1]
    flat = jnp.concatenate([rot[:, part, :] for part in range(3)], axis=1)
    padded = jnp.concatenate([flat, jnp.zeros((5, depth), F32)], axis=0)
    stacked = jnp.concatenate(three_pieces(padded), axis=0)
    product = jnp.dot(stacked, coords.reshape(depth, coords.shape[2]), preferred_element_type=F32)
    return (product[16:19] + product[8:11]) + product[0:3]


def put_block(out_ref, block, value):
    local = value.shape[1]
    out_ref[:, pl.ds(pl.multiple_of(block * local, local), local), :] = value


def load_kernel(rot_hbm, coords_hbm, rot_ref, coords_ref, sems):
    copies = [
        pltpu.make_async_copy(rot_hbm, rot_ref, sems.at[0]),
        pltpu.make_async_copy(coords_hbm, coords_ref, sems.at[1]),
    ]
    for copy in copies:
        copy.start()
    for copy in copies:
        copy.wait()


def rows_kernel(col, rot_ref, *refs):
    blocks, (rows_ref, centre_ref) = refs[:-2], refs[-2:]
    for shift, ref in enumerate(blocks):
        put_block(rows_ref, lax.rem(col[0] + shift, len(blocks)), ref[...])
    centre = rotated_sum(rot_ref[...], rows_ref[...]) * (1.0 / rows_ref.shape[1])
    flat = jnp.concatenate([centre[comp : comp + 1, :] for comp in range(3)], axis=1)
    centre_ref[...] = jnp.broadcast_to(flat[None], centre_ref.shape)


def pick_kernel(members, step, row, col, rows_ref, *refs):
    far_refs, out_ref = refs[:-1], refs[-1]
    col_count, local = len(far_refs) + 1, out_ref.shape[1]
    index = lax.rem(col[0] + 2 * col_count - row[0] // members - step, col_count)

    @pl.when(index == 0)
    def _():
        out_ref[...] = rows_ref[:, pl.ds(pl.multiple_of(col[0] * local, local), local), :]

    for shift, ref in enumerate(far_refs):

        @pl.when(index == shift + 1)
        def _(ref=ref):
            out_ref[...] = ref[...]


def assemble_kernel(members, row, col, centres_ref, rows_ref, *refs):
    sources, out_ref = refs[:-1], refs[-1]
    far_refs, across_refs = sources[: len(sources) // 2], sources[len(sources) // 2 :]
    col_count = len(far_refs) + 1
    distance = lax.rem(col[0] + col_count - row[0] // members, col_count)

    @pl.when(distance == 0)
    def _():
        out_ref[...] = rows_ref[...]

    for step, ref in enumerate(far_refs):

        @pl.when(distance == step + 1)
        def _(ref=ref):
            put_block(out_ref, col[0], ref[...])
            for shift, across_ref in enumerate(across_refs):
                put_block(out_ref, lax.rem(col[0] + 1 + shift, col_count), across_ref[...])


def weighted_fit_kernel(members, row, col, inv_ref, centres_ref, rows_ref, out_ref, token_ref, strips_ref, wide_ref, weighted_ref, sems):
    strips, height, col_width = strips_ref.shape
    width = rows_ref.shape[2]

    def fetch(strip):
        rows = pl.ds(pl.multiple_of(strip * height, height), height)
        return pltpu.make_async_copy(inv_ref.at[rows, :], strips_ref.at[strip], sems.at[strip])

    for strip in range(strips):
        fetch(strip).start()
    for block in range(members):
        centre = centres_ref[col[0] * members + block]
        for comp in range(3):
            factor = jnp.broadcast_to(centre[:, comp * width : (comp + 1) * width], (8, width))
            wide_ref[comp, :, block * width : (block + 1) * width] = factor
    lane = lax.broadcasted_iota(jnp.int32, (height, LANES), 1)
    chunks = col_width // LANES

    def strip_body(strip, carry):
        fetch(strip).wait()

        def body(chunk, sums):
            span = pl.ds(pl.multiple_of(chunk * LANES, LANES), LANES)
            value = strips_ref[strip, :, span].reshape(height // 8, 8, LANES)
            return tuple(sums[comp] + value * wide_ref[comp, :, span][None] for comp in range(3))

        sums = (jnp.zeros((height // 8, 8, LANES), F32),) * 3
        sums = lax.fori_loop(0, chunks, body, sums, unroll=12 if chunks % 12 == 0 else 1)
        packed = jnp.zeros((height, LANES), F32)
        for comp in range(3):
            total = jnp.sum(sums[comp].reshape(height, LANES), axis=1, keepdims=True)
            packed = jnp.where(lane == comp, total, packed)
        weighted_ref[pl.ds(pl.multiple_of(strip * height, height), height), :] = packed
        return carry

    lax.fori_loop(0, strips, strip_body, 0)
    frame_total = rows_ref.shape[1]
    rows = rows_ref[...].reshape(3 * frame_total, width)
    high, mid, low = (jnp.dot(rows, piece, preferred_element_type=F32) for piece in three_pieces(weighted_ref[...]))
    fits = ((low + mid) + high).T
    entries = [
        fits[comp : comp + 1, part * frame_total : (part + 1) * frame_total] for part in range(3) for comp in range(3)
    ]
    first = jnp.concatenate(entries[:8], axis=0)
    last = jnp.concatenate([entries[8], jnp.zeros((7, frame_total), F32)], axis=0)
    message = jnp.concatenate([first, last], axis=1)
    out_ref[...] = jnp.broadcast_to(message[None], out_ref.shape)
    token_ref[...] = message


def orthogonalized(message, frame_total):
    fitted = [message[entry : entry + 1, :frame_total] for entry in range(8)]
    fitted.append(message[0:1, frame_total:])
    norm = functools.reduce(lambda a, b: a + b, [value * value for value in fitted])
    scaling = jnp.sqrt(1.0 + norm)
    current = [[fitted[3 * col + row] / scaling for col in range(3)] for row in range(3)]
    for _ in range(POLAR):
        square = [[None] * 3 for _ in range(3)]
        for a in range(3):
            for b in range(a, 3):
                x, y = current[a], current[b]
                square[a][b] = square[b][a] = x[0] * y[0] + x[1] * y[1] + x[2] * y[2]
        cubed = [
            [square[a][0] * current[0][b] + square[a][1] * current[1][b] + square[a][2] * current[2][b] for b in range(3)]
            for a in range(3)
        ]
        current = [[1.5 * current[a][b] - 0.5 * cubed[a][b] for b in range(3)] for a in range(3)]
    return current


def put_deviations(wide_ref, coords_ref, centres_ref, row, chunk, dev_ref):
    frame_total, width = coords_ref.shape[1:]
    span = slice(chunk * LANES, (chunk + 1) * LANES)
    coords = [coords_ref[part, :, span].astype(F32) for part in range(3)]
    for comp in range(3):
        moved = wide_ref[3 * comp] * coords[0]
        moved = moved + wide_ref[3 * comp + 1] * coords[1]
        moved = moved + wide_ref[3 * comp + 2] * coords[2]
        start = comp * width + chunk * LANES
        value = moved - centres_ref[row, :, start : start + LANES]
        dev_ref[comp * frame_total : (comp + 1) * frame_total, span] = value.astype(BF16)


def put_tile(wide_ref, coords_ref, centres_ref, row, rows_dev_ref, dev_ref, out_ref):
    width = coords_ref.shape[2]
    scale = 1.0 / (3 * coords_ref.shape[1])
    stride = 2 * LANES if width % (2 * LANES) == 0 else LANES
    for start in range(0, width, stride):
        for chunk in range(start // LANES, (start + stride) // LANES):
            put_deviations(wide_ref, coords_ref, centres_ref, row, chunk, dev_ref)
        product = jnp.dot(rows_dev_ref[...], dev_ref[:, start : start + stride], preferred_element_type=F32)
        out_ref[:, start : start + stride] = product * scale


def covariance_kernel(members, row, col, token_ref, fits_ref, rows_ref, centres_ref, *refs):
    panel_refs = refs[:members]
    out_ref, rot_out_ref, wide_ref, rows_dev_ref, dev_ref = refs[members:]
    frame_total = rows_ref.shape[1]
    local = rot_out_ref.shape[2]

    @pl.when(pl.program_id(0) == 0)
    def _():
        current = orthogonalized(jnp.sum(fits_ref[...], axis=0), frame_total)
        for a in range(3):
            flat = jnp.concatenate(current[a], axis=0)
            kept = flat[:, :local]
            for block in range(1, frame_total // local):
                kept = jnp.where(col[0] == block, flat[:, block * local : (block + 1) * local], kept)
            rot_out_ref[a] = kept
        entries = [current[a][b] for a in range(3) for b in range(3)]
        columns = jnp.concatenate(entries + [jnp.zeros((7, frame_total), F32)], axis=0).T
        for entry in range(9):
            wide_ref[entry] = jnp.broadcast_to(columns[:, entry : entry + 1], (frame_total, LANES))
        for chunk in range(rows_ref.shape[2] // LANES):
            put_deviations(wide_ref, rows_ref, centres_ref, row[0], chunk, dev_ref)
        rows_dev_ref[...] = dev_ref[...].T

    for step in range(members):

        @pl.when(pl.program_id(0) == step)
        def _(step=step):
            block = col[0] * members + (lax.rem(row[0], members) ^ step)
            put_tile(wide_ref, panel_refs[step], centres_ref, block, rows_dev_ref, dev_ref, out_ref)


def per_device(frames, rotations, inverse_cov):
    row_count, col_count = lax.axis_size("row"), lax.axis_size("col")
    members = row_count // col_count
    row = lax.axis_index("row").astype(jnp.int32).reshape(1)
    col = lax.axis_index("col").astype(jnp.int32).reshape(1)
    local, _, width = frames.shape
    frame_total = local * col_count
    device_total = row_count * col_count
    col_width = inverse_cov.shape[1]
    half = members // 2
    coords = jnp.transpose(frames, (1, 0, 2))

    def limit(mib):
        return pltpu.CompilerParams(vmem_limit_bytes=mib * MIB)

    def move(value, source_of, receives=lambda group, col: True):
        pairs = []
        for group in range(col_count):
            for member in range(members):
                for place in range(col_count):
                    if receives(group, place):
                        from_group, from_member, from_col = source_of(group, member, place)
                        source = (from_group * members + from_member) * col_count + from_col
                        pairs.append((source, (group * members + member) * col_count + place))
        return lax.ppermute(value, ("row", "col"), pairs)

    def from_panel_row(value, step):
        return move(value, lambda g, m, c: (c, m, (g + step) % col_count))

    def from_member(value, mask):
        return move(value, lambda g, m, c: (g, m ^ mask, c))

    def limit(mib):
        return pltpu.CompilerParams(vmem_limit_bytes=mib * MIB)

    def in_hbm(value):
        return pltpu.with_memory_space_constraint(value, pltpu.HBM)

    far = [move(coords, lambda g, m, c, s=step: ((g + s) % col_count, m, c)) for step in range(1, col_count)]
    others = [move(coords, lambda g, m, c, s=step: (g, m, (c + s) % col_count)) for step in range(1, col_count)]
    rot_here, coords_here = pl.pallas_call(
        load_kernel,
        out_shape=(jax.ShapeDtypeStruct(rotations.shape, F32), jax.ShapeDtypeStruct(coords.shape, BF16)),
        in_specs=[hbm(), hbm()],
        out_specs=(vmem(), vmem()),
        scratch_shapes=[pltpu.SemaphoreType.DMA((2,))],
        compiler_params=limit(4),
        name="load",
    )(in_hbm(rotations), in_hbm(coords))
    rows_all, repeated = pl.pallas_call(
        rows_kernel,
        out_shape=(
            jax.ShapeDtypeStruct((3, frame_total, width), BF16),
            jax.ShapeDtypeStruct((row_count, 1, 3 * width), F32),
        ),
        in_specs=[smem()] + [vmem()] * (1 + col_count),
        out_specs=(vmem(), vmem()),
        compiler_params=limit(8),
        name="rows",
    )(col, rot_here, coords_here, *others)
    centres = lax.all_to_all(repeated, "row", split_axis=0, concat_axis=0, tiled=True)

    across = []
    for step in range(1, col_count):
        held = pl.pallas_call(
            functools.partial(pick_kernel, members, step),
            out_shape=jax.ShapeDtypeStruct((3, local, width), BF16),
            in_specs=[smem(), smem()] + [vmem()] * col_count,
            out_specs=vmem(),
            compiler_params=limit(4),
            name="pick",
        )(row, col, rows_all, *far)
        across.append(move(held, lambda g, m, c, s=step: (g, m, (c + s) % col_count), lambda g, c: g != c))
    own_block = pl.pallas_call(
        functools.partial(assemble_kernel, members),
        out_shape=jax.ShapeDtypeStruct((3, frame_total, width), BF16),
        in_specs=[smem(), smem()] + [vmem()] * (2 * col_count),
        out_specs=vmem(),
        compiler_params=limit(8),
        name="assemble",
    )(row, col, centres, rows_all, *far, *across)
    evens = [own_block] + [from_member(own_block, 2 * step) for step in range(1, half)]

    height = 64 if width % 64 == 0 else 8
    message, token = pl.pallas_call(
        functools.partial(weighted_fit_kernel, members),
        in_specs=[smem(), smem(), hbm(), vmem(), vmem()],
        out_specs=(vmem(), vmem()),
        scratch_shapes=[
            pltpu.VMEM((width // height, height, col_width), F32),
            pltpu.VMEM((3, 8, col_width), F32),
            pltpu.VMEM((width, LANES), F32),
            pltpu.SemaphoreType.DMA((width // height,)),
        ],
        out_shape=(
            jax.ShapeDtypeStruct((device_total, 8, 2 * frame_total), F32),
            jax.ShapeDtypeStruct((8, 2 * frame_total), F32),
        ),
        compiler_params=limit(28),
        cost_estimate=pl.CostEstimate(
            flops=6 * width * col_width, bytes_accessed=4 * width * col_width, transcendentals=0
        ),
        name="weighted_fit",
    )(row, col, in_hbm(inverse_cov), centres, rows_all)
    fits = lax.all_to_all(message, ("row", "col"), split_axis=0, concat_axis=0, tiled=True)
    token, evens = lax.optimization_barrier((token, evens))
    panel = [None] * members
    panel[0::2] = evens
    panel[1::2] = [from_member(block, 1) for block in evens]

    covariance, transforms = pl.pallas_call(
        functools.partial(covariance_kernel, members),
        grid_spec=pltpu.PrefetchScalarGridSpec(
            num_scalar_prefetch=2,
            grid=(members,),
            in_specs=[vmem()] * (4 + members),
            out_specs=(
                pl.BlockSpec((width, width), lambda i, row, col: (0, lax.rem(row[0], members) ^ i)),
                vmem(),
            ),
            scratch_shapes=[
                pltpu.VMEM((9, frame_total, LANES), F32),
                pltpu.VMEM((width, 3 * frame_total), BF16),
                pltpu.VMEM((3 * frame_total, width), BF16),
            ],
        ),
        out_shape=(
            jax.ShapeDtypeStruct((width, col_width), F32),
            jax.ShapeDtypeStruct((3, 3, local), F32),
        ),
        compiler_params=limit(16),
        cost_estimate=pl.CostEstimate(
            flops=6 * frame_total * width * col_width, bytes_accessed=4 * width * col_width, transcendentals=0
        ),
        name="covariance",
    )(row, col, token, fits, rows_all, centres, *panel)
    return (covariance, transforms)


def solution(mesh):
    placed = (P("col", None, "row"), P(), P("row", "col"))
    return jax.shard_map(
        per_device,
        mesh=mesh,
        in_specs=placed,
        out_specs=(P("row", "col"), P(None, None, "col")),
        check_vma=False,
    )
```

```python
import functools

import jax
import jax.numpy as jnp
from jax import lax
from jax.experimental import pallas as pl
from jax.experimental.pallas import tpu as pltpu
from jax.sharding import PartitionSpec as P

POLAR = 12
LANES = 128
F32 = jnp.float32
BF16 = jnp.bfloat16
MIB = 1 << 20


def vmem():
    return pl.BlockSpec(memory_space=pltpu.VMEM)


def hbm():
    return pl.BlockSpec(memory_space=pl.ANY)


def smem():
    return pl.BlockSpec(memory_space=pltpu.SMEM)


def three_pieces(value):
    high = value.astype(BF16)
    rest = value - high.astype(F32)
    mid = rest.astype(BF16)
    low = (rest - mid.astype(F32)).astype(BF16)
    return high, mid, low


def rotated_sum(rot, coords):
    depth = coords.shape[0] * coords.shape[1]
    flat = jnp.concatenate([rot[:, part, :] for part in range(3)], axis=1)
    padded = jnp.concatenate([flat, jnp.zeros((5, depth), F32)], axis=0)
    stacked = jnp.concatenate(three_pieces(padded), axis=0)
    product = jnp.dot(stacked, coords.reshape(depth, coords.shape[2]), preferred_element_type=F32)
    return (product[16:19] + product[8:11]) + product[0:3]


def put_block(out_ref, block, value):
    local = value.shape[1]
    out_ref[:, pl.ds(pl.multiple_of(block * local, local), local), :] = value


def load_kernel(rot_hbm, coords_hbm, rot_ref, coords_ref, sems):
    copies = [
        pltpu.make_async_copy(rot_hbm, rot_ref, sems.at[0]),
        pltpu.make_async_copy(coords_hbm, coords_ref, sems.at[1]),
    ]
    for copy in copies:
        copy.start()
    for copy in copies:
        copy.wait()


def rows_kernel(col, rot_ref, *refs):
    blocks, (rows_ref, centre_ref) = refs[:-2], refs[-2:]
    for shift, ref in enumerate(blocks):
        put_block(rows_ref, lax.rem(col[0] + shift, len(blocks)), ref[...])
    centre = rotated_sum(rot_ref[...], rows_ref[...]) * (1.0 / rows_ref.shape[1])
    flat = jnp.concatenate([centre[comp : comp + 1, :] for comp in range(3)], axis=1)
    centre_ref[...] = jnp.broadcast_to(flat[None], centre_ref.shape)


def pick_kernel(members, step, row, col, rows_ref, *refs):
    far_refs, out_ref = refs[:-1], refs[-1]
    col_count, local = len(far_refs) + 1, out_ref.shape[1]
    index = lax.rem(col[0] + 2 * col_count - row[0] // members - step, col_count)

    @pl.when(index == 0)
    def _():
        out_ref[...] = rows_ref[:, pl.ds(pl.multiple_of(col[0] * local, local), local), :]

    for shift, ref in enumerate(far_refs):

        @pl.when(index == shift + 1)
        def _(ref=ref):
            out_ref[...] = ref[...]


def assemble_kernel(members, row, col, centres_ref, rows_ref, *refs):
    sources, out_ref = refs[:-1], refs[-1]
    far_refs, across_refs = sources[: len(sources) // 2], sources[len(sources) // 2 :]
    col_count = len(far_refs) + 1
    distance = lax.rem(col[0] + col_count - row[0] // members, col_count)

    @pl.when(distance == 0)
    def _():
        out_ref[...] = rows_ref[...]

    for step, ref in enumerate(far_refs):

        @pl.when(distance == step + 1)
        def _(ref=ref):
            put_block(out_ref, col[0], ref[...])
            for shift, across_ref in enumerate(across_refs):
                put_block(out_ref, lax.rem(col[0] + 1 + shift, col_count), across_ref[...])


def weighted_fit_kernel(members, row, col, inv_ref, centres_ref, rows_ref, out_ref, strips_ref, wide_ref, weighted_ref, sems):
    strips, height, col_width = strips_ref.shape
    width = rows_ref.shape[2]

    def fetch(strip):
        rows = pl.ds(pl.multiple_of(strip * height, height), height)
        return pltpu.make_async_copy(inv_ref.at[rows, :], strips_ref.at[strip], sems.at[strip])

    for strip in range(strips):
        fetch(strip).start()
    for block in range(members):
        centre = centres_ref[col[0] * members + block]
        for comp in range(3):
            factor = jnp.broadcast_to(centre[:, comp * width : (comp + 1) * width], (8, width))
            wide_ref[comp, :, block * width : (block + 1) * width] = factor
    lane = lax.broadcasted_iota(jnp.int32, (height, LANES), 1)
    chunks = col_width // LANES

    def strip_body(strip, carry):
        fetch(strip).wait()

        def body(chunk, sums):
            span = pl.ds(pl.multiple_of(chunk * LANES, LANES), LANES)
            value = strips_ref[strip, :, span].reshape(height // 8, 8, LANES)
            return tuple(sums[comp] + value * wide_ref[comp, :, span][None] for comp in range(3))

        sums = (jnp.zeros((height // 8, 8, LANES), F32),) * 3
        sums = lax.fori_loop(0, chunks, body, sums, unroll=12 if chunks % 12 == 0 else 1)
        packed = jnp.zeros((height, LANES), F32)
        for comp in range(3):
            total = jnp.sum(sums[comp].reshape(height, LANES), axis=1, keepdims=True)
            packed = jnp.where(lane == comp, total, packed)
        weighted_ref[pl.ds(pl.multiple_of(strip * height, height), height), :] = packed
        return carry

    lax.fori_loop(0, strips, strip_body, 0)
    frame_total = rows_ref.shape[1]
    rows = rows_ref[...].reshape(3 * frame_total, width)
    high, mid, low = (jnp.dot(rows, piece, preferred_element_type=F32) for piece in three_pieces(weighted_ref[...]))
    fits = ((low + mid) + high).T
    entries = [
        fits[comp : comp + 1, part * frame_total : (part + 1) * frame_total] for part in range(3) for comp in range(3)
    ]
    first = jnp.concatenate(entries[:8], axis=0)
    last = jnp.concatenate([entries[8], jnp.zeros((7, frame_total), F32)], axis=0)
    message = jnp.concatenate([first, last], axis=1)
    out_ref[...] = jnp.broadcast_to(message[None], out_ref.shape)


def stack_kernel(*refs):
    for index, ref in enumerate(refs[:-1]):
        refs[-1][index] = ref[...]


def orthogonalized(message, frame_total):
    fitted = [message[entry : entry + 1, :frame_total] for entry in range(8)]
    fitted.append(message[0:1, frame_total:])
    norm = functools.reduce(lambda a, b: a + b, [value * value for value in fitted])
    scaling = jnp.sqrt(1.0 + norm)
    current = [[fitted[3 * col + row] / scaling for col in range(3)] for row in range(3)]
    for _ in range(POLAR):
        square = [[None] * 3 for _ in range(3)]
        for a in range(3):
            for b in range(a, 3):
                x, y = current[a], current[b]
                square[a][b] = square[b][a] = x[0] * y[0] + x[1] * y[1] + x[2] * y[2]
        cubed = [
            [square[a][0] * current[0][b] + square[a][1] * current[1][b] + square[a][2] * current[2][b] for b in range(3)]
            for a in range(3)
        ]
        current = [[1.5 * current[a][b] - 0.5 * cubed[a][b] for b in range(3)] for a in range(3)]
    return current


def put_deviations(wide_ref, coords_ref, centres_ref, row, chunk, dev_ref):
    frame_total, width = coords_ref.shape[1:]
    span = slice(chunk * LANES, (chunk + 1) * LANES)
    coords = [coords_ref[part, :, span].astype(F32) for part in range(3)]
    for comp in range(3):
        moved = wide_ref[3 * comp] * coords[0]
        moved = moved + wide_ref[3 * comp + 1] * coords[1]
        moved = moved + wide_ref[3 * comp + 2] * coords[2]
        start = comp * width + chunk * LANES
        value = moved - centres_ref[row, :, start : start + LANES]
        dev_ref[comp * frame_total : (comp + 1) * frame_total, span] = value.astype(BF16)


def put_tile(wide_ref, coords_ref, centres_ref, row, rows_dev_ref, dev_ref, out_ref):
    width = coords_ref.shape[2]
    scale = 1.0 / (3 * coords_ref.shape[1])
    stride = 2 * LANES if width % (2 * LANES) == 0 else LANES
    for start in range(0, width, stride):
        for chunk in range(start // LANES, (start + stride) // LANES):
            put_deviations(wide_ref, coords_ref, centres_ref, row, chunk, dev_ref)
        product = jnp.dot(rows_dev_ref[...], dev_ref[:, start : start + stride], preferred_element_type=F32)
        out_ref[:, start : start + stride] = product * scale


def first_tiles_kernel(count, row, col, fits_ref, rows_ref, centres_ref, *refs):
    panel_refs = refs[:count]
    out_ref, rot_out_ref, wide_ref, rows_dev_ref, dev_ref = refs[count:]
    frame_total = rows_ref.shape[1]
    local = rot_out_ref.shape[2]

    @pl.when(pl.program_id(0) == 0)
    def _():
        current = orthogonalized(jnp.sum(fits_ref[...], axis=0), frame_total)
        for a in range(3):
            flat = jnp.concatenate(current[a], axis=0)
            kept = flat[:, :local]
            for block in range(1, frame_total // local):
                kept = jnp.where(col[0] == block, flat[:, block * local : (block + 1) * local], kept)
            rot_out_ref[a] = kept
        entries = [current[a][b] for a in range(3) for b in range(3)]
        columns = jnp.concatenate(entries + [jnp.zeros((7, frame_total), F32)], axis=0).T
        for entry in range(9):
            wide_ref[entry] = jnp.broadcast_to(columns[:, entry : entry + 1], (frame_total, LANES))
        for chunk in range(rows_ref.shape[2] // LANES):
            put_deviations(wide_ref, rows_ref, centres_ref, row[0], chunk, dev_ref)
        rows_dev_ref[...] = dev_ref[...].T

    for step in range(count):

        @pl.when(pl.program_id(0) == step)
        def _(step=step):
            block = col[0] * 2 * count + (lax.rem(row[0], 2 * count) ^ (2 * step))
            put_tile(wide_ref, panel_refs[step], centres_ref, block, rows_dev_ref, dev_ref, out_ref)


def last_tiles_kernel(count, row, col, before_ref, wide_ref, rows_dev_ref, centres_ref, panel_ref, out_ref, dev_ref):
    for step in range(count):

        @pl.when(pl.program_id(0) == step)
        def _(step=step):
            block = col[0] * 2 * count + (lax.rem(row[0], 2 * count) ^ (2 * step + 1))
            put_tile(wide_ref, panel_ref.at[step], centres_ref, block, rows_dev_ref, dev_ref, out_ref)


def per_device(frames, rotations, inverse_cov):
    row_count, col_count = lax.axis_size("row"), lax.axis_size("col")
    members = row_count // col_count
    row = lax.axis_index("row").astype(jnp.int32).reshape(1)
    col = lax.axis_index("col").astype(jnp.int32).reshape(1)
    local, _, width = frames.shape
    frame_total = local * col_count
    device_total = row_count * col_count
    col_width = inverse_cov.shape[1]
    half = members // 2
    coords = jnp.transpose(frames, (1, 0, 2))

    def limit(mib):
        return pltpu.CompilerParams(vmem_limit_bytes=mib * MIB)

    def move(value, source_of, receives=lambda group, col: True):
        pairs = []
        for group in range(col_count):
            for member in range(members):
                for place in range(col_count):
                    if receives(group, place):
                        from_group, from_member, from_col = source_of(group, member, place)
                        source = (from_group * members + from_member) * col_count + from_col
                        pairs.append((source, (group * members + member) * col_count + place))
        return lax.ppermute(value, ("row", "col"), pairs)

    def from_panel_row(value, step):
        return move(value, lambda g, m, c: (c, m, (g + step) % col_count))

    def from_member(value, mask):
        return move(value, lambda g, m, c: (g, m ^ mask, c))

    def limit(mib):
        return pltpu.CompilerParams(vmem_limit_bytes=mib * MIB)

    def in_hbm(value):
        return pltpu.with_memory_space_constraint(value, pltpu.HBM)

    far = [move(coords, lambda g, m, c, s=step: ((g + s) % col_count, m, c)) for step in range(1, col_count)]
    others = [move(coords, lambda g, m, c, s=step: (g, m, (c + s) % col_count)) for step in range(1, col_count)]
    rot_here, coords_here = pl.pallas_call(
        load_kernel,
        out_shape=(jax.ShapeDtypeStruct(rotations.shape, F32), jax.ShapeDtypeStruct(coords.shape, BF16)),
        in_specs=[hbm(), hbm()],
        out_specs=(vmem(), vmem()),
        scratch_shapes=[pltpu.SemaphoreType.DMA((2,))],
        compiler_params=limit(4),
        name="load",
    )(in_hbm(rotations), in_hbm(coords))
    rows_all, repeated = pl.pallas_call(
        rows_kernel,
        out_shape=(
            jax.ShapeDtypeStruct((3, frame_total, width), BF16),
            jax.ShapeDtypeStruct((row_count, 1, 3 * width), F32),
        ),
        in_specs=[smem()] + [vmem()] * (1 + col_count),
        out_specs=(vmem(), vmem()),
        compiler_params=limit(8),
        name="rows",
    )(col, rot_here, coords_here, *others)
    centres = lax.all_to_all(repeated, "row", split_axis=0, concat_axis=0, tiled=True)

    across = []
    for step in range(1, col_count):
        held = pl.pallas_call(
            functools.partial(pick_kernel, members, step),
            out_shape=jax.ShapeDtypeStruct((3, local, width), BF16),
            in_specs=[smem(), smem()] + [vmem()] * col_count,
            out_specs=vmem(),
            compiler_params=limit(4),
            name="pick",
        )(row, col, rows_all, *far)
        across.append(move(held, lambda g, m, c, s=step: (g, m, (c + s) % col_count), lambda g, c: g != c))
    own_block = pl.pallas_call(
        functools.partial(assemble_kernel, members),
        out_shape=jax.ShapeDtypeStruct((3, frame_total, width), BF16),
        in_specs=[smem(), smem()] + [vmem()] * (2 * col_count),
        out_specs=vmem(),
        compiler_params=limit(8),
        name="assemble",
    )(row, col, centres, rows_all, *far, *across)
    evens = [own_block] + [from_member(own_block, 2 * step) for step in range(1, half)]

    height = 64 if width % 64 == 0 else 8
    message = pl.pallas_call(
        functools.partial(weighted_fit_kernel, members),
        in_specs=[smem(), smem(), hbm(), vmem(), vmem()],
        out_specs=vmem(),
        scratch_shapes=[
            pltpu.VMEM((width // height, height, col_width), F32),
            pltpu.VMEM((3, 8, col_width), F32),
            pltpu.VMEM((width, LANES), F32),
            pltpu.SemaphoreType.DMA((width // height,)),
        ],
        out_shape=jax.ShapeDtypeStruct((device_total, 8, 2 * frame_total), F32),
        compiler_params=limit(28),
        cost_estimate=pl.CostEstimate(
            flops=6 * width * col_width, bytes_accessed=4 * width * col_width, transcendentals=0
        ),
        name="weighted_fit",
    )(row, col, in_hbm(inverse_cov), centres, rows_all)
    fits = lax.all_to_all(message, ("row", "col"), split_axis=0, concat_axis=0, tiled=True)
    fits, evens = lax.optimization_barrier((fits, evens))
    stacked = pl.pallas_call(
        stack_kernel,
        out_shape=jax.ShapeDtypeStruct((half, 3, frame_total, width), BF16),
        in_specs=[vmem()] * half,
        out_specs=vmem(),
        compiler_params=limit(8),
        name="stack_panel",
    )(*evens)
    odds = from_member(stacked, 1)

    def tile_spec(odd):
        return pl.BlockSpec((width, width), lambda i, row, *_: (0, lax.rem(row[0], members) ^ (2 * i + odd)))

    tiles_cost = pl.CostEstimate(
        flops=3 * frame_total * width * col_width, bytes_accessed=2 * width * col_width, transcendentals=0
    )
    dev_scratch = pltpu.VMEM((3 * frame_total, width), BF16)
    half_done, transforms, wide, rows_dev = pl.pallas_call(
        functools.partial(first_tiles_kernel, half),
        grid_spec=pltpu.PrefetchScalarGridSpec(
            num_scalar_prefetch=2,
            grid=(half,),
            in_specs=[vmem()] * (3 + half),
            out_specs=(tile_spec(0), vmem(), vmem(), vmem()),
            scratch_shapes=[dev_scratch],
        ),
        out_shape=(
            jax.ShapeDtypeStruct((width, col_width), F32),
            jax.ShapeDtypeStruct((3, 3, local), F32),
            jax.ShapeDtypeStruct((9, frame_total, LANES), F32),
            jax.ShapeDtypeStruct((width, 3 * frame_total), BF16),
        ),
        compiler_params=limit(16),
        cost_estimate=tiles_cost,
        name="steps_and_even_tiles",
    )(row, col, fits, rows_all, centres, *evens)
    covariance = pl.pallas_call(
        functools.partial(last_tiles_kernel, half),
        grid_spec=pltpu.PrefetchScalarGridSpec(
            num_scalar_prefetch=2,
            grid=(half,),
            in_specs=[pl.BlockSpec(memory_space=pl.ANY)] + [vmem()] * 4,
            out_specs=tile_spec(1),
            scratch_shapes=[dev_scratch],
        ),
        out_shape=jax.ShapeDtypeStruct((width, col_width), F32),
        input_output_aliases={2: 0},
        compiler_params=limit(16),
        cost_estimate=tiles_cost,
        name="odd_tiles",
    )(row, col, half_done, wide, rows_dev, centres, odds)
    return (covariance, transforms)


def solution(mesh):
    placed = (P("col", None, "row"), P(), P("row", "col"))
    return jax.shard_map(
        per_device,
        mesh=mesh,
        in_specs=placed,
        out_specs=(P("row", "col"), P(None, None, "col")),
        check_vma=False,
    )
```

```python
import functools

import jax
import jax.numpy as jnp
from jax import lax
from jax.experimental import pallas as pl
from jax.experimental.pallas import tpu as pltpu
from jax.sharding import PartitionSpec as P

POLAR = 12
LANES = 128
F32 = jnp.float32
BF16 = jnp.bfloat16
MIB = 1 << 20


def vmem():
    return pl.BlockSpec(memory_space=pltpu.VMEM)


def hbm():
    return pl.BlockSpec(memory_space=pl.ANY)


def smem():
    return pl.BlockSpec(memory_space=pltpu.SMEM)


def three_pieces(value):
    high = value.astype(BF16)
    rest = value - high.astype(F32)
    mid = rest.astype(BF16)
    low = (rest - mid.astype(F32)).astype(BF16)
    return high, mid, low


def rotated_sum(rot, coords):
    depth = coords.shape[0] * coords.shape[1]
    flat = jnp.concatenate([rot[:, part, :] for part in range(3)], axis=1)
    padded = jnp.concatenate([flat, jnp.zeros((5, depth), F32)], axis=0)
    stacked = jnp.concatenate(three_pieces(padded), axis=0)
    product = jnp.dot(stacked, coords.reshape(depth, coords.shape[2]), preferred_element_type=F32)
    return (product[16:19] + product[8:11]) + product[0:3]


def put_block(out_ref, block, value):
    local = value.shape[1]
    out_ref[:, pl.ds(pl.multiple_of(block * local, local), local), :] = value


def load_kernel(rot_hbm, coords_hbm, rot_ref, coords_ref, sems):
    copies = [
        pltpu.make_async_copy(rot_hbm, rot_ref, sems.at[0]),
        pltpu.make_async_copy(coords_hbm, coords_ref, sems.at[1]),
    ]
    for copy in copies:
        copy.start()
    for copy in copies:
        copy.wait()


def rows_kernel(col, rot_ref, *refs):
    blocks, (rows_ref, centre_ref) = refs[:-2], refs[-2:]
    for shift, ref in enumerate(blocks):
        put_block(rows_ref, lax.rem(col[0] + shift, len(blocks)), ref[...])
    centre = rotated_sum(rot_ref[...], rows_ref[...]) * (1.0 / rows_ref.shape[1])
    flat = jnp.concatenate([centre[comp : comp + 1, :] for comp in range(3)], axis=1)
    centre_ref[...] = jnp.broadcast_to(flat[None], centre_ref.shape)


def pick_kernel(members, step, row, col, rows_ref, *refs):
    far_refs, out_ref = refs[:-1], refs[-1]
    col_count, local = len(far_refs) + 1, out_ref.shape[1]
    index = lax.rem(col[0] + 2 * col_count - row[0] // members - step, col_count)

    @pl.when(index == 0)
    def _():
        out_ref[...] = rows_ref[:, pl.ds(pl.multiple_of(col[0] * local, local), local), :]

    for shift, ref in enumerate(far_refs):

        @pl.when(index == shift + 1)
        def _(ref=ref):
            out_ref[...] = ref[...]


def assemble_kernel(members, row, col, centres_ref, rows_ref, *refs):
    sources, out_ref = refs[:-1], refs[-1]
    far_refs, across_refs = sources[: len(sources) // 2], sources[len(sources) // 2 :]
    col_count = len(far_refs) + 1
    distance = lax.rem(col[0] + col_count - row[0] // members, col_count)

    @pl.when(distance == 0)
    def _():
        out_ref[...] = rows_ref[...]

    for step, ref in enumerate(far_refs):

        @pl.when(distance == step + 1)
        def _(ref=ref):
            put_block(out_ref, col[0], ref[...])
            for shift, across_ref in enumerate(across_refs):
                put_block(out_ref, lax.rem(col[0] + 1 + shift, col_count), across_ref[...])


def weighted_fit_kernel(members, row, col, inv_ref, centres_ref, rows_ref, out_ref, strips_ref, wide_ref, weighted_ref, sems):
    strips, height, col_width = strips_ref.shape
    width = rows_ref.shape[2]

    def fetch(strip):
        rows = pl.ds(pl.multiple_of(strip * height, height), height)
        return pltpu.make_async_copy(inv_ref.at[rows, :], strips_ref.at[strip], sems.at[strip])

    for strip in range(strips):
        fetch(strip).start()
    for block in range(members):
        centre = centres_ref[col[0] * members + block]
        for comp in range(3):
            factor = jnp.broadcast_to(centre[:, comp * width : (comp + 1) * width], (8, width))
            wide_ref[comp, :, block * width : (block + 1) * width] = factor
    lane = lax.broadcasted_iota(jnp.int32, (height, LANES), 1)
    chunks = col_width // LANES

    def strip_body(strip, carry):
        fetch(strip).wait()

        def body(chunk, sums):
            span = pl.ds(pl.multiple_of(chunk * LANES, LANES), LANES)
            value = strips_ref[strip, :, span].reshape(height // 8, 8, LANES)
            return tuple(sums[comp] + value * wide_ref[comp, :, span][None] for comp in range(3))

        sums = (jnp.zeros((height // 8, 8, LANES), F32),) * 3
        sums = lax.fori_loop(0, chunks, body, sums, unroll=12 if chunks % 12 == 0 else 1)
        packed = jnp.zeros((height, LANES), F32)
        for comp in range(3):
            total = jnp.sum(sums[comp].reshape(height, LANES), axis=1, keepdims=True)
            packed = jnp.where(lane == comp, total, packed)
        weighted_ref[pl.ds(pl.multiple_of(strip * height, height), height), :] = packed
        return carry

    lax.fori_loop(0, strips, strip_body, 0)
    frame_total = rows_ref.shape[1]
    rows = rows_ref[...].reshape(3 * frame_total, width)
    high, mid, low = (jnp.dot(rows, piece, preferred_element_type=F32) for piece in three_pieces(weighted_ref[...]))
    fits = ((low + mid) + high).T
    entries = [
        fits[comp : comp + 1, part * frame_total : (part + 1) * frame_total] for part in range(3) for comp in range(3)
    ]
    first = jnp.concatenate(entries[:8], axis=0)
    last = jnp.concatenate([entries[8], jnp.zeros((7, frame_total), F32)], axis=0)
    message = jnp.concatenate([first, last], axis=1)
    out_ref[...] = jnp.broadcast_to(message[None], out_ref.shape)


def stack_kernel(*refs):
    for index, ref in enumerate(refs[:-1]):
        refs[-1][index] = ref[...]


def orthogonalized(message, frame_total):
    fitted = [message[entry : entry + 1, :frame_total] for entry in range(8)]
    fitted.append(message[0:1, frame_total:])
    norm = functools.reduce(lambda a, b: a + b, [value * value for value in fitted])
    scaling = jnp.sqrt(1.0 + norm)
    current = [[fitted[3 * col + row] / scaling for col in range(3)] for row in range(3)]
    for _ in range(POLAR):
        square = [[None] * 3 for _ in range(3)]
        for a in range(3):
            for b in range(a, 3):
                x, y = current[a], current[b]
                square[a][b] = square[b][a] = x[0] * y[0] + x[1] * y[1] + x[2] * y[2]
        cubed = [
            [square[a][0] * current[0][b] + square[a][1] * current[1][b] + square[a][2] * current[2][b] for b in range(3)]
            for a in range(3)
        ]
        current = [[1.5 * current[a][b] - 0.5 * cubed[a][b] for b in range(3)] for a in range(3)]
    return current


def put_deviations(wide_ref, coords_ref, centres_ref, row, chunk, dev_ref):
    frame_total, width = coords_ref.shape[1:]
    span = slice(chunk * LANES, (chunk + 1) * LANES)
    coords = [coords_ref[part, :, span].astype(F32) for part in range(3)]
    for comp in range(3):
        moved = wide_ref[3 * comp] * coords[0]
        moved = moved + wide_ref[3 * comp + 1] * coords[1]
        moved = moved + wide_ref[3 * comp + 2] * coords[2]
        start = comp * width + chunk * LANES
        value = moved - centres_ref[row, :, start : start + LANES]
        dev_ref[comp * frame_total : (comp + 1) * frame_total, span] = value.astype(BF16)


def put_tile(wide_ref, coords_ref, centres_ref, row, rows_dev_ref, dev_ref, out_ref):
    width = coords_ref.shape[2]
    scale = 1.0 / (3 * coords_ref.shape[1])
    stride = 2 * LANES if width % (2 * LANES) == 0 else LANES
    for start in range(0, width, stride):
        for chunk in range(start // LANES, (start + stride) // LANES):
            put_deviations(wide_ref, coords_ref, centres_ref, row, chunk, dev_ref)
        product = jnp.dot(rows_dev_ref[...], dev_ref[:, start : start + stride], preferred_element_type=F32)
        out_ref[:, start : start + stride] = product * scale


def put_tiles(odd, row, col, wide_ref, centres_ref, panel, rows_dev_ref, dev_ref, tile_ref, sems, out_ref):
    width = tile_ref.shape[1]
    members = out_ref.shape[1] // width
    parts = sems.shape[1]
    strip = width // parts
    writes = []
    for step, coords_ref in enumerate(panel):
        slot = step % 2
        if step >= 2:
            for write in writes[step - 2]:
                write.wait()
        block = lax.rem(row[0], members) ^ (2 * step + odd)
        tile = tile_ref.at[slot]
        put_tile(wide_ref, coords_ref, centres_ref, col[0] * members + block, rows_dev_ref, dev_ref, tile)
        columns = pl.ds(pl.multiple_of(block * width, LANES), width)
        copies = []
        for part in range(parts):
            span = pl.ds(part * strip, strip)
            copies.append(pltpu.make_async_copy(tile.at[span, :], out_ref.at[span, columns], sems.at[slot, part]))
            copies[-1].start()
        writes.append(copies)
    for copies in writes[-2:]:
        for write in copies:
            write.wait()


def first_tiles_kernel(count, row, col, fits_ref, rows_ref, centres_ref, *refs):
    panel_refs = refs[:count]
    out_ref, rot_out_ref, wide_ref, rows_dev_ref, rows_t_ref, dev_ref, tile_ref, sems = refs[count:]
    frame_total = rows_ref.shape[1]
    local = rot_out_ref.shape[2]

    current = orthogonalized(jnp.sum(fits_ref[...], axis=0), frame_total)
    for a in range(3):
        flat = jnp.concatenate(current[a], axis=0)
        kept = flat[:, :local]
        for block in range(1, frame_total // local):
            kept = jnp.where(col[0] == block, flat[:, block * local : (block + 1) * local], kept)
        rot_out_ref[a] = kept
    entries = [current[a][b] for a in range(3) for b in range(3)]
    columns = jnp.concatenate(entries + [jnp.zeros((7, frame_total), F32)], axis=0).T
    for entry in range(9):
        wide_ref[entry] = jnp.broadcast_to(columns[:, entry : entry + 1], (frame_total, LANES))
    for chunk in range(rows_ref.shape[2] // LANES):
        put_deviations(wide_ref, rows_ref, centres_ref, row[0], chunk, rows_t_ref)
    rows_dev_ref[...] = rows_t_ref[...].T

    put_tiles(0, row, col, wide_ref, centres_ref, panel_refs, rows_dev_ref, dev_ref, tile_ref, sems, out_ref)


def last_tiles_kernel(
    count, row, col, before_ref, wide_ref, rows_dev_ref, centres_ref, panel_ref, out_ref, dev_ref, tile_ref, sems
):
    panel = [panel_ref.at[step] for step in range(count)]
    put_tiles(1, row, col, wide_ref, centres_ref, panel, rows_dev_ref, dev_ref, tile_ref, sems, out_ref)


def per_device(frames, rotations, inverse_cov):
    row_count, col_count = lax.axis_size("row"), lax.axis_size("col")
    members = row_count // col_count
    row = lax.axis_index("row").astype(jnp.int32).reshape(1)
    col = lax.axis_index("col").astype(jnp.int32).reshape(1)
    local, _, width = frames.shape
    frame_total = local * col_count
    device_total = row_count * col_count
    col_width = inverse_cov.shape[1]
    half = members // 2
    coords = jnp.transpose(frames, (1, 0, 2))

    def limit(mib):
        return pltpu.CompilerParams(vmem_limit_bytes=mib * MIB)

    def move(value, source_of, receives=lambda group, col: True):
        pairs = []
        for group in range(col_count):
            for member in range(members):
                for place in range(col_count):
                    if receives(group, place):
                        from_group, from_member, from_col = source_of(group, member, place)
                        source = (from_group * members + from_member) * col_count + from_col
                        pairs.append((source, (group * members + member) * col_count + place))
        return lax.ppermute(value, ("row", "col"), pairs)

    def from_panel_row(value, step):
        return move(value, lambda g, m, c: (c, m, (g + step) % col_count))

    def from_member(value, mask):
        return move(value, lambda g, m, c: (g, m ^ mask, c))

    def limit(mib):
        return pltpu.CompilerParams(vmem_limit_bytes=mib * MIB)

    def in_hbm(value):
        return pltpu.with_memory_space_constraint(value, pltpu.HBM)

    far = [move(coords, lambda g, m, c, s=step: ((g + s) % col_count, m, c)) for step in range(1, col_count)]
    others = [move(coords, lambda g, m, c, s=step: (g, m, (c + s) % col_count)) for step in range(1, col_count)]
    rot_here, coords_here = pl.pallas_call(
        load_kernel,
        out_shape=(jax.ShapeDtypeStruct(rotations.shape, F32), jax.ShapeDtypeStruct(coords.shape, BF16)),
        in_specs=[hbm(), hbm()],
        out_specs=(vmem(), vmem()),
        scratch_shapes=[pltpu.SemaphoreType.DMA((2,))],
        compiler_params=limit(4),
        name="load",
    )(in_hbm(rotations), in_hbm(coords))
    rows_all, repeated = pl.pallas_call(
        rows_kernel,
        out_shape=(
            jax.ShapeDtypeStruct((3, frame_total, width), BF16),
            jax.ShapeDtypeStruct((row_count, 1, 3 * width), F32),
        ),
        in_specs=[smem()] + [vmem()] * (1 + col_count),
        out_specs=(vmem(), vmem()),
        compiler_params=limit(8),
        name="rows",
    )(col, rot_here, coords_here, *others)
    centres = lax.all_to_all(repeated, "row", split_axis=0, concat_axis=0, tiled=True)

    across = []
    for step in range(1, col_count):
        held = pl.pallas_call(
            functools.partial(pick_kernel, members, step),
            out_shape=jax.ShapeDtypeStruct((3, local, width), BF16),
            in_specs=[smem(), smem()] + [vmem()] * col_count,
            out_specs=vmem(),
            compiler_params=limit(4),
            name="pick",
        )(row, col, rows_all, *far)
        across.append(move(held, lambda g, m, c, s=step: (g, m, (c + s) % col_count), lambda g, c: g != c))
    own_block = pl.pallas_call(
        functools.partial(assemble_kernel, members),
        out_shape=jax.ShapeDtypeStruct((3, frame_total, width), BF16),
        in_specs=[smem(), smem()] + [vmem()] * (2 * col_count),
        out_specs=vmem(),
        compiler_params=limit(8),
        name="assemble",
    )(row, col, centres, rows_all, *far, *across)
    evens = [own_block] + [from_member(own_block, 2 * step) for step in range(1, half)]

    height = 64 if width % 64 == 0 else 8
    message = pl.pallas_call(
        functools.partial(weighted_fit_kernel, members),
        in_specs=[smem(), smem(), hbm(), vmem(), vmem()],
        out_specs=vmem(),
        scratch_shapes=[
            pltpu.VMEM((width // height, height, col_width), F32),
            pltpu.VMEM((3, 8, col_width), F32),
            pltpu.VMEM((width, LANES), F32),
            pltpu.SemaphoreType.DMA((width // height,)),
        ],
        out_shape=jax.ShapeDtypeStruct((device_total, 8, 2 * frame_total), F32),
        compiler_params=limit(28),
        cost_estimate=pl.CostEstimate(
            flops=6 * width * col_width, bytes_accessed=4 * width * col_width, transcendentals=0
        ),
        name="weighted_fit",
    )(row, col, in_hbm(inverse_cov), centres, rows_all)
    fits = lax.all_to_all(message, ("row", "col"), split_axis=0, concat_axis=0, tiled=True)
    fits, evens = lax.optimization_barrier((fits, evens))
    stacked = pl.pallas_call(
        stack_kernel,
        out_shape=jax.ShapeDtypeStruct((half, 3, frame_total, width), BF16),
        in_specs=[vmem()] * half,
        out_specs=vmem(),
        compiler_params=limit(8),
        name="stack_panel",
    )(*evens)
    odds = from_member(stacked, 1)

    depth = 3 * frame_total
    parts = 4 if width % 64 == 0 else 1
    tile_scratch = [
        pltpu.VMEM((depth, width), BF16),
        pltpu.VMEM((2, width, width), F32),
        pltpu.SemaphoreType.DMA((2, parts)),
    ]
    tiles_cost = pl.CostEstimate(
        flops=3 * frame_total * width * col_width, bytes_accessed=2 * width * col_width, transcendentals=0
    )
    half_done, transforms, wide, rows_dev = pl.pallas_call(
        functools.partial(first_tiles_kernel, half),
        in_specs=[smem(), smem()] + [vmem()] * (3 + half),
        out_specs=(hbm(), vmem(), vmem(), vmem()),
        scratch_shapes=[pltpu.VMEM((depth, width), BF16)] + tile_scratch,
        out_shape=(
            jax.ShapeDtypeStruct((width, col_width), F32),
            jax.ShapeDtypeStruct((3, 3, local), F32),
            jax.ShapeDtypeStruct((9, frame_total, LANES), F32),
            jax.ShapeDtypeStruct((width, depth), BF16),
        ),
        compiler_params=limit(16),
        cost_estimate=tiles_cost,
        name="steps_and_even_tiles",
    )(row, col, fits, rows_all, centres, *evens)
    covariance = pl.pallas_call(
        functools.partial(last_tiles_kernel, half),
        in_specs=[smem(), smem(), hbm()] + [vmem()] * 4,
        out_specs=hbm(),
        scratch_shapes=tile_scratch,
        out_shape=jax.ShapeDtypeStruct((width, col_width), F32),
        input_output_aliases={2: 0},
        compiler_params=limit(16),
        cost_estimate=tiles_cost,
        name="odd_tiles",
    )(row, col, half_done, wide, rows_dev, centres, odds)
    return (covariance, transforms)


def solution(mesh):
    placed = (P("col", None, "row"), P(), P("row", "col"))
    return jax.shard_map(
        per_device,
        mesh=mesh,
        in_specs=placed,
        out_specs=(P("row", "col"), P(None, None, "col")),
        check_vma=False,
    )
```

```python
import functools

import jax
import jax.numpy as jnp
from jax import lax
from jax.experimental import pallas as pl
from jax.experimental.pallas import tpu as pltpu
from jax.sharding import PartitionSpec as P

POLAR = 12
LANES = 128
F32 = jnp.float32
BF16 = jnp.bfloat16
MIB = 1 << 20


def vmem():
    return pl.BlockSpec(memory_space=pltpu.VMEM)


def hbm():
    return pl.BlockSpec(memory_space=pl.ANY)


def smem():
    return pl.BlockSpec(memory_space=pltpu.SMEM)


def three_pieces(value):
    high = value.astype(BF16)
    rest = value - high.astype(F32)
    mid = rest.astype(BF16)
    low = (rest - mid.astype(F32)).astype(BF16)
    return high, mid, low


def rotated_sum(rot, coords):
    depth = coords.shape[0] * coords.shape[1]
    flat = jnp.concatenate([rot[:, part, :] for part in range(3)], axis=1)
    padded = jnp.concatenate([flat, jnp.zeros((5, depth), F32)], axis=0)
    stacked = jnp.concatenate(three_pieces(padded), axis=0)
    product = jnp.dot(stacked, coords.reshape(depth, coords.shape[2]), preferred_element_type=F32)
    return (product[16:19] + product[8:11]) + product[0:3]


def put_block(out_ref, block, value):
    local = value.shape[1]
    out_ref[:, pl.ds(pl.multiple_of(block * local, local), local), :] = value


def load_kernel(rot_hbm, coords_hbm, rot_ref, coords_ref, sems):
    copies = [
        pltpu.make_async_copy(rot_hbm, rot_ref, sems.at[0]),
        pltpu.make_async_copy(coords_hbm, coords_ref, sems.at[1]),
    ]
    for copy in copies:
        copy.start()
    for copy in copies:
        copy.wait()


def rows_kernel(col, rot_ref, *refs):
    blocks, (rows_ref, centre_ref) = refs[:-2], refs[-2:]
    for shift, ref in enumerate(blocks):
        put_block(rows_ref, lax.rem(col[0] + shift, len(blocks)), ref[...])
    centre = rotated_sum(rot_ref[...], rows_ref[...]) * (1.0 / rows_ref.shape[1])
    flat = jnp.concatenate([centre[comp : comp + 1, :] for comp in range(3)], axis=1)
    centre_ref[...] = jnp.broadcast_to(flat[None], centre_ref.shape)


def pick_kernel(members, step, row, col, rows_ref, *refs):
    far_refs, out_ref = refs[:-1], refs[-1]
    col_count, local = len(far_refs) + 1, out_ref.shape[1]
    index = lax.rem(col[0] + 2 * col_count - row[0] // members - step, col_count)

    @pl.when(index == 0)
    def _():
        out_ref[...] = rows_ref[:, pl.ds(pl.multiple_of(col[0] * local, local), local), :]

    for shift, ref in enumerate(far_refs):

        @pl.when(index == shift + 1)
        def _(ref=ref):
            out_ref[...] = ref[...]


def assemble_kernel(members, row, col, centres_ref, rows_ref, *refs):
    sources, out_ref = refs[:-1], refs[-1]
    far_refs, across_refs = sources[: len(sources) // 2], sources[len(sources) // 2 :]
    col_count = len(far_refs) + 1
    distance = lax.rem(col[0] + col_count - row[0] // members, col_count)

    @pl.when(distance == 0)
    def _():
        out_ref[...] = rows_ref[...]

    for step, ref in enumerate(far_refs):

        @pl.when(distance == step + 1)
        def _(ref=ref):
            put_block(out_ref, col[0], ref[...])
            for shift, across_ref in enumerate(across_refs):
                put_block(out_ref, lax.rem(col[0] + 1 + shift, col_count), across_ref[...])


def weighted_fit_kernel(members, row, col, inv_ref, centres_ref, rows_ref, out_ref, strips_ref, wide_ref, weighted_ref, sems):
    strips, height, col_width = strips_ref.shape
    width = rows_ref.shape[2]

    def fetch(strip):
        rows = pl.ds(pl.multiple_of(strip * height, height), height)
        return pltpu.make_async_copy(inv_ref.at[rows, :], strips_ref.at[strip], sems.at[strip])

    for strip in range(strips):
        fetch(strip).start()
    for block in range(members):
        centre = centres_ref[col[0] * members + block]
        for comp in range(3):
            factor = jnp.broadcast_to(centre[:, comp * width : (comp + 1) * width], (8, width))
            wide_ref[comp, :, block * width : (block + 1) * width] = factor
    lane = lax.broadcasted_iota(jnp.int32, (height, LANES), 1)
    chunks = col_width // LANES

    def strip_body(strip, carry):
        fetch(strip).wait()

        def body(chunk, sums):
            span = pl.ds(pl.multiple_of(chunk * LANES, LANES), LANES)
            value = strips_ref[strip, :, span].reshape(height // 8, 8, LANES)
            return tuple(sums[comp] + value * wide_ref[comp, :, span][None] for comp in range(3))

        sums = (jnp.zeros((height // 8, 8, LANES), F32),) * 3
        sums = lax.fori_loop(0, chunks, body, sums, unroll=12 if chunks % 12 == 0 else 1)
        packed = jnp.zeros((height, LANES), F32)
        for comp in range(3):
            total = jnp.sum(sums[comp].reshape(height, LANES), axis=1, keepdims=True)
            packed = jnp.where(lane == comp, total, packed)
        weighted_ref[pl.ds(pl.multiple_of(strip * height, height), height), :] = packed
        return carry

    lax.fori_loop(0, strips, strip_body, 0)
    frame_total = rows_ref.shape[1]
    rows = rows_ref[...].reshape(3 * frame_total, width)
    high, mid, low = (jnp.dot(rows, piece, preferred_element_type=F32) for piece in three_pieces(weighted_ref[...]))
    fits = ((low + mid) + high).T
    entries = [
        fits[comp : comp + 1, part * frame_total : (part + 1) * frame_total] for part in range(3) for comp in range(3)
    ]
    first = jnp.concatenate(entries[:8], axis=0)
    last = jnp.concatenate([entries[8], jnp.zeros((7, frame_total), F32)], axis=0)
    message = jnp.concatenate([first, last], axis=1)
    out_ref[...] = jnp.broadcast_to(message[None], out_ref.shape)


def stack_kernel(*refs):
    for index, ref in enumerate(refs[:-1]):
        refs[-1][index] = ref[...]


def orthogonalized(message, frame_total):
    fitted = [message[entry : entry + 1, :frame_total] for entry in range(8)]
    fitted.append(message[0:1, frame_total:])
    norm = functools.reduce(lambda a, b: a + b, [value * value for value in fitted])
    scaling = jnp.sqrt(1.0 + norm)
    current = [[fitted[3 * col + row] / scaling for col in range(3)] for row in range(3)]
    for _ in range(POLAR):
        square = [[None] * 3 for _ in range(3)]
        for a in range(3):
            for b in range(a, 3):
                x, y = current[a], current[b]
                square[a][b] = square[b][a] = x[0] * y[0] + x[1] * y[1] + x[2] * y[2]
        cubed = [
            [square[a][0] * current[0][b] + square[a][1] * current[1][b] + square[a][2] * current[2][b] for b in range(3)]
            for a in range(3)
        ]
        current = [[1.5 * current[a][b] - 0.5 * cubed[a][b] for b in range(3)] for a in range(3)]
    return current


def put_deviations(wide_ref, coords_ref, centres_ref, row, chunk, dev_ref):
    frame_total, width = coords_ref.shape[1:]
    span = slice(chunk * LANES, (chunk + 1) * LANES)
    coords = [coords_ref[part, :, span].astype(F32) for part in range(3)]
    for comp in range(3):
        moved = wide_ref[3 * comp] * coords[0]
        moved = moved + wide_ref[3 * comp + 1] * coords[1]
        moved = moved + wide_ref[3 * comp + 2] * coords[2]
        start = comp * width + chunk * LANES
        value = moved - centres_ref[row, :, start : start + LANES]
        dev_ref[comp * frame_total : (comp + 1) * frame_total, span] = value.astype(BF16)


def put_tile(wide_ref, coords_ref, centres_ref, row, rows_dev_ref, dev_ref, out_ref):
    width = coords_ref.shape[2]
    scale = 1.0 / (3 * coords_ref.shape[1])
    stride = 2 * LANES if width % (2 * LANES) == 0 else LANES
    for start in range(0, width, stride):
        for chunk in range(start // LANES, (start + stride) // LANES):
            put_deviations(wide_ref, coords_ref, centres_ref, row, chunk, dev_ref)
        product = jnp.dot(rows_dev_ref[...], dev_ref[:, start : start + stride], preferred_element_type=F32)
        out_ref[:, start : start + stride] = product * scale


def first_tiles_kernel(count, row, col, fits_ref, rows_ref, centres_ref, *refs):
    panel_refs = refs[:count]
    out_ref, rot_out_ref, wide_ref, rows_dev_ref, dev_ref, rows_t_ref = refs[count:]
    frame_total = rows_ref.shape[1]
    local = rot_out_ref.shape[2]

    def head():
        current = orthogonalized(jnp.sum(fits_ref[...], axis=0), frame_total)
        for a in range(3):
            flat = jnp.concatenate(current[a], axis=0)
            kept = flat[:, :local]
            for block in range(1, frame_total // local):
                kept = jnp.where(col[0] == block, flat[:, block * local : (block + 1) * local], kept)
            rot_out_ref[a] = kept
        entries = [current[a][b] for a in range(3) for b in range(3)]
        columns = jnp.concatenate(entries + [jnp.zeros((7, frame_total), F32)], axis=0).T
        for entry in range(9):
            wide_ref[entry] = jnp.broadcast_to(columns[:, entry : entry + 1], (frame_total, LANES))
        for chunk in range(rows_ref.shape[2] // LANES):
            put_deviations(wide_ref, rows_ref, centres_ref, row[0], chunk, rows_t_ref)
        rows_dev_ref[...] = rows_t_ref[...].T

    for step in range(count):

        @pl.when(pl.program_id(0) == step)
        def _(step=step):
            if step == 0:
                head()
            block = col[0] * 2 * count + (lax.rem(row[0], 2 * count) ^ (2 * step))
            put_tile(wide_ref, panel_refs[step], centres_ref, block, rows_dev_ref, dev_ref, out_ref)


def last_tiles_kernel(count, row, col, before_ref, wide_ref, rows_dev_ref, centres_ref, panel_ref, out_ref, dev_ref):
    for step in range(count):

        @pl.when(pl.program_id(0) == step)
        def _(step=step):
            block = col[0] * 2 * count + (lax.rem(row[0], 2 * count) ^ (2 * step + 1))
            put_tile(wide_ref, panel_ref.at[step], centres_ref, block, rows_dev_ref, dev_ref, out_ref)


def per_device(frames, rotations, inverse_cov):
    row_count, col_count = lax.axis_size("row"), lax.axis_size("col")
    members = row_count // col_count
    row = lax.axis_index("row").astype(jnp.int32).reshape(1)
    col = lax.axis_index("col").astype(jnp.int32).reshape(1)
    local, _, width = frames.shape
    frame_total = local * col_count
    device_total = row_count * col_count
    col_width = inverse_cov.shape[1]
    half = members // 2
    coords = jnp.transpose(frames, (1, 0, 2))

    def limit(mib):
        return pltpu.CompilerParams(vmem_limit_bytes=mib * MIB)

    def move(value, source_of, receives=lambda group, col: True):
        pairs = []
        for group in range(col_count):
            for member in range(members):
                for place in range(col_count):
                    if receives(group, place):
                        from_group, from_member, from_col = source_of(group, member, place)
                        source = (from_group * members + from_member) * col_count + from_col
                        pairs.append((source, (group * members + member) * col_count + place))
        return lax.ppermute(value, ("row", "col"), pairs)

    def from_panel_row(value, step):
        return move(value, lambda g, m, c: (c, m, (g + step) % col_count))

    def from_member(value, mask):
        return move(value, lambda g, m, c: (g, m ^ mask, c))

    def limit(mib):
        return pltpu.CompilerParams(vmem_limit_bytes=mib * MIB)

    def in_hbm(value):
        return pltpu.with_memory_space_constraint(value, pltpu.HBM)

    far = [move(coords, lambda g, m, c, s=step: ((g + s) % col_count, m, c)) for step in range(1, col_count)]
    others = [move(coords, lambda g, m, c, s=step: (g, m, (c + s) % col_count)) for step in range(1, col_count)]
    rot_here, coords_here = pl.pallas_call(
        load_kernel,
        out_shape=(jax.ShapeDtypeStruct(rotations.shape, F32), jax.ShapeDtypeStruct(coords.shape, BF16)),
        in_specs=[hbm(), hbm()],
        out_specs=(vmem(), vmem()),
        scratch_shapes=[pltpu.SemaphoreType.DMA((2,))],
        compiler_params=limit(4),
        name="load",
    )(in_hbm(rotations), in_hbm(coords))
    rows_all, repeated = pl.pallas_call(
        rows_kernel,
        out_shape=(
            jax.ShapeDtypeStruct((3, frame_total, width), BF16),
            jax.ShapeDtypeStruct((row_count, 1, 3 * width), F32),
        ),
        in_specs=[smem()] + [vmem()] * (1 + col_count),
        out_specs=(vmem(), vmem()),
        compiler_params=limit(8),
        name="rows",
    )(col, rot_here, coords_here, *others)
    centres = lax.all_to_all(repeated, "row", split_axis=0, concat_axis=0, tiled=True)

    across = []
    for step in range(1, col_count):
        held = pl.pallas_call(
            functools.partial(pick_kernel, members, step),
            out_shape=jax.ShapeDtypeStruct((3, local, width), BF16),
            in_specs=[smem(), smem()] + [vmem()] * col_count,
            out_specs=vmem(),
            compiler_params=limit(4),
            name="pick",
        )(row, col, rows_all, *far)
        across.append(move(held, lambda g, m, c, s=step: (g, m, (c + s) % col_count), lambda g, c: g != c))
    own_block = pl.pallas_call(
        functools.partial(assemble_kernel, members),
        out_shape=jax.ShapeDtypeStruct((3, frame_total, width), BF16),
        in_specs=[smem(), smem()] + [vmem()] * (2 * col_count),
        out_specs=vmem(),
        compiler_params=limit(8),
        name="assemble",
    )(row, col, centres, rows_all, *far, *across)
    evens = [own_block] + [from_member(own_block, 2 * step) for step in range(1, half)]

    height = 64 if width % 64 == 0 else 8
    message = pl.pallas_call(
        functools.partial(weighted_fit_kernel, members),
        in_specs=[smem(), smem(), hbm(), vmem(), vmem()],
        out_specs=vmem(),
        scratch_shapes=[
            pltpu.VMEM((width // height, height, col_width), F32),
            pltpu.VMEM((3, 8, col_width), F32),
            pltpu.VMEM((width, LANES), F32),
            pltpu.SemaphoreType.DMA((width // height,)),
        ],
        out_shape=jax.ShapeDtypeStruct((device_total, 8, 2 * frame_total), F32),
        compiler_params=limit(28),
        cost_estimate=pl.CostEstimate(
            flops=6 * width * col_width, bytes_accessed=4 * width * col_width, transcendentals=0
        ),
        name="weighted_fit",
    )(row, col, in_hbm(inverse_cov), centres, rows_all)
    fits = lax.all_to_all(message, ("row", "col"), split_axis=0, concat_axis=0, tiled=True)
    fits, evens = lax.optimization_barrier((fits, evens))
    stacked = pl.pallas_call(
        stack_kernel,
        out_shape=jax.ShapeDtypeStruct((half, 3, frame_total, width), BF16),
        in_specs=[vmem()] * half,
        out_specs=vmem(),
        compiler_params=limit(8),
        name="stack_panel",
    )(*evens)
    odds = from_member(stacked, 1)

    def tile_spec(odd):
        return pl.BlockSpec((width, width), lambda i, row, *_: (0, lax.rem(row[0], members) ^ (2 * i + odd)))

    tiles_cost = pl.CostEstimate(
        flops=3 * frame_total * width * col_width, bytes_accessed=2 * width * col_width, transcendentals=0
    )
    dev_scratch = pltpu.VMEM((3 * frame_total, width), BF16)
    half_done, transforms, wide, rows_dev = pl.pallas_call(
        functools.partial(first_tiles_kernel, half),
        grid_spec=pltpu.PrefetchScalarGridSpec(
            num_scalar_prefetch=2,
            grid=(half,),
            in_specs=[vmem()] * (3 + half),
            out_specs=(tile_spec(0), vmem(), vmem(), vmem()),
            scratch_shapes=[dev_scratch, dev_scratch],
        ),
        out_shape=(
            jax.ShapeDtypeStruct((width, col_width), F32),
            jax.ShapeDtypeStruct((3, 3, local), F32),
            jax.ShapeDtypeStruct((9, frame_total, LANES), F32),
            jax.ShapeDtypeStruct((width, 3 * frame_total), BF16),
        ),
        compiler_params=limit(16),
        cost_estimate=tiles_cost,
        name="steps_and_even_tiles",
    )(row, col, fits, rows_all, centres, *evens)
    covariance = pl.pallas_call(
        functools.partial(last_tiles_kernel, half),
        grid_spec=pltpu.PrefetchScalarGridSpec(
            num_scalar_prefetch=2,
            grid=(half,),
            in_specs=[pl.BlockSpec(memory_space=pl.ANY)] + [vmem()] * 4,
            out_specs=tile_spec(1),
            scratch_shapes=[dev_scratch],
        ),
        out_shape=jax.ShapeDtypeStruct((width, col_width), F32),
        input_output_aliases={2: 0},
        compiler_params=limit(16),
        cost_estimate=tiles_cost,
        name="odd_tiles",
    )(row, col, half_done, wide, rows_dev, centres, odds)
    return (covariance, transforms)


def solution(mesh):
    placed = (P("col", None, "row"), P(), P("row", "col"))
    return jax.shard_map(
        per_device,
        mesh=mesh,
        in_specs=placed,
        out_specs=(P("row", "col"), P(None, None, "col")),
        check_vma=False,
    )
```

```python
import functools

import jax
import jax.numpy as jnp
from jax import lax
from jax.experimental import pallas as pl
from jax.experimental.pallas import tpu as pltpu
from jax.sharding import PartitionSpec as P

POLAR = 12
LANES = 128
F32 = jnp.float32
BF16 = jnp.bfloat16
MIB = 1 << 20


def vmem():
    return pl.BlockSpec(memory_space=pltpu.VMEM)


def hbm():
    return pl.BlockSpec(memory_space=pl.ANY)


def smem():
    return pl.BlockSpec(memory_space=pltpu.SMEM)


def three_pieces(value):
    high = value.astype(BF16)
    rest = value - high.astype(F32)
    mid = rest.astype(BF16)
    low = (rest - mid.astype(F32)).astype(BF16)
    return high, mid, low


def rotated_sum(rot, coords):
    depth = coords.shape[0] * coords.shape[1]
    flat = jnp.concatenate([rot[:, part, :] for part in range(3)], axis=1)
    padded = jnp.concatenate([flat, jnp.zeros((5, depth), F32)], axis=0)
    stacked = jnp.concatenate(three_pieces(padded), axis=0)
    product = jnp.dot(stacked, coords.reshape(depth, coords.shape[2]), preferred_element_type=F32)
    return (product[16:19] + product[8:11]) + product[0:3]


def put_block(out_ref, block, value):
    local = value.shape[1]
    out_ref[:, pl.ds(pl.multiple_of(block * local, local), local), :] = value


def load_kernel(rot_hbm, coords_hbm, rot_ref, coords_ref, sems):
    copies = [
        pltpu.make_async_copy(rot_hbm, rot_ref, sems.at[0]),
        pltpu.make_async_copy(coords_hbm, coords_ref, sems.at[1]),
    ]
    for copy in copies:
        copy.start()
    for copy in copies:
        copy.wait()


def rows_kernel(col, rot_ref, *refs):
    blocks, (rows_ref, centre_ref) = refs[:-2], refs[-2:]
    for shift, ref in enumerate(blocks):
        put_block(rows_ref, lax.rem(col[0] + shift, len(blocks)), ref[...])
    centre = rotated_sum(rot_ref[...], rows_ref[...]) * (1.0 / rows_ref.shape[1])
    flat = jnp.concatenate([centre[comp : comp + 1, :] for comp in range(3)], axis=1)
    centre_ref[...] = jnp.broadcast_to(flat[None], centre_ref.shape)


def pick_kernel(members, step, row, col, rows_ref, *refs):
    far_refs, out_ref = refs[:-1], refs[-1]
    col_count, local = len(far_refs) + 1, out_ref.shape[1]
    index = lax.rem(col[0] + 2 * col_count - row[0] // members - step, col_count)

    @pl.when(index == 0)
    def _():
        out_ref[...] = rows_ref[:, pl.ds(pl.multiple_of(col[0] * local, local), local), :]

    for shift, ref in enumerate(far_refs):

        @pl.when(index == shift + 1)
        def _(ref=ref):
            out_ref[...] = ref[...]


def assemble_kernel(members, row, col, centres_ref, rows_ref, *refs):
    sources, out_ref = refs[:-1], refs[-1]
    far_refs, across_refs = sources[: len(sources) // 2], sources[len(sources) // 2 :]
    col_count = len(far_refs) + 1
    distance = lax.rem(col[0] + col_count - row[0] // members, col_count)

    @pl.when(distance == 0)
    def _():
        out_ref[...] = rows_ref[...]

    for step, ref in enumerate(far_refs):

        @pl.when(distance == step + 1)
        def _(ref=ref):
            put_block(out_ref, col[0], ref[...])
            for shift, across_ref in enumerate(across_refs):
                put_block(out_ref, lax.rem(col[0] + 1 + shift, col_count), across_ref[...])


def weighted_fit_kernel(members, row, col, inv_ref, centres_ref, rows_ref, out_ref, strips_ref, wide_ref, weighted_ref, sems):
    strips, height, col_width = strips_ref.shape
    width = rows_ref.shape[2]

    def fetch(strip):
        rows = pl.ds(pl.multiple_of(strip * height, height), height)
        return pltpu.make_async_copy(inv_ref.at[rows, :], strips_ref.at[strip], sems.at[strip])

    for strip in range(strips):
        fetch(strip).start()
    for block in range(members):
        centre = centres_ref[col[0] * members + block]
        for comp in range(3):
            factor = jnp.broadcast_to(centre[:, comp * width : (comp + 1) * width], (8, width))
            wide_ref[comp, :, block * width : (block + 1) * width] = factor
    lane = lax.broadcasted_iota(jnp.int32, (height, LANES), 1)
    chunks = col_width // LANES

    def strip_body(strip, carry):
        fetch(strip).wait()

        def body(chunk, sums):
            span = pl.ds(pl.multiple_of(chunk * LANES, LANES), LANES)
            value = strips_ref[strip, :, span].reshape(height // 8, 8, LANES)
            return tuple(sums[comp] + value * wide_ref[comp, :, span][None] for comp in range(3))

        sums = (jnp.zeros((height // 8, 8, LANES), F32),) * 3
        sums = lax.fori_loop(0, chunks, body, sums, unroll=12 if chunks % 12 == 0 else 1)
        packed = jnp.zeros((height, LANES), F32)
        for comp in range(3):
            total = jnp.sum(sums[comp].reshape(height, LANES), axis=1, keepdims=True)
            packed = jnp.where(lane == comp, total, packed)
        weighted_ref[pl.ds(pl.multiple_of(strip * height, height), height), :] = packed
        return carry

    lax.fori_loop(0, strips, strip_body, 0)
    frame_total = rows_ref.shape[1]
    rows = rows_ref[...].reshape(3 * frame_total, width)
    high, mid, low = (jnp.dot(rows, piece, preferred_element_type=F32) for piece in three_pieces(weighted_ref[...]))
    fits = ((low + mid) + high).T
    entries = [
        fits[comp : comp + 1, part * frame_total : (part + 1) * frame_total] for part in range(3) for comp in range(3)
    ]
    first = jnp.concatenate(entries[:8], axis=0)
    last = jnp.concatenate([entries[8], jnp.zeros((7, frame_total), F32)], axis=0)
    message = jnp.concatenate([first, last], axis=1)
    out_ref[...] = jnp.broadcast_to(message[None], out_ref.shape)


def stack_kernel(*refs):
    for index, ref in enumerate(refs[:-1]):
        refs[-1][index] = ref[...]


def orthogonalized(message, frame_total):
    fitted = [message[entry : entry + 1, :frame_total] for entry in range(8)]
    fitted.append(message[0:1, frame_total:])
    norm = functools.reduce(lambda a, b: a + b, [value * value for value in fitted])
    scaling = jnp.sqrt(1.0 + norm)
    current = [[fitted[3 * col + row] / scaling for col in range(3)] for row in range(3)]
    for _ in range(POLAR):
        square = [[None] * 3 for _ in range(3)]
        for a in range(3):
            for b in range(a, 3):
                x, y = current[a], current[b]
                square[a][b] = square[b][a] = x[0] * y[0] + x[1] * y[1] + x[2] * y[2]
        cubed = [
            [square[a][0] * current[0][b] + square[a][1] * current[1][b] + square[a][2] * current[2][b] for b in range(3)]
            for a in range(3)
        ]
        current = [[1.5 * current[a][b] - 0.5 * cubed[a][b] for b in range(3)] for a in range(3)]
    return current


def put_deviations(wide_ref, coords_ref, centres_ref, row, chunk, dev_ref):
    frame_total, width = coords_ref.shape[1:]
    span = slice(chunk * LANES, (chunk + 1) * LANES)
    coords = [coords_ref[part, :, span].astype(F32) for part in range(3)]
    for comp in range(3):
        moved = wide_ref[3 * comp] * coords[0]
        moved = moved + wide_ref[3 * comp + 1] * coords[1]
        moved = moved + wide_ref[3 * comp + 2] * coords[2]
        start = comp * width + chunk * LANES
        value = moved - centres_ref[row, :, start : start + LANES]
        dev_ref[comp * frame_total : (comp + 1) * frame_total, span] = value.astype(BF16)


def put_tile(wide_ref, coords_ref, centres_ref, row, rows_dev_ref, dev_ref, out_ref):
    width = coords_ref.shape[2]
    scale = 1.0 / (3 * coords_ref.shape[1])
    stride = 2 * LANES if width % (2 * LANES) == 0 else LANES
    for start in range(0, width, stride):
        for chunk in range(start // LANES, (start + stride) // LANES):
            put_deviations(wide_ref, coords_ref, centres_ref, row, chunk, dev_ref)
        product = jnp.dot(rows_dev_ref[...], dev_ref[:, start : start + stride], preferred_element_type=F32)
        out_ref[:, start : start + stride] = product * scale


def first_tiles_kernel(count, row, col, fits_ref, rows_ref, centres_ref, *refs):
    panel_refs = refs[:count]
    out_ref, rot_out_ref, wide_ref, rows_dev_ref, dev_ref, rows_t_ref = refs[count:]
    frame_total = rows_ref.shape[1]
    local = rot_out_ref.shape[2]

    def head():
        current = orthogonalized(jnp.sum(fits_ref[...], axis=0), frame_total)
        for a in range(3):
            flat = jnp.concatenate(current[a], axis=0)
            kept = flat[:, :local]
            for block in range(1, frame_total // local):
                kept = jnp.where(col[0] == block, flat[:, block * local : (block + 1) * local], kept)
            rot_out_ref[a] = kept
        entries = [current[a][b] for a in range(3) for b in range(3)]
        columns = jnp.concatenate(entries + [jnp.zeros((7, frame_total), F32)], axis=0).T
        for entry in range(9):
            wide_ref[entry] = jnp.broadcast_to(columns[:, entry : entry + 1], (frame_total, LANES))
        for chunk in range(rows_ref.shape[2] // LANES):
            put_deviations(wide_ref, rows_ref, centres_ref, row[0], chunk, rows_t_ref)
        rows_dev_ref[...] = rows_t_ref[...].T

    for step in range(count):

        @pl.when(pl.program_id(0) == step)
        def _(step=step):
            if step == 0:
                head()
            block = col[0] * 2 * count + (lax.rem(row[0], 2 * count) ^ (2 * step))
            put_tile(wide_ref, panel_refs[step], centres_ref, block, rows_dev_ref, dev_ref, out_ref)


def last_tiles_kernel(count, row, col, before_ref, wide_ref, rows_dev_ref, centres_ref, panel_ref, out_ref, dev_ref):
    for step in range(count):

        @pl.when(pl.program_id(0) == step)
        def _(step=step):
            block = col[0] * 2 * count + (lax.rem(row[0], 2 * count) ^ (2 * step + 1))
            put_tile(wide_ref, panel_ref.at[step], centres_ref, block, rows_dev_ref, dev_ref, out_ref)


def per_device(frames, rotations, inverse_cov):
    row_count, col_count = lax.axis_size("row"), lax.axis_size("col")
    members = row_count // col_count
    row = lax.axis_index("row").astype(jnp.int32).reshape(1)
    col = lax.axis_index("col").astype(jnp.int32).reshape(1)
    local, _, width = frames.shape
    frame_total = local * col_count
    device_total = row_count * col_count
    col_width = inverse_cov.shape[1]
    half = members // 2
    coords = jnp.transpose(frames, (1, 0, 2))

    def limit(mib):
        return pltpu.CompilerParams(vmem_limit_bytes=mib * MIB)

    def move(value, source_of, receives=lambda group, col: True):
        pairs = []
        for group in range(col_count):
            for member in range(members):
                for place in range(col_count):
                    if receives(group, place):
                        from_group, from_member, from_col = source_of(group, member, place)
                        source = (from_group * members + from_member) * col_count + from_col
                        pairs.append((source, (group * members + member) * col_count + place))
        return lax.ppermute(value, ("row", "col"), pairs)

    def from_panel_row(value, step):
        return move(value, lambda g, m, c: (c, m, (g + step) % col_count))

    def from_member(value, mask):
        return move(value, lambda g, m, c: (g, m ^ mask, c))

    def limit(mib):
        return pltpu.CompilerParams(vmem_limit_bytes=mib * MIB)

    def in_hbm(value):
        return pltpu.with_memory_space_constraint(value, pltpu.HBM)

    far = [move(coords, lambda g, m, c, s=step: ((g + s) % col_count, m, c)) for step in range(1, col_count)]
    others = [move(coords, lambda g, m, c, s=step: (g, m, (c + s) % col_count)) for step in range(1, col_count)]
    rot_here, coords_here = pl.pallas_call(
        load_kernel,
        out_shape=(jax.ShapeDtypeStruct(rotations.shape, F32), jax.ShapeDtypeStruct(coords.shape, BF16)),
        in_specs=[hbm(), hbm()],
        out_specs=(vmem(), vmem()),
        scratch_shapes=[pltpu.SemaphoreType.DMA((2,))],
        compiler_params=limit(4),
        name="load",
    )(in_hbm(rotations), in_hbm(coords))
    rows_all, repeated = pl.pallas_call(
        rows_kernel,
        out_shape=(
            jax.ShapeDtypeStruct((3, frame_total, width), BF16),
            jax.ShapeDtypeStruct((row_count, 1, 3 * width), F32),
        ),
        in_specs=[smem()] + [vmem()] * (1 + col_count),
        out_specs=(vmem(), vmem()),
        compiler_params=limit(8),
        name="rows",
    )(col, rot_here, coords_here, *others)
    centres = lax.all_to_all(repeated, "row", split_axis=0, concat_axis=0, tiled=True)

    across = []
    for step in range(1, col_count):
        held = pl.pallas_call(
            functools.partial(pick_kernel, members, step),
            out_shape=jax.ShapeDtypeStruct((3, local, width), BF16),
            in_specs=[smem(), smem()] + [vmem()] * col_count,
            out_specs=vmem(),
            compiler_params=limit(4),
            name="pick",
        )(row, col, rows_all, *far)
        across.append(move(held, lambda g, m, c, s=step: (g, m, (c + s) % col_count), lambda g, c: g != c))
    own_block = pl.pallas_call(
        functools.partial(assemble_kernel, members),
        out_shape=jax.ShapeDtypeStruct((3, frame_total, width), BF16),
        in_specs=[smem(), smem()] + [vmem()] * (2 * col_count),
        out_specs=vmem(),
        compiler_params=limit(8),
        name="assemble",
    )(row, col, centres, rows_all, *far, *across)
    evens = [own_block] + [from_member(own_block, 2 * step) for step in range(1, half)]

    height = 32 if width % 32 == 0 else 8
    message = pl.pallas_call(
        functools.partial(weighted_fit_kernel, members),
        in_specs=[smem(), smem(), hbm(), vmem(), vmem()],
        out_specs=vmem(),
        scratch_shapes=[
            pltpu.VMEM((width // height, height, col_width), F32),
            pltpu.VMEM((3, 8, col_width), F32),
            pltpu.VMEM((width, LANES), F32),
            pltpu.SemaphoreType.DMA((width // height,)),
        ],
        out_shape=jax.ShapeDtypeStruct((device_total, 8, 2 * frame_total), F32),
        compiler_params=limit(28),
        cost_estimate=pl.CostEstimate(
            flops=6 * width * col_width, bytes_accessed=4 * width * col_width, transcendentals=0
        ),
        name="weighted_fit",
    )(row, col, in_hbm(inverse_cov), centres, rows_all)
    fits = lax.all_to_all(message, ("row", "col"), split_axis=0, concat_axis=0, tiled=True)
    fits, evens = lax.optimization_barrier((fits, evens))
    stacked = pl.pallas_call(
        stack_kernel,
        out_shape=jax.ShapeDtypeStruct((half, 3, frame_total, width), BF16),
        in_specs=[vmem()] * half,
        out_specs=vmem(),
        compiler_params=limit(8),
        name="stack_panel",
    )(*evens)
    odds = from_member(stacked, 1)

    def tile_spec(odd):
        return pl.BlockSpec((width, width), lambda i, row, *_: (0, lax.rem(row[0], members) ^ (2 * i + odd)))

    tiles_cost = pl.CostEstimate(
        flops=3 * frame_total * width * col_width, bytes_accessed=2 * width * col_width, transcendentals=0
    )
    dev_scratch = pltpu.VMEM((3 * frame_total, width), BF16)
    half_done, transforms, wide, rows_dev = pl.pallas_call(
        functools.partial(first_tiles_kernel, half),
        grid_spec=pltpu.PrefetchScalarGridSpec(
            num_scalar_prefetch=2,
            grid=(half,),
            in_specs=[vmem()] * (3 + half),
            out_specs=(tile_spec(0), vmem(), vmem(), vmem()),
            scratch_shapes=[dev_scratch, dev_scratch],
        ),
        out_shape=(
            jax.ShapeDtypeStruct((width, col_width), F32),
            jax.ShapeDtypeStruct((3, 3, local), F32),
            jax.ShapeDtypeStruct((9, frame_total, LANES), F32),
            jax.ShapeDtypeStruct((width, 3 * frame_total), BF16),
        ),
        compiler_params=limit(16),
        cost_estimate=tiles_cost,
        name="steps_and_even_tiles",
    )(row, col, fits, rows_all, centres, *evens)
    covariance = pl.pallas_call(
        functools.partial(last_tiles_kernel, half),
        grid_spec=pltpu.PrefetchScalarGridSpec(
            num_scalar_prefetch=2,
            grid=(half,),
            in_specs=[pl.BlockSpec(memory_space=pl.ANY)] + [vmem()] * 4,
            out_specs=tile_spec(1),
            scratch_shapes=[dev_scratch],
        ),
        out_shape=jax.ShapeDtypeStruct((width, col_width), F32),
        input_output_aliases={2: 0},
        compiler_params=limit(16),
        cost_estimate=tiles_cost,
        name="odd_tiles",
    )(row, col, half_done, wide, rows_dev, centres, odds)
    return (covariance, transforms)


def solution(mesh):
    placed = (P("col", None, "row"), P(), P("row", "col"))
    return jax.shard_map(
        per_device,
        mesh=mesh,
        in_specs=placed,
        out_specs=(P("row", "col"), P(None, None, "col")),
        check_vma=False,
    )
```
